32 devices in a mesh: bucket: 8 (over z, y), mem: 4 (over x, core).
Axes of the slice: x: 2, y: 2, z: 4, core: 2. Of those that a mesh axis runs over, the one named last changes fastest.
Arguments:
- decoder_in: bfloat16 [64, 128, 512], P(('bucket', 'mem')), may hold values from -6 to 6
- memory: bfloat16 [64, 1024, 512], P('bucket', 'mem'), may hold values from -6 to 6
- grad_out: bfloat16 [64, 128, 512], P(('bucket', 'mem')), may hold values from -6 to 6
- decoder_lengths: int32 [64], P(('bucket', 'mem')), may hold values from 1 to 128, as said below
- memory_lengths: int32 [64], P(('bucket', 'mem')), may hold values from 256 to 1024, as said below
- item_route: int32 [64], P(('bucket', 'mem')), may hold values from -1 to 1, as said below
- in_projection: bfloat16 [6, 512, 512], P(None, ('bucket', 'mem')), may hold values from -0.25 to 0.25
- out_projection: bfloat16 [2, 512, 512], P(None, ('bucket', 'mem')), may hold values from -2 to 2
- attention_bias: bfloat16 [6, 512], P(None, ('bucket', 'mem')), may hold values from -3 to 3
- expand_weight: bfloat16 [512, 2048], P(('bucket', 'mem')), may hold values from -0.25 to 0.25
- expand_bias: bfloat16 [2048], P(('bucket', 'mem')), may hold values from -3 to 3
- reduce_weight: bfloat16 [2048, 512], P(None, ('bucket', 'mem')), may hold values from -0.125 to 0.125
- reduce_bias: bfloat16 [512], P(('bucket', 'mem')), may hold values from -3 to 3
- norm_gain: bfloat16 [3, 512], P(None, ('bucket', 'mem')), may hold values from 0.25 to 1.75
- norm_bias: bfloat16 [3, 512], P(None, ('bucket', 'mem')), may hold values from -2 to 2
Outputs:
- decoder_out: bfloat16 [64, 128, 512], P(('bucket', 'mem'))
- grad_decoder: bfloat16 [64, 128, 512], P(('bucket', 'mem'))
- grad_memory: bfloat16 [64, 1024, 512], P('bucket', 'mem')
- grad_in_projection: float32 [6, 512, 512], P(None, ('bucket', 'mem'))
- grad_out_projection: float32 [2, 512, 512], P(None, ('bucket', 'mem'))
- grad_attention_bias: float32 [6, 512], P(None, ('bucket', 'mem'))
- grad_expand_weight: float32 [512, 2048], P(('bucket', 'mem'))
- grad_expand_bias: float32 [2048], P(('bucket', 'mem'))
- grad_reduce_weight: float32 [2048, 512], P(None, ('bucket', 'mem'))
- grad_reduce_bias: float32 [512], P(('bucket', 'mem'))
- grad_norm_gain: float32 [3, 512], P(None, ('bucket', 'mem'))
- grad_norm_bias: float32 [3, 512], P(None, ('bucket', 'mem'))
The draws below stay inside these ranges and needn't reach their ends.
Inputs may be any that keep to these rules, and one draw needn't show every extreme that they name: `item_route`: -1 marks an empty slot. A value c below 1 means the item is worked on in its own bucket, by the device with the same mem index, in work slot c; a value c of 1 or more means the next bucket (bucket index + 1), same mem index, work slot c - 1. Every work slot of every device receives exactly one item; items of the last bucket stay in it. Some device has no empty slot, and some device receives all its items from the bucket before. `decoder_lengths`: an item's decoder tokens are its first rows; some live item has 128. `memory_lengths`: an item's memory tokens are its first positions; every bucket works on some item with 1024.
All inputs are finite; a program needn't handle non-finite values.
Results may differ from the reference program's by a relative error of at most 0.02.
Values may be sent and summed in bfloat16 or wider, within the bound.
A program may use at most 128 MiB of HBM per device.

```python
import jax
import jax.numpy as jnp
from jax import lax

D = 512
H = 8
HD = 64
FF = 2048
DEC = 128
MEM = 1024
WORK_DEV = 1
IN_DEV = 2
ITEMS = 64
N_BUCKET = 8
N_MEM = 4


def plan_codes(key):
    work_count = WORK_DEV
    offsets = jax.random.randint(jax.random.fold_in(key, 101), (N_BUCKET, N_MEM, work_count), 0, 2)
    chosen = jax.random.randint(jax.random.fold_in(key, 102), (), 0, N_BUCKET - 1)
    bucket_ids = jnp.arange(N_BUCKET)[:, None, None]
    offsets = jnp.where(bucket_ids == 0, 0, offsets)
    offsets = jnp.where(bucket_ids == chosen, 0, offsets)
    offsets = jnp.where(bucket_ids == chosen + 1, 1, offsets)
    staying = offsets == 0
    leaving = jnp.roll(offsets, -1, axis=0) == 1
    present = jnp.concatenate([staying, leaving], axis=2)
    scores = jax.random.randint(jax.random.fold_in(key, 103), (N_BUCKET, N_MEM, 2 * work_count), 0, 1 << 20) * (2 * work_count) + jnp.arange(2 * work_count)
    ordering = jnp.argsort(scores, axis=2)
    filled = jnp.take_along_axis(present, ordering, axis=2)
    return jnp.where(filled, ordering, -1).astype(jnp.int32).reshape(-1)


def slot_places():
    places = jnp.arange(ITEMS)
    bucket = places // (N_MEM * 2 * WORK_DEV)
    column = places // (2 * WORK_DEV) % N_MEM
    return (bucket, column)


def draw_item_route(key, part):
    codes = plan_codes(key)
    return codes


def draw_decoder_lengths(key, part):
    codes = plan_codes(key)
    key = jax.random.fold_in(key, 5)
    bucket, column = slot_places()
    base = DEC // 4 + (DEC - DEC // 4) * bucket // max(N_BUCKET - 1, 1)
    lowest = jnp.maximum(base // 2, 1)
    lengths = jax.random.randint(key, (ITEMS,), lowest, base + 1)
    forced = (column == 0) & ((bucket == N_BUCKET - 1) & (codes == 0) | (bucket == N_BUCKET - 2) & (codes == WORK_DEV))
    return jnp.where(forced, DEC, lengths).astype(jnp.int32)


def draw_memory_lengths(key, part):
    codes = plan_codes(key)
    key = jax.random.fold_in(key, 9)
    bucket, column = slot_places()
    lengths = jax.random.randint(key, (ITEMS,), MEM // 4, MEM + 1)
    forced = (column == 0) & ((codes == 0) | (codes == WORK_DEV))
    return jnp.where(forced, MEM, lengths).astype(jnp.int32)


def spiked(entries, stream_key, source, target, blocks, factor):
    owner, partner = [(jnp.arange(entries.shape[position]) // (entries.shape[position] // blocks)).reshape([-1 if axis == position else 1 for axis in range(entries.ndim)]) for position in (source, target)]
    chosen = jax.random.permutation(stream_key, blocks)[partner]
    strong = (owner == chosen) | (owner == (partner + blocks // 2) % blocks)
    return jnp.where(strong, factor * entries, entries)


def shard_levels(key, dims, pieces, low, largest):
    loudness, own = 1.0, jax.random.fold_in(key, 6)
    for axis_at, blocks in pieces:
        draws = jnp.exp(jax.random.uniform(jax.random.fold_in(own, axis_at), (blocks,), jnp.float32, low / len(pieces), largest / len(pieces)))
        loudness = loudness * jnp.repeat(draws, dims[axis_at] // blocks).reshape([-1 if axis == axis_at else 1 for axis in range(len(dims))])
    return loudness


def centred(stream_key, extent, scale, most, split=(), dtype=jnp.bfloat16):
    drawn = jax.random.normal(stream_key, extent, jnp.float32) * scale
    if len(split) > 0:
        drawn = shard_levels(stream_key, extent, split, -0.22, 0.18) * drawn
    return jnp.clip(drawn, min=-most, max=most).astype(dtype)


def heavy_noise(stream_key, extent, deviation, reach, split, heavy, dtype=jnp.bfloat16):
    drawn = deviation * jax.random.normal(stream_key, extent, jnp.float32)
    if split:
        drawn = drawn * shard_levels(stream_key, extent, split, -0.22, 0.18)
    return jnp.clip(spiked(drawn, jax.random.fold_in(stream_key, 3), *heavy), -reach, reach).astype(dtype)


def setup_inputs(seed: int = 0) -> dict:
    seeds = jax.random.split(jax.random.key(seed), 16)
    decoder_in = centred(seeds[0], (ITEMS, DEC, D), 1.0, 6.0, ((0, 32),))
    memory = centred(seeds[1], (ITEMS, MEM, D), 1.0, 6.0, ((0, 8), (1, 4)))
    grad_out = heavy_noise(seeds[2], (ITEMS, DEC, D), 1.0, 6.0, ((0, 32),), (0, 2, 32, 2.75))
    decoder_lengths = draw_decoder_lengths(jax.random.fold_in(seeds[15], 71), 0)
    memory_lengths = draw_memory_lengths(jax.random.fold_in(seeds[15], 71), 0)
    item_route = draw_item_route(jax.random.fold_in(seeds[15], 71), 0)
    in_projection = centred(seeds[6], (6, D, D), D ** -0.5, 0.25, ((1, 32),))
    out_projection = centred(seeds[7], (2, D, D), (D // 64) ** -0.5, 2.0, ((1, 32),))
    attention_bias = centred(seeds[8], (6, D), 0.5, 3.0, ((1, 32),))
    expand_weight = centred(seeds[9], (D, FF), D ** -0.5, 0.25, ((0, 32),))
    expand_bias = centred(seeds[10], (FF,), 0.5, 3.0, ((0, 32),))
    reduce_weight = centred(seeds[11], (FF, D), FF ** -0.5, 0.125, ((1, 32),))
    reduce_bias = centred(seeds[12], (D,), 0.5, 3.0, ((0, 32),))
    norm_gain = jnp.clip(1.0 + 0.15 * jax.random.normal(seeds[13], (3, D), jnp.float32), 0.25, 1.75).astype(jnp.bfloat16)
    norm_bias = centred(seeds[14], (3, D), 0.3, 2.0, ((1, 32),))
    return {"decoder_in": decoder_in, "memory": memory, "grad_out": grad_out, "decoder_lengths": decoder_lengths, "memory_lengths": memory_lengths, "item_route": item_route, "in_projection": in_projection, "out_projection": out_projection, "attention_bias": attention_bias, "expand_weight": expand_weight, "expand_bias": expand_bias, "reduce_weight": reduce_weight, "reduce_bias": reduce_bias, "norm_gain": norm_gain, "norm_bias": norm_bias}


EPS = 1e-05
NEG = -1e+30

@jax.custom_vjp
def low(v):
    return lax.optimization_barrier(v.astype(jnp.bfloat16)).astype(jnp.float32)

@jax.custom_vjp
def low_back(v):
    return v

def low_keep(v):
    return (low(v), None)

def low_pass(kept, grad):
    return (grad,)

def back_keep(v):
    return (v, None)

def back_low(kept, grad):
    return (low(grad),)
low.defvjp(low_keep, low_pass)
low_back.defvjp(back_keep, back_low)

def round_both(value):
    return low(low_back(value))

def matmul(left, right):
    return jnp.matmul(left, right, precision=lax.Precision.HIGHEST)

def layer_norm(value, gain, shift):
    centered = value - lax.optimization_barrier(jnp.mean(value, axis=-1, keepdims=True))
    spread = lax.optimization_barrier(jnp.mean(centered * centered, axis=-1, keepdims=True))
    return centered * lax.rsqrt(spread + EPS) * gain + shift

def activate(value):
    return jax.nn.silu(value)

def attend(query_rows, key_rows, value_rows, keep_mask):
    item_count = query_rows.shape[0]
    query_span = query_rows.shape[1]
    key_span = key_rows.shape[1]
    query_heads = query_rows.reshape(item_count, query_span, H, HD)
    key_heads = key_rows.reshape(item_count, key_span, H, HD)
    value_heads = value_rows.reshape(item_count, key_span, H, HD)
    scores = jnp.einsum('gqhe,gkhe->ghqk', query_heads, key_heads, precision=lax.Precision.HIGHEST) * HD ** (-0.5)
    scores = jnp.where(keep_mask, low_back(scores), NEG)
    weights_low = low(jax.nn.softmax(scores, axis=-1))
    mixed_heads = jnp.einsum('ghqk,gkhe->gqhe', weights_low, value_heads, precision=lax.Precision.HIGHEST)
    return round_both(mixed_heads.reshape(item_count, query_span, H * HD))

def decoder_layer(inputs, memory_rows, lengths, reaches, params):
    in_projection, out_projection, attention_bias, expand_weight, expand_bias, reduce_weight, reduce_bias, norm_gain, norm_bias = params
    dec_span = inputs.shape[1]
    key_span = memory_rows.shape[1]
    places = jnp.arange(dec_span)
    keep_self = (places[None, :] <= places[:, None])[None, None] & (places[None, None, None, :] < lengths[:, None, None, None])
    keep_cross = jnp.arange(key_span)[None, None, None, :] < reaches[:, None, None, None]
    query_rows = round_both(matmul(inputs, in_projection[0]) + attention_bias[0])
    key_rows = round_both(matmul(inputs, in_projection[1]))
    value_rows = round_both(matmul(inputs, in_projection[2]) + attention_bias[1])
    mixed = attend(query_rows, key_rows, value_rows, keep_self)
    branch = low_back(matmul(mixed, out_projection[0]) + attention_bias[2])
    first_norm = layer_norm(inputs + branch, norm_gain[0], norm_bias[0])
    first_low = low(first_norm)
    cross_query = round_both(matmul(first_low, in_projection[3]) + attention_bias[3])
    cross_keys = round_both(matmul(memory_rows, in_projection[4]))
    cross_values = round_both(matmul(memory_rows, in_projection[5]) + attention_bias[4])
    cross_mixed = attend(cross_query, cross_keys, cross_values, keep_cross)
    cross_branch = low_back(matmul(cross_mixed, out_projection[1]) + attention_bias[5])
    second_norm = layer_norm(first_norm + cross_branch, norm_gain[1], norm_bias[1])
    second_low = low(second_norm)
    hidden_in = low_back(matmul(second_low, expand_weight) + expand_bias)
    hidden = low(activate(hidden_in))
    feed_branch = low_back(matmul(hidden, reduce_weight) + reduce_bias)
    return layer_norm(second_norm + feed_branch, norm_gain[2], norm_bias[2])

def reference(decoder_in, memory, grad_out, decoder_lengths, memory_lengths, item_route, in_projection, out_projection, attention_bias, expand_weight, expand_bias, reduce_weight, reduce_bias, norm_gain, norm_bias):
    params = tuple((weight.astype(jnp.float32) for weight in (in_projection, out_projection, attention_bias, expand_weight, expand_bias, reduce_weight, reduce_bias, norm_gain, norm_bias)))
    live = item_route >= 0
    token_count = jnp.sum(jnp.where(live, decoder_lengths, 0)).astype(jnp.float32)
    group_size = IN_DEV * max(1, 4 // IN_DEV)
    block_count = ITEMS // group_size
    blocks = (decoder_in.reshape(block_count, group_size, DEC, D), memory.reshape(block_count, group_size, MEM, D), grad_out.reshape(block_count, group_size, DEC, D), decoder_lengths.reshape(block_count, group_size), memory_lengths.reshape(block_count, group_size), live.reshape(block_count, group_size))

    def step(totals, block):
        inputs, memory_rows, cotangent, lengths, reaches, present = block
        inputs = inputs.astype(jnp.float32)
        memory_rows = memory_rows.astype(jnp.float32)
        cotangent = cotangent.astype(jnp.float32)
        row_mask = (jnp.arange(DEC)[None, :] < lengths[:, None]) & present[:, None]

        def loss_of(inputs_now, memory_now, params_now):
            output = decoder_layer(inputs_now, memory_now, lengths, reaches, params_now)
            loss = jnp.sum(jnp.where(row_mask[:, :, None], cotangent * output, 0.0))
            return (loss, output)
        loss, pullback, output = jax.vjp(loss_of, inputs, memory_rows, params, has_aux=True)
        grad_inputs, grad_mem, grad_params = pullback(jnp.ones_like(loss))
        totals = jax.tree.map(jnp.add, totals, grad_params)
        output = jnp.where(present[:, None, None], output, 0.0).astype(jnp.bfloat16)
        return (totals, (output, grad_inputs.astype(jnp.bfloat16), grad_mem.astype(jnp.bfloat16)))
    zeros = tuple((jnp.zeros_like(weight) for weight in params))
    totals, results = lax.scan(step, zeros, blocks)
    grads = tuple((total_grad / token_count for total_grad in totals))
    return (results[0].reshape(ITEMS, DEC, D), results[1].reshape(ITEMS, DEC, D), results[2].reshape(ITEMS, MEM, D), grads[0], grads[1], grads[2], grads[3], grads[4], grads[5], grads[6], grads[7], grads[8])
```

```python
import functools

import jax
import jax.numpy as jnp
from jax import lax
from jax.experimental import pallas as pl
from jax.experimental.pallas import tpu as pltpu
from jax.sharding import PartitionSpec as P

HD = 64
EPS = 1e-05
NEG = -1e30
F32 = jnp.float32
BF16 = jnp.bfloat16
MESH = pl.DeviceIdType.MESH
LANES = 128
ROWS = 16

SQ, SK, SV, SO, CK, CV, CQ, CO, EXPAND, REDUCE = 0, 1, 2, 3, 4, 5, 6, 7, 8, 12
BLOCKS = 16
GATHER_CHUNKS = tuple((low, low + 2, "zxyc") for low in range(0, BLOCKS, 2))
SCATTER_CHUNKS = tuple((low, low + 2, "cyxz") for low in range(BLOCKS - 2, -1, -2))
AXES = "zyxc"


def mm(left, right):
    return lax.dot_general(left, right, (((1,), (0,)), ((), ())), preferred_element_type=F32)


def mm_nt(left, right):
    return lax.dot_general(left, right, (((1,), (1,)), ((), ())), preferred_element_type=F32)


def mm_tn(left, right):
    return lax.dot_general(left, right, (((0,), (0,)), ((), ())), preferred_element_type=F32)


class Links:
    def __init__(self, send_sems, recv_sems):
        self.send_sems, self.recv_sems, self.used, self.sent = send_sems, recv_sems, 0, []

    def pair(self):
        self.used += 1
        return self.send_sems.at[self.used - 1], self.recv_sems.at[self.used - 1]

    def copy(self, source, target, landing, device):
        send, recv = self.pair()
        out = pltpu.make_async_remote_copy(
            src_ref=source, dst_ref=target, send_sem=send, recv_sem=recv,
            device_id=device, device_id_type=MESH,
        )
        out.start()
        self.sent.append(out)
        return pltpu.make_async_remote_copy(
            src_ref=source, dst_ref=landing, send_sem=send, recv_sem=recv,
            device_id=device, device_id_type=MESH,
        )

    def finish(self):
        for out in self.sent:
            out.wait_send()


class Place:
    def __init__(self, sizes):
        self.sizes = sizes
        bucket, mem = lax.axis_index("bucket"), lax.axis_index("mem")
        self.bucket, self.mem = bucket, mem
        self.at = {
            "z": bucket // sizes["y"], "y": bucket % sizes["y"],
            "x": mem // sizes["c"], "c": mem % sizes["c"],
        }

    def shifted(self, axis, step):
        size = self.sizes[axis]
        return lax.rem(self.at[axis] + (step % size), size)

    def device(self, axis, step):
        at = dict(self.at)
        at[axis] = self.shifted(axis, step)
        return (at["z"] * self.sizes["y"] + at["y"], at["x"] * self.sizes["c"] + at["c"])


def block_view(ref, lead, index):
    return ref.at[tuple(lead) + tuple(index[axis] for axis in AXES)]


class Gather:
    def __init__(self, links, place, grid, order, parts):
        self.links, self.place, self.parts = links, place, parts
        self.order = [axis for axis in order if grid[axis] > 1]
        self.grid, self.waits, self.done = grid, [], 0

    def step(self):
        for wait in self.waits:
            wait.wait_recv()
        self.waits = []
        if self.done < len(self.order):
            axis = self.order[self.done]
            known = self.order[: self.done]
            for hop in range(1, self.grid[axis]):
                mine, theirs = {}, {}
                for other in AXES:
                    if other in known:
                        mine[other] = theirs[other] = slice(None)
                    else:
                        at = self.place.at[other] if self.grid[other] > 1 else 0
                        mine[other] = theirs[other] = at
                theirs[axis] = self.place.shifted(axis, -hop)
                for ref, lead in self.parts:
                    self.waits.append(
                        self.links.copy(
                            block_view(ref, lead, mine), block_view(ref, lead, mine),
                            block_view(ref, lead, theirs), self.place.device(axis, hop),
                        )
                    )
        self.done += 1


class Scatter:
    def __init__(self, links, place, grid, order, parts, landings, emit):
        self.links, self.place, self.parts, self.landings = links, place, parts, landings
        self.order = [axis for axis in order if grid[axis] > 1]
        self.grid, self.waits, self.done, self.emit = grid, [], 0, emit

    def index(self, known):
        return {
            axis: (self.place.at[axis] if self.grid[axis] > 1 else 0) if axis in known or self.grid[axis] == 1
            else slice(None)
            for axis in AXES
        }

    def step(self):
        for wait in self.waits:
            wait.wait_recv()
        self.waits = []
        if self.done > 0:
            axis = self.order[self.done - 1]
            last = self.done == len(self.order)
            index = self.index(self.order[: self.done])
            for number, (ref, lead) in enumerate(self.parts):
                where = tuple(lead) + tuple(index[name] for name in AXES)
                total = ref[where].astype(F32)
                for hop in range(1, self.grid[axis]):
                    total += self.landings[number][self.done - 1][hop - 1].astype(F32)
                if last:
                    self.emit[number](total)
                else:
                    ref[where] = total.astype(ref.dtype)
        if self.done < len(self.order):
            axis = self.order[self.done]
            known = self.order[: self.done]
            for hop in range(1, self.grid[axis]):
                theirs = self.index(known)
                theirs[axis] = self.place.shifted(axis, hop)
                for number, (ref, lead) in enumerate(self.parts):
                    landing = self.landings[number][self.done].at[hop - 1]
                    self.waits.append(
                        self.links.copy(
                            block_view(ref, lead, theirs), landing, landing, self.place.device(axis, hop)
                        )
                    )
        self.done += 1


def landing_shapes(grid, order, lead_shape, tail_shape):
    shapes, left = [], {axis: grid[axis] for axis in AXES}
    for axis in order:
        if grid[axis] == 1:
            continue
        left[axis] = 1
        kept = tuple(left[name] for name in AXES if left[name] > 1)
        shapes.append(pltpu.VMEM((grid[axis] - 1,) + lead_shape + kept + tail_shape, BF16))
    return shapes


def layer_kernel(
    sizes, grid,
    lengths_ref, reaches_ref, routes_ref, x_ref, dy_ref, pack_ref, small_ref, memory_ref,
    out_ref, dx_ref, gw_ref, gs_ref, gmem_ref,
    scratch,
):
    s = scratch
    place = Place(sizes)
    links = Links(s["send"], s["recv"])
    slots, span, width = x_ref.shape
    rows = slots * span
    members, chunk = s["mem"].shape[1], s["mem"].shape[2]
    reach_span = members * chunk
    heads = width // HD
    pairs = heads // 2
    ff_blocks = (BLOCKS - EXPAND) // 2

    barrier = pltpu.get_barrier_semaphore()
    peers = []
    for axis in "zy":
        peers += [place.device(axis, hop) for hop in range(1, sizes[axis])]
    others = [lax.rem(place.mem + hop, members) for hop in range(1, members)]
    peers += [(place.bucket, other) for other in others]
    for peer in peers:
        pl.semaphore_signal(barrier, inc=1, device_id=peer, device_id_type=MESH)

    def here(ref, lead=()):
        return block_view(ref, lead, {a: place.at[a] if grid[a] > 1 else 0 for a in AXES})

    own = [
        pltpu.make_async_copy(pack_ref, here(s["w"], (slice(None),)), s["local"].at[0]),
        pltpu.make_async_copy(small_ref, here(s["small"]), s["local"].at[1]),
    ]
    own_memory = pltpu.make_async_copy(
        memory_ref.at[pl.ds(place.mem * slots, slots)], s["mem"].at[:, place.mem], s["local"].at[2]
    )
    for copy in own:
        copy.start()
    own_memory.start()
    for copy in own:
        copy.wait()
    pl.semaphore_wait(barrier, len(peers))

    gathers = []
    for number, (low, high, order) in enumerate(GATHER_CHUNKS):
        parts = [(s["w"], (slice(low, high),))]
        if number == 0:
            parts.append((s["small"], ()))
        gathers.append(Gather(links, place, grid, order, parts))
    memory_waits = []

    def send_memory():
        for hop, other in zip(range(1, members), others):
            sender = lax.rem(place.mem + members - hop, members)
            memory_waits.append(
                links.copy(
                    memory_ref.at[pl.ds(other * slots, slots)], s["mem"].at[:, place.mem],
                    s["mem"].at[:, sender], (place.bucket, other),
                )
            )

    def weight(number):
        return s["w"][number].reshape(width, width)

    def put_grad(number, value):
        ref = s["gw"]
        ref[number] = value.astype(BF16).reshape(ref.shape[1:])

    lane = lax.broadcasted_iota(jnp.int32, (1, LANES), 1)
    even = jnp.where(lane < HD, 1.0, 0.0)
    odd = 1.0 - even
    scale = HD ** (-0.5)

    def stack(value, factor=1.0):
        return jnp.concatenate([value * (even * factor).astype(BF16), value * (odd * factor).astype(BF16)], axis=0)

    def unstack(value, factor=1.0):
        return value[:span] * (even * factor) + value[span:] * (odd * factor)

    def normed(value):
        centered = value - jnp.mean(value, axis=-1, keepdims=True)
        rstd = lax.rsqrt(jnp.mean(centered * centered, axis=-1, keepdims=True) + EPS)
        return centered * rstd, rstd

    def norm_back(grad, unit, rstd, number):
        s["rows_grad"][6 + number : 7 + number, :] = jnp.sum(grad * unit, axis=0, keepdims=True)
        s["rows_grad"][9 + number : 10 + number, :] = jnp.sum(grad, axis=0, keepdims=True)
        scaled = grad * s["rows"][6 + number : 7 + number, :]
        return (
            scaled - jnp.mean(scaled, axis=-1, keepdims=True)
            - unit * jnp.mean(scaled * unit, axis=-1, keepdims=True)
        ) * rstd

    def column_sum(value):
        return jnp.sum(value.astype(F32), axis=0, keepdims=True)

    def bias(number):
        return s["rows"][number : number + 1, :]

    def unpack_small():
        places = width // ROWS
        every = s["small"][...].reshape(places, ROWS, LANES).astype(F32)
        group = LANES // ROWS
        columns = [jnp.sum(every[g * group : (g + 1) * group], axis=0) for g in range(places // group)]
        s["rows"][...] = jnp.concatenate(columns, axis=1)
        share = LANES // (width * ff_blocks // places)
        pieces = [
            jnp.sum(every[g * share : (g + 1) * share, 13], axis=0, keepdims=True) for g in range(places // share)
        ]
        s["ebias"][...] = jnp.concatenate(pieces, axis=1)
        tokens = jnp.sum(jnp.sum(every[:, 14], axis=0, keepdims=True), axis=1, keepdims=True)
        s["tokens"][...] = jnp.broadcast_to(tokens, s["tokens"].shape)

    def self_project():
        x = x_ref[...].reshape(rows, width)
        s["q"][...] = (mm(x, weight(SQ)) + bias(0)).astype(BF16)
        s["k"][...] = mm(x, weight(SK)).astype(BF16)
        s["v"][...] = (mm(x, weight(SV)) + bias(1)).astype(BF16)

    def softmax(scores):
        top = jnp.max(scores, axis=-1, keepdims=True)
        weights = jnp.exp(scores - top)
        return (weights * (1.0 / jnp.sum(weights, axis=-1, keepdims=True))).astype(BF16)

    def self_attend():
        row = lax.broadcasted_iota(jnp.int32, (2 * span, span), 0) % span
        col = lax.broadcasted_iota(jnp.int32, (2 * span, span), 1)
        for slot in range(slots):
            keep = (col <= row) & (col < lengths_ref[slot])
            at = slice(slot * span, (slot + 1) * span)
            for pair in range(pairs):
                lanes = slice(pair * LANES, (pair + 1) * LANES)
                scores = mm_nt(stack(s["q"][at, lanes], scale), s["k"][at, lanes])
                low = softmax(jnp.where(keep, scores, NEG))
                s["ps"][slot, pair] = low
                s["a"][at, lanes] = unstack(mm(low, s["v"][at, lanes])).astype(BF16)

    def self_close():
        x = x_ref[...].reshape(rows, width).astype(F32)
        unit, rstd = normed(x + mm(s["a"][...], weight(SO)) + bias(2))
        s["n1"][...], s["d1"][...] = unit, rstd
        h1 = unit * bias(6) + bias(9)
        s["h1"][...] = h1
        s["h1b"][...] = h1.astype(BF16)

    def cross_query():
        s["q2"][...] = (mm(s["h1b"][...], weight(CQ)) + bias(3)).astype(BF16)

    def cross_memory(slot):
        for which, number in (("k2", CK), ("v2", CV)):
            def body(part, carry, which=which, number=number):
                value = mm(s["mem"][slot, part], weight(number))
                if which == "v2":
                    value = value + bias(4)
                s[which][slot, part] = value.astype(BF16)
                return carry
            lax.fori_loop(0, members, body, 0)

    def keys(name, slot, lanes):
        return s[name][slot, :, :, lanes].reshape(reach_span, LANES)

    def cross_attend(slot):
        col = lax.broadcasted_iota(jnp.int32, (1, reach_span), 1)
        keep = col < reaches_ref[slot]
        at = slice(slot * span, (slot + 1) * span)

        def body(pair, carry):
            lanes = pl.ds(pl.multiple_of(pair * LANES, LANES), LANES)
            scores = mm_nt(stack(s["q2"][at, lanes], scale), keys("k2", slot, lanes))
            low = softmax(jnp.where(keep, scores, NEG))
            s["pc"][slot, pair] = low
            s["a2"][at, lanes] = unstack(mm(low, keys("v2", slot, lanes))).astype(BF16)
            return carry
        lax.fori_loop(0, pairs, body, 0)

    def cross_close():
        unit, rstd = normed(s["h1"][...] + mm(s["a2"][...], weight(CO)) + bias(5))
        s["n2"][...], s["d2"][...] = unit, rstd
        h2 = unit * bias(7) + bias(10)
        s["h2b"][...] = h2.astype(BF16)
        s["r3"][...] = h2 + bias(12)

    def ff_up(block):
        lanes = slice(block * width, (block + 1) * width)
        u = mm(s["h2b"][...], weight(EXPAND + block)) + s["ebias"][:, lanes]
        sig = 1.0 / (1.0 + jnp.exp(-u))
        s["f"][block] = (u * sig).astype(BF16)
        s["slope"][block] = sig * (1.0 + u * (1.0 - sig))

    def ff_down(block):
        s["r3"][...] += mm_nt(s["f"][block], weight(REDUCE + block))

    def live_rows(each):
        row = lax.broadcasted_iota(jnp.int32, (rows, 1), 0)
        count = jnp.zeros((rows, 1), jnp.int32)
        for slot in range(slots):
            here_count = jnp.where(routes_ref[slot] >= 0, each(slot), 0)
            count = jnp.where((row >= slot * span) & (row < (slot + 1) * span), here_count + slot * span, count)
        return row < count

    def close():
        unit, rstd = normed(s["r3"][...])
        y = unit * bias(8) + bias(11)
        y = jnp.where(live_rows(lambda slot: span), y, 0.0)
        out_ref[...] = y.astype(BF16).reshape(out_ref.shape)
        dy = dy_ref[...].reshape(rows, width).astype(F32)
        dy = jnp.where(live_rows(lambda slot: lengths_ref[slot]), dy, 0.0)
        dr3 = norm_back(dy, unit, rstd, 2)
        s["dr"][...] = dr3
        s["e"][...] = dr3.astype(BF16)
        s["rows_grad"][12:13, :] = column_sum(s["e"][...])

    def reduce_grad(block):
        put_grad(REDUCE + block, mm_tn(s["e"][...], s["f"][block]))

    def ff_back(block):
        lanes = slice(block * width, (block + 1) * width)
        du = (mm(s["e"][...], weight(REDUCE + block)) * s["slope"][block]).astype(BF16)
        s["ebias_grad"][:, lanes] = column_sum(du)
        put_grad(EXPAND + block, mm_tn(s["h2b"][...], du))
        s["dr"][...] += mm_nt(du, weight(EXPAND + block))

    def cross_open():
        dr2 = norm_back(s["dr"][...], s["n2"][...], s["d2"][...], 1)
        s["dr"][...] = dr2
        e2 = dr2.astype(BF16)
        s["rows_grad"][5:6, :] = column_sum(e2)
        put_grad(CO, mm_tn(s["a2"][...], e2))
        s["da"][...] = mm_nt(e2, weight(CO)).astype(BF16)

    def score_grad(low, grads):
        weights = low.astype(F32)
        return (weights * (grads - jnp.sum(weights * grads, axis=-1, keepdims=True))).astype(BF16)

    def cross_back(slot):
        at = slice(slot * span, (slot + 1) * span)

        def body(pair, carry):
            lanes = pl.ds(pl.multiple_of(pair * LANES, LANES), LANES)
            da = stack(s["da"][at, lanes])
            low = s["pc"][slot, pair]
            ds = score_grad(low, mm_nt(da, keys("v2", slot, lanes)))
            s["dq"][at, lanes] = unstack(mm(ds, keys("k2", slot, lanes)), scale).astype(BF16)
            shape = (members, chunk, LANES)
            s["dk2"][slot, :, :, lanes] = mm_tn(ds, stack(s["q2"][at, lanes], scale)).astype(BF16).reshape(shape)
            s["dv2"][slot, :, :, lanes] = mm_tn(low, da).astype(BF16).reshape(shape)
            return carry
        lax.fori_loop(0, pairs, body, 0)

    def memory_grad(slot):
        def body(part, carry):
            value = mm_nt(s["dk2"][slot, part], weight(CK)) + mm_nt(s["dv2"][slot, part], weight(CV))
            s["gmem"][slot, part] = value.astype(BF16)
            return carry
        lax.fori_loop(0, members, body, 0)

    def send_memory_grad(slot):
        mine = gmem_ref.at[place.mem * slots + slot]
        keep = pltpu.make_async_copy(s["gmem"].at[slot, place.mem], mine, s["local"].at[3 + slot])
        keep.start()
        local_waits.append(keep)
        for hop, other in zip(range(1, members), others):
            sender = lax.rem(place.mem + members - hop, members)
            grad_waits.append(
                links.copy(
                    s["gmem"].at[slot, other], mine, gmem_ref.at[sender * slots + slot], (place.bucket, other)
                )
            )

    local_waits, grad_waits = [], []

    def cross_query_grad():
        dq = s["dq"][...]
        s["rows_grad"][3:4, :] = column_sum(dq)
        put_grad(CQ, mm_tn(s["h1b"][...], dq))

    def memory_weight_grad():
        for name, number in (("dk2", CK), ("dv2", CV)):
            s["acc"][...] = jnp.zeros_like(s["acc"])

            def body(part, carry, name=name):
                for slot in range(slots):
                    s["acc"][...] += mm_tn(s["mem"][slot, part], s[name][slot, part])
                return carry
            lax.fori_loop(0, members, body, 0)
            put_grad(number, s["acc"][...])
        total = jnp.zeros((1, width), F32)
        for slot in range(slots):
            for part in range(members):
                total += column_sum(s["dv2"][slot, part])
        s["rows_grad"][4:5, :] = total

    def self_open():
        dh1 = s["dr"][...] + mm_nt(s["dq"][...], weight(CQ))
        dr1 = norm_back(dh1, s["n1"][...], s["d1"][...], 0)
        s["dr"][...] = dr1
        e1 = dr1.astype(BF16)
        s["rows_grad"][2:3, :] = column_sum(e1)
        put_grad(SO, mm_tn(s["a"][...], e1))
        s["da"][...] = mm_nt(e1, weight(SO)).astype(BF16)

    def self_back():
        for slot in range(slots):
            at = slice(slot * span, (slot + 1) * span)
            for pair in range(pairs):
                lanes = slice(pair * LANES, (pair + 1) * LANES)
                da = stack(s["da"][at, lanes])
                low = s["ps"][slot, pair]
                ds = score_grad(low, mm_nt(da, s["v"][at, lanes]))
                s["dq"][at, lanes] = unstack(mm(ds, s["k"][at, lanes]), scale).astype(BF16)
                s["dk"][at, lanes] = mm_tn(ds, stack(s["q"][at, lanes], scale)).astype(BF16)
                s["dv"][at, lanes] = mm_tn(low, da).astype(BF16)

    def self_grads():
        x = x_ref[...].reshape(rows, width)
        put_grad(SV, mm_tn(x, s["dv"][...]))
        put_grad(SQ, mm_tn(x, s["dq"][...]))
        put_grad(SK, mm_tn(x, s["dk"][...]))
        s["rows_grad"][0:1, :] = column_sum(s["dq"][...])
        s["rows_grad"][1:2, :] = column_sum(s["dv"][...])

    def input_grad():
        total = s["dr"][...] + mm_nt(s["dq"][...], weight(SQ))
        total += mm_nt(s["dk"][...], weight(SK)) + mm_nt(s["dv"][...], weight(SV))
        dx_ref[...] = total.astype(BF16).reshape(dx_ref.shape)

    def pack_small():
        places = width // ROWS
        group, share = LANES // ROWS, LANES // (width * ff_blocks // places)
        row = lax.broadcasted_iota(jnp.int32, (ROWS, LANES), 0)
        for first in range(0, places, share):
            g = first // group
            base = s["rows_grad"][:, g * LANES : (g + 1) * LANES]
            piece = first // share
            extra = s["ebias_grad"][:, piece * LANES : (piece + 1) * LANES]
            value = jnp.where(row == 13, extra, base).astype(BF16)
            for number in range(first, first + share):
                index, rest = [], number
                for axis in reversed(AXES):
                    index.insert(0, rest % grid[axis])
                    rest //= grid[axis]
                s["gsmall"][tuple(index)] = value

    def emit_weight(low, high):
        def emit(total):
            gw_ref[low:high] = total / s["tokens"][0:1, 0:1]
        return emit

    def emit_small(total):
        gs_ref[...] = total / s["tokens"][0:1, 0:1]

    scatters = []
    for number, (low, high, order) in enumerate(SCATTER_CHUNKS):
        parts, landings, emit = [(s["gw"], (slice(low, high),))], [s["land"][number]], [emit_weight(low, high)]
        if number == len(SCATTER_CHUNKS) - 1:
            parts.append((s["gsmall"], ()))
            landings.append(s["land_small"])
            emit.append(emit_small)
        scatters.append(Scatter(links, place, grid, order, parts, landings, emit))

    def advance(work, upto, depth):
        for number in range(min(upto, len(work) - 1), -1, -1):
            pass

    s["rows_grad"][...] = jnp.zeros_like(s["rows_grad"])
    for gather in gathers:
        gather.step()
    send_memory()
    steps = len(gathers[0].order) + 1

    def wave(work, time):
        for number in range(len(work)):
            if work[number].done == time - number and 1 <= work[number].done < steps:
                work[number].step()

    time = 1

    def until(number):
        nonlocal time
        while gathers[number].done < steps:
            wave(gathers, time)
            time += 1

    until(0)
    unpack_small()
    until(1)
    self_project()
    self_attend()
    until(2)
    own_memory.wait()
    for wait in memory_waits:
        wait.wait_recv()
    cross_memory(0)
    cross_memory(1)
    until(3)
    self_close()
    cross_query()
    cross_attend(0)
    until(4)
    cross_attend(1)
    cross_close()
    for block in range(2):
        ff_up(block)
    until(5)
    for block in range(2, 4):
        ff_up(block)
    until(6)
    for block in range(2):
        ff_down(block)
    until(7)
    for block in range(2, 4):
        ff_down(block)
    close()

    started = 0

    def launch():
        nonlocal started
        scatters[started].step()
        started += 1

    def tick():
        for number in range(started):
            if scatters[number].done < steps:
                scatters[number].step()

    reduce_grad(3)
    reduce_grad(2)
    launch()
    reduce_grad(1)
    reduce_grad(0)
    tick()
    launch()
    ff_back(3)
    ff_back(2)
    tick()
    launch()
    ff_back(1)
    ff_back(0)
    tick()
    launch()
    cross_open()
    cross_back(0)
    memory_grad(0)
    send_memory_grad(0)
    tick()
    cross_back(1)
    memory_grad(1)
    send_memory_grad(1)
    tick()
    cross_query_grad()
    launch()
    memory_weight_grad()
    tick()
    launch()
    self_open()
    self_back()
    self_grads()
    pack_small()
    tick()
    launch()
    launch()
    input_grad()
    while any(scatter.done < steps for scatter in scatters):
        tick()
    for wait in grad_waits:
        wait.wait_recv()
    for wait in local_waits:
        wait.wait()
    links.finish()


def copy_count(grid, members, slots):
    count = 0
    for index, (_, _, order) in enumerate(GATHER_CHUNKS):
        count += sum(grid[axis] - 1 for axis in order) * (2 if index == 0 else 1)
    for index, (_, _, order) in enumerate(SCATTER_CHUNKS):
        count += sum(grid[axis] - 1 for axis in order) * (2 if index == len(SCATTER_CHUNKS) - 1 else 1)
    return count + (members - 1) * (1 + slots)


def run_layer(sizes, grid, lengths, reaches, routes, x, dy, pack, small, memory):
    slots, span, width = x.shape
    rows = slots * span
    members = sizes["x"] * sizes["c"]
    chunk = memory.shape[1]
    pairs = width // HD // 2
    ff_blocks = (BLOCKS - EXPAND) // 2
    place = tuple(grid[axis] for axis in AXES)
    mem_shape = (slots, members, chunk, width)
    count = copy_count(grid, members, slots)
    scratch = {
        "w": pltpu.VMEM((BLOCKS,) + place + (ROWS, width), BF16),
        "small": pltpu.VMEM(place + (ROWS, LANES), BF16),
        "gw": pltpu.VMEM((BLOCKS,) + place + (ROWS, width), BF16),
        "gsmall": pltpu.VMEM(place + (ROWS, LANES), BF16),
        "land": [
            landing_shapes(grid, order, (high - low,), (ROWS, width)) for low, high, order in SCATTER_CHUNKS
        ],
        "land_small": landing_shapes(grid, SCATTER_CHUNKS[-1][2], (), (ROWS, LANES)),
        "pc": pltpu.VMEM((slots, pairs, 2 * span, members * chunk), BF16),
        "ps": pltpu.VMEM((slots, pairs, 2 * span, span), BF16),
        "f": pltpu.VMEM((ff_blocks, rows, width), BF16),
        "slope": pltpu.VMEM((ff_blocks, rows, width), F32),
        "rows": pltpu.VMEM((ROWS, width), F32),
        "rows_grad": pltpu.VMEM((ROWS, width), F32),
        "ebias": pltpu.VMEM((1, width * ff_blocks), F32),
        "ebias_grad": pltpu.VMEM((1, width * ff_blocks), F32),
        "tokens": pltpu.VMEM((8, LANES), F32),
        "acc": pltpu.VMEM((width, width), F32),
        "d1": pltpu.VMEM((rows, 1), F32),
        "d2": pltpu.VMEM((rows, 1), F32),
        "send": pltpu.SemaphoreType.DMA((count,)),
        "recv": pltpu.SemaphoreType.DMA((count,)),
        "local": pltpu.SemaphoreType.DMA((3 + slots,)),
    }
    for name in ("mem", "k2", "v2", "dk2", "dv2", "gmem"):
        scratch[name] = pltpu.VMEM(mem_shape, BF16)
    for name in ("q", "k", "v", "a", "h1b", "q2", "a2", "h2b", "e", "da", "dq", "dk", "dv"):
        scratch[name] = pltpu.VMEM((rows, width), BF16)
    for name in ("n1", "n2", "h1", "r3", "dr"):
        scratch[name] = pltpu.VMEM((rows, width), F32)
    leaves, tree = jax.tree.flatten(scratch)

    def kernel(*refs):
        fixed = refs[: len(refs) - len(leaves)]
        layer_kernel(sizes, grid, *fixed, jax.tree.unflatten(tree, refs[len(fixed) :]))

    vmem, smem = pl.BlockSpec(memory_space=pltpu.VMEM), pl.BlockSpec(memory_space=pltpu.SMEM)
    anywhere = pl.BlockSpec(memory_space=pl.ANY)
    return pl.pallas_call(
        kernel,
        out_shape=(
            jax.ShapeDtypeStruct(x.shape, BF16),
            jax.ShapeDtypeStruct(x.shape, BF16),
            jax.ShapeDtypeStruct(pack.shape, F32),
            jax.ShapeDtypeStruct(small.shape, F32),
            jax.ShapeDtypeStruct(memory.shape, BF16),
        ),
        in_specs=[smem] * 3 + [vmem] * 2 + [anywhere] * 3,
        out_specs=[vmem] * 4 + [anywhere],
        scratch_shapes=leaves,
        compiler_params=pltpu.CompilerParams(
            collective_id=0, has_side_effects=True, vmem_limit_bytes=62 << 20
        ),
    )(lengths, reaches, routes, x, dy, pack, small, memory)


def shards(
    sizes,
    decoder_in, memory, grad_out, decoder_lengths, memory_lengths, item_route,
    in_projection, out_projection, attention_bias, expand_weight, expand_bias,
    reduce_weight, reduce_bias, norm_gain, norm_bias,
):
    own_rows, width = in_projection.shape[1:]
    ff = expand_weight.shape[1] // width

    def cut(weight):
        return weight.reshape(own_rows, ff, width).transpose(1, 0, 2)

    pack = jnp.concatenate(
        [
            in_projection[0:3], out_projection[0:1], in_projection[4:6], in_projection[3:4],
            out_projection[1:2], cut(expand_weight), cut(reduce_weight.T),
        ],
        axis=0,
    )
    narrow = jnp.concatenate([attention_bias, norm_gain, norm_bias, reduce_bias[None]], axis=0)
    live = jnp.where(item_route >= 0, decoder_lengths, 0).astype(BF16)
    joined = own_rows < ROWS
    bucket, mem = lax.axis_index("bucket"), lax.axis_index("mem")
    if joined:
        pack = lax.all_gather(pack, "mem", axis=1, tiled=True)
        narrow = lax.all_gather(narrow, "mem", axis=1, tiled=True)
        expand_bias = lax.all_gather(expand_bias, "mem", axis=0, tiled=True)
        live = lax.all_gather(live, "mem", axis=0, tiled=True)
        grid = dict(sizes, x=1, c=1)
        spot = bucket
    else:
        grid = dict(sizes)
        spot = bucket * (sizes["x"] * sizes["c"]) + mem
    lane = jnp.arange(LANES)

    def spread(values):
        size = values.shape[-1]
        tiled = jnp.tile(values, (1, LANES // size))
        return jnp.where(lane // size == spot % (LANES // size), tiled, jnp.zeros_like(tiled))

    small = jnp.concatenate(
        [
            spread(narrow), spread(expand_bias[None]),
            jnp.pad(live[None], ((0, 2), (0, LANES - live.shape[0])))[:2],
        ],
        axis=0,
    )
    small = jnp.pad(small, ((0, ROWS - small.shape[0]), (0, 0)))
    decoder_out, grad_decoder, grad_blocks, grad_small, grad_memory = run_layer(
        sizes, grid, decoder_lengths, memory_lengths, item_route, decoder_in, grad_out, pack, small, memory
    )

    def picked(values, size):
        return lax.dynamic_slice_in_dim(values, (spot % (LANES // size)) * size, size, axis=1)

    grad_narrow = picked(grad_small[0:13], ROWS)
    grad_ebias = picked(grad_small[13:14], expand_bias.shape[0])[0]
    if joined:
        grad_blocks = lax.psum_scatter(grad_blocks, "mem", scatter_dimension=1, tiled=True)
        grad_narrow = lax.psum_scatter(grad_narrow, "mem", scatter_dimension=1, tiled=True)
        grad_ebias = lax.psum_scatter(grad_ebias, "mem", scatter_dimension=0, tiled=True)

    def joined_back(blocks):
        return blocks.transpose(1, 0, 2).reshape(own_rows, ff * width)

    g = grad_blocks
    return (
        decoder_out,
        grad_decoder,
        grad_memory,
        jnp.concatenate([g[0:3], g[CQ : CQ + 1], g[CK : CV + 1]], axis=0),
        jnp.concatenate([g[SO : SO + 1], g[CO : CO + 1]], axis=0),
        grad_narrow[0:6],
        joined_back(g[EXPAND:REDUCE]),
        grad_ebias,
        joined_back(g[REDUCE:BLOCKS]).T,
        grad_narrow[12],
        grad_narrow[6:9],
        grad_narrow[9:12],
    )


def solution(mesh):
    both = ("bucket", "mem")
    buckets, members = mesh.shape["bucket"], mesh.shape["mem"]
    cores = 2
    across = members // cores
    sizes = {"z": buckets // across, "y": across, "x": across, "c": cores}
    in_specs = (
        P(both, None, None), P("bucket", "mem", None), P(both, None, None), P(both), P(both), P(both),
        P(None, both, None), P(None, both, None), P(None, both), P(both, None), P(both),
        P(None, both), P(both), P(None, both), P(None, both),
    )
    out_specs = (
        P(both, None, None), P(both, None, None), P("bucket", "mem", None),
        P(None, both, None), P(None, both, None), P(None, both), P(both, None), P(both),
        P(None, both), P(both), P(None, both), P(None, both),
    )
    return jax.shard_map(
        functools.partial(shards, sizes), mesh=mesh, in_specs=in_specs, out_specs=out_specs, check_vma=False
    )
```

```python
import functools

import jax
import jax.numpy as jnp
from jax import lax
from jax.experimental import pallas as pl
from jax.experimental.pallas import tpu as pltpu
from jax.sharding import PartitionSpec as P

HD = 64
EPS = 1e-05
NEG = -1e30
F32 = jnp.float32
BF16 = jnp.bfloat16
MESH = pl.DeviceIdType.MESH
LANES = 128
ROWS = 16

SQ, SK, SV, SO, CK, CV, CQ, CO, EXPAND, REDUCE = 0, 1, 2, 3, 4, 5, 6, 7, 8, 12
BLOCKS = 16
GATHER_CHUNKS = (
    (0, 2, "xzyc"), (2, 4, "xzyc"), (4, 6, "zyxc"), (6, 8, "xzyc"),
    (8, 10, "xzyc"), (10, 12, "xzyc"), (12, 14, "zyxc"), (14, 16, "xyzc"),
)
SCATTER_CHUNKS = (
    (14, 16, "cyzx"), (12, 14, "cyzx"), (10, 12, "czyx"), (8, 10, "cyzx"),
    (6, 8, "cyzx"), (4, 6, "cyzx"), (2, 4, "cxzy"), (0, 2, "cyxz"),
)
AXES = "zyxc"


def mm(left, right):
    return lax.dot_general(left, right, (((1,), (0,)), ((), ())), preferred_element_type=F32)


def mm_nt(left, right):
    return lax.dot_general(left, right, (((1,), (1,)), ((), ())), preferred_element_type=F32)


def mm_tn(left, right):
    return lax.dot_general(left, right, (((0,), (0,)), ((), ())), preferred_element_type=F32)


class Links:
    def __init__(self, send_sems, recv_sems):
        self.send_sems, self.recv_sems, self.used, self.sent = send_sems, recv_sems, 0, []

    def pair(self):
        self.used += 1
        return self.send_sems.at[self.used - 1], self.recv_sems.at[self.used - 1]

    def copy(self, source, target, landing, device):
        send, recv = self.pair()
        out = pltpu.make_async_remote_copy(
            src_ref=source, dst_ref=target, send_sem=send, recv_sem=recv,
            device_id=device, device_id_type=MESH,
        )
        out.start()
        self.sent.append(out)
        return pltpu.make_async_remote_copy(
            src_ref=source, dst_ref=landing, send_sem=send, recv_sem=recv,
            device_id=device, device_id_type=MESH,
        )

    def finish(self):
        for out in self.sent:
            out.wait_send()


class Place:
    def __init__(self, sizes):
        self.sizes = sizes
        bucket, mem = lax.axis_index("bucket"), lax.axis_index("mem")
        self.bucket, self.mem = bucket, mem
        self.at = {
            "z": bucket // sizes["y"], "y": bucket % sizes["y"],
            "x": mem // sizes["c"], "c": mem % sizes["c"],
        }

    def shifted(self, axis, step):
        size = self.sizes[axis]
        return lax.rem(self.at[axis] + (step % size), size)

    def device(self, axis, step):
        at = dict(self.at)
        at[axis] = self.shifted(axis, step)
        return (at["z"] * self.sizes["y"] + at["y"], at["x"] * self.sizes["c"] + at["c"])


def block_view(ref, lead, index):
    return ref.at[tuple(lead) + tuple(index[axis] for axis in AXES)]


class Gather:
    def __init__(self, links, place, grid, order, parts):
        self.links, self.place, self.parts = links, place, parts
        self.order = [axis for axis in order if grid[axis] > 1]
        self.grid, self.waits, self.done = grid, [], 0

    @property
    def over(self):
        return self.done > len(self.order)

    def step(self):
        if self.over:
            return
        for wait in self.waits:
            wait.wait_recv()
        self.waits = []
        if self.done < len(self.order):
            axis = self.order[self.done]
            known = self.order[: self.done]
            for hop in range(1, self.grid[axis]):
                mine, theirs = {}, {}
                for other in AXES:
                    if other in known:
                        mine[other] = theirs[other] = slice(None)
                    else:
                        at = self.place.at[other] if self.grid[other] > 1 else 0
                        mine[other] = theirs[other] = at
                theirs[axis] = self.place.shifted(axis, -hop)
                for ref, lead in self.parts:
                    self.waits.append(
                        self.links.copy(
                            block_view(ref, lead, mine), block_view(ref, lead, mine),
                            block_view(ref, lead, theirs), self.place.device(axis, hop),
                        )
                    )
        self.done += 1


class Scatter:
    def __init__(self, links, place, grid, order, parts, landings, emit):
        self.links, self.place, self.parts, self.landings = links, place, parts, landings
        self.order = [axis for axis in order if grid[axis] > 1]
        self.grid, self.waits, self.done, self.emit = grid, [], 0, emit

    def index(self, known):
        return {
            axis: (self.place.at[axis] if self.grid[axis] > 1 else 0) if axis in known or self.grid[axis] == 1
            else slice(None)
            for axis in AXES
        }

    @property
    def over(self):
        return self.done > len(self.order)

    def step(self):
        if self.over:
            return
        for wait in self.waits:
            wait.wait_recv()
        self.waits = []
        if self.done > 0:
            axis = self.order[self.done - 1]
            last = self.done == len(self.order)
            index = self.index(self.order[: self.done])
            for number, (ref, lead) in enumerate(self.parts):
                where = tuple(lead) + tuple(index[name] for name in AXES)
                landed = self.landings[number][self.done - 1]
                if self.grid[axis] == 2 and not last:
                    ref[where] = ref[where] + landed[0]
                    continue
                total = ref[where].astype(F32)
                for hop in range(1, self.grid[axis]):
                    total += landed[hop - 1].astype(F32)
                if last:
                    self.emit[number](total)
                else:
                    ref[where] = total.astype(ref.dtype)
        if self.done < len(self.order):
            axis = self.order[self.done]
            known = self.order[: self.done]
            for hop in range(1, self.grid[axis]):
                theirs = self.index(known)
                theirs[axis] = self.place.shifted(axis, hop)
                for number, (ref, lead) in enumerate(self.parts):
                    landing = self.landings[number][self.done].at[hop - 1]
                    self.waits.append(
                        self.links.copy(
                            block_view(ref, lead, theirs), landing, landing, self.place.device(axis, hop)
                        )
                    )
        self.done += 1


def landing_shapes(grid, order, lead_shape, tail_shape):
    shapes, left = [], {axis: grid[axis] for axis in AXES}
    for axis in order:
        if grid[axis] == 1:
            continue
        left[axis] = 1
        kept = tuple(left[name] for name in AXES if left[name] > 1)
        shapes.append(pltpu.VMEM((grid[axis] - 1,) + lead_shape + kept + tail_shape, BF16))
    return shapes


def layer_kernel(
    sizes, grid,
    lengths_ref, reaches_ref, routes_ref, all_lengths_ref, all_routes_ref,
    attention_bias_ref, gain_ref, shift_ref, reduce_bias_ref, expand_bias_ref,
    x_hbm, dy_hbm, in_hbm, out_hbm, expand_hbm, reduce_hbm, memory_ref,
    grad_bias_ref, grad_gain_ref, grad_shift_ref, grad_reduce_bias_ref, grad_expand_bias_ref,
    y_hbm, dx_hbm, grad_in_hbm, grad_out_hbm, grad_expand_hbm, grad_reduce_hbm, gmem_ref,
    scratch,
):
    s = scratch
    place = Place(sizes)
    links = Links(s["send"], s["recv"])
    x_ref, dy_ref = s["x"], s["dy"]
    slots, span, width = x_ref.shape
    rows = slots * span
    members, chunk = s["mem"].shape[1], s["mem"].shape[2]
    reach_span = members * chunk
    heads = width // HD
    pairs = heads // 2
    ff_blocks = (BLOCKS - EXPAND) // 2
    places = width // ROWS
    locals_used = [0]

    def local_copy(source, target):
        locals_used[0] += 1
        copy = pltpu.make_async_copy(source, target, s["local"].at[locals_used[0] - 1])
        copy.start()
        return copy

    barrier = pltpu.get_barrier_semaphore()
    peers = []
    for axis in "zy":
        peers += [place.device(axis, hop) for hop in range(1, sizes[axis])]
    others = [lax.rem(place.mem + hop, members) for hop in range(1, members)]
    peers += [(place.bucket, other) for other in others]
    for peer in peers:
        pl.semaphore_signal(barrier, inc=1, device_id=peer, device_id_type=MESH)

    here = tuple(place.at[axis] if grid[axis] > 1 else 0 for axis in AXES)

    def block_parts(in_ref, out_ref, expand_ref, reduce_ref):
        parts = [(SQ + k, in_ref.at[k]) for k in range(3)] + [(CQ, in_ref.at[3]), (CK, in_ref.at[4])]
        parts += [(CV, in_ref.at[5]), (SO, out_ref.at[0]), (CO, out_ref.at[1])]
        for k in range(ff_blocks):
            lanes = pl.ds(k * width, width)
            parts += [(EXPAND + k, expand_ref.at[:, lanes]), (REDUCE + k, reduce_ref.at[:, lanes])]
        return sorted(parts, key=lambda part: part[0])

    own = [
        local_copy(part, s["w"].at[(number,) + here])
        for number, part in block_parts(in_hbm, out_hbm, expand_hbm, reduce_hbm)
    ]
    own_rows = [local_copy(x_hbm, x_ref), local_copy(dy_hbm, dy_ref)]
    own_memory = local_copy(memory_ref.at[pl.ds(place.mem * slots, slots)], s["mem"].at[:, place.mem])

    spot = here[0]
    for axis, at in zip(AXES[1:], here[1:]):
        spot = spot * grid[axis] + at
    share = expand_bias_ref.shape[1]
    group, pieces = LANES // ROWS, LANES // share
    packet = s["packet"]
    packet[...] = jnp.zeros_like(packet)
    packet[0:6, 0:ROWS] = attention_bias_ref[...].astype(F32)
    packet[6:9, 0:ROWS] = gain_ref[...].astype(F32)
    packet[9:12, 0:ROWS] = shift_ref[...].astype(F32)
    packet[12:13, 0:ROWS] = reduce_bias_ref[...].astype(F32)
    packet[13:14, 0:share] = expand_bias_ref[...].astype(F32)
    narrow = pltpu.roll(packet[...], lax.rem(spot, group) * ROWS, 1)
    wide = pltpu.roll(packet[...], lax.rem(spot, pieces) * share, 1)
    row = lax.broadcasted_iota(jnp.int32, (ROWS, LANES), 0)
    lane = lax.broadcasted_iota(jnp.int32, (ROWS, LANES), 1)
    live = jnp.zeros((ROWS, LANES), jnp.int32)
    for slot in range(all_lengths_ref.shape[0]):
        count = jnp.where(all_routes_ref[slot] >= 0, all_lengths_ref[slot], 0)
        live = jnp.where(lane == slot, count, live)
    value = jnp.where(row == 13, wide, jnp.where(row == 14, live.astype(F32), narrow))
    s["small"][here] = value.astype(BF16)
    for copy in own:
        copy.wait()
    pl.semaphore_wait(barrier, len(peers))

    gathers = []
    for number, (low, high, order) in enumerate(GATHER_CHUNKS):
        parts = [(s["w"], (slice(low, high),))]
        if number == 0:
            parts.append((s["small"], ()))
        gathers.append(Gather(links, place, grid, order, parts))
    memory_waits = [[] for _ in range(slots)]
    half = chunk // 2

    def send_memory(slot, part):
        at = pl.ds(part * half, half)
        for hop, other in zip(range(1, members), others):
            sender = lax.rem(place.mem + members - hop, members)
            memory_waits[slot].append(
                links.copy(
                    memory_ref.at[other * slots + slot, at], s["mem"].at[slot, place.mem, at],
                    s["mem"].at[slot, sender, at], (place.bucket, other),
                )
            )

    def weight(number):
        return s["w"][number].reshape(width, width)

    def put_grad(number, value):
        ref = s["gw"]
        ref[number] = value.astype(BF16).reshape(ref.shape[1:])

    even_lanes = lax.broadcasted_iota(jnp.int32, (1, LANES), 1) < HD
    even = jnp.where(even_lanes, 1.0, 0.0)
    odd = 1.0 - even
    scale = HD ** (-0.5)

    def stack(value, factor=1.0):
        return jnp.concatenate([value * (even * factor).astype(BF16), value * (odd * factor).astype(BF16)], axis=0)

    def unstack(value, factor=1.0):
        return value[:span] * (even * factor) + value[span:] * (odd * factor)

    def normed(value):
        centered = value - jnp.mean(value, axis=-1, keepdims=True)
        rstd = lax.rsqrt(jnp.mean(centered * centered, axis=-1, keepdims=True) + EPS)
        return centered * rstd, rstd

    def norm_back(grad, unit, rstd, number):
        s["rows_grad"][6 + number : 7 + number, :] = jnp.sum(grad * unit, axis=0, keepdims=True)
        s["rows_grad"][9 + number : 10 + number, :] = jnp.sum(grad, axis=0, keepdims=True)
        scaled = grad * s["rows"][6 + number : 7 + number, :]
        return (
            scaled - jnp.mean(scaled, axis=-1, keepdims=True)
            - unit * jnp.mean(scaled * unit, axis=-1, keepdims=True)
        ) * rstd

    def column_sum(value):
        return jnp.sum(value.astype(F32), axis=0, keepdims=True)

    def bias(number):
        return s["rows"][number : number + 1, :]

    def unpack_small():
        every = s["small"][...].reshape(places, ROWS, LANES).astype(F32)
        columns = [jnp.sum(every[g * group : (g + 1) * group], axis=0) for g in range(places // group)]
        s["rows"][...] = jnp.concatenate(columns, axis=1)
        columns = [
            jnp.sum(every[g * pieces : (g + 1) * pieces, 13], axis=0, keepdims=True) for g in range(places // pieces)
        ]
        s["ebias"][...] = jnp.concatenate(columns, axis=1)
        tokens = jnp.sum(jnp.sum(every[:, 14], axis=0, keepdims=True), axis=1, keepdims=True)
        s["tokens"][...] = jnp.broadcast_to(tokens, s["tokens"].shape)

    def self_project():
        x = x_ref[...].reshape(rows, width)
        s["q"][...] = (mm(x, weight(SQ)) + bias(0)).astype(BF16)
        s["k"][...] = mm(x, weight(SK)).astype(BF16)
        s["v"][...] = (mm(x, weight(SV)) + bias(1)).astype(BF16)

    def softmax(scores):
        top = jnp.max(scores, axis=-1, keepdims=True)
        weights = jnp.exp(scores - top)
        return (weights * (1.0 / jnp.sum(weights, axis=-1, keepdims=True))).astype(BF16)

    def self_attend():
        row = lax.broadcasted_iota(jnp.int32, (2 * span, span), 0) % span
        col = lax.broadcasted_iota(jnp.int32, (2 * span, span), 1)
        for slot in range(slots):
            keep = (col <= row) & (col < lengths_ref[slot])
            at = slice(slot * span, (slot + 1) * span)
            for pair in range(pairs):
                lanes = slice(pair * LANES, (pair + 1) * LANES)
                scores = mm_nt(stack(s["q"][at, lanes], scale), s["k"][at, lanes])
                low = softmax(jnp.where(keep, scores, NEG))
                s["ps"][slot, pair] = low
                s["a"][at, lanes] = unstack(mm(low, s["v"][at, lanes])).astype(BF16)

    def self_close():
        x = x_ref[...].reshape(rows, width).astype(F32)
        unit, rstd = normed(x + mm(s["a"][...], weight(SO)) + bias(2))
        s["n1"][...], s["d1"][...] = unit, rstd
        h1 = unit * bias(6) + bias(9)
        s["h1"][...] = h1
        s["h1b"][...] = h1.astype(BF16)

    def cross_query():
        s["q2"][...] = (mm(s["h1b"][...], weight(CQ)) + bias(3)).astype(BF16)

    def cross_memory(slot):
        for which, number in (("k2", CK), ("v2", CV)):
            def body(part, carry, which=which, number=number):
                value = mm(s["mem"][slot, part], weight(number))
                if which == "v2":
                    value = value + bias(4)
                s[which][slot, part] = value.astype(BF16)
                return carry
            lax.fori_loop(0, members, body, 0)

    def keys(name, slot, lanes):
        return s[name][slot, :, :, lanes].reshape(reach_span, LANES)

    def cross_attend(slot):
        col = lax.broadcasted_iota(jnp.int32, (1, reach_span), 1)
        keep = col < reaches_ref[slot]
        at = slice(slot * span, (slot + 1) * span)

        def body(pair, carry):
            lanes = pl.ds(pl.multiple_of(pair * LANES, LANES), LANES)
            scores = mm_nt(stack(s["q2"][at, lanes], scale), keys("k2", slot, lanes))
            low = softmax(jnp.where(keep, scores, NEG))
            s["pc"][slot, pair] = low
            s["a2"][at, lanes] = unstack(mm(low, keys("v2", slot, lanes))).astype(BF16)
            return carry
        lax.fori_loop(0, pairs, body, 0)

    def cross_close():
        unit, rstd = normed(s["h1"][...] + mm(s["a2"][...], weight(CO)) + bias(5))
        s["n2"][...], s["d2"][...] = unit, rstd
        h2 = unit * bias(7) + bias(10)
        s["h2b"][...] = h2.astype(BF16)
        s["r3"][...] = h2 + bias(12)

    def ff_up(block):
        lanes = slice(block * width, (block + 1) * width)
        u = mm(s["h2b"][...], weight(EXPAND + block)) + s["ebias"][:, lanes]
        sig = 1.0 / (1.0 + jnp.exp(-u))
        s["f"][block] = (u * sig).astype(BF16)
        s["slope"][block] = sig * (1.0 + u * (1.0 - sig))

    def ff_down(block):
        s["r3"][...] += mm_nt(s["f"][block], weight(REDUCE + block))

    def live_rows(each):
        row = lax.broadcasted_iota(jnp.int32, (rows, 1), 0)
        count = jnp.zeros((rows, 1), jnp.int32)
        for slot in range(slots):
            here_count = jnp.where(routes_ref[slot] >= 0, each(slot), 0)
            count = jnp.where((row >= slot * span) & (row < (slot + 1) * span), here_count + slot * span, count)
        return row < count

    def close():
        unit, rstd = normed(s["r3"][...])
        y = unit * bias(8) + bias(11)
        y = jnp.where(live_rows(lambda slot: span), y, 0.0)
        s["y"][...] = y.astype(BF16).reshape(x_ref.shape)
        local_waits.append(local_copy(s["y"], y_hbm))
        dy = dy_ref[...].reshape(rows, width).astype(F32)
        dy = jnp.where(live_rows(lambda slot: lengths_ref[slot]), dy, 0.0)
        dr3 = norm_back(dy, unit, rstd, 2)
        s["dr"][...] = dr3
        s["e"][...] = dr3.astype(BF16)
        s["rows_grad"][12:13, :] = column_sum(s["e"][...])

    def reduce_grad(block):
        put_grad(REDUCE + block, mm_tn(s["e"][...], s["f"][block]))

    def ff_back(block):
        lanes = slice(block * width, (block + 1) * width)
        du = (mm(s["e"][...], weight(REDUCE + block)) * s["slope"][block]).astype(BF16)
        s["ebias_grad"][:, lanes] = column_sum(du)
        put_grad(EXPAND + block, mm_tn(s["h2b"][...], du))
        s["dr"][...] += mm_nt(du, weight(EXPAND + block))

    def cross_open():
        dr2 = norm_back(s["dr"][...], s["n2"][...], s["d2"][...], 1)
        s["dr"][...] = dr2
        e2 = dr2.astype(BF16)
        s["rows_grad"][5:6, :] = column_sum(e2)
        put_grad(CO, mm_tn(s["a2"][...], e2))
        s["da"][...] = mm_nt(e2, weight(CO)).astype(BF16)

    def score_grad(low, grads):
        weights = low.astype(F32)
        return (weights * (grads - jnp.sum(weights * grads, axis=-1, keepdims=True))).astype(BF16)

    def cross_back(slot):
        at = slice(slot * span, (slot + 1) * span)

        def body(pair, carry):
            lanes = pl.ds(pl.multiple_of(pair * LANES, LANES), LANES)
            da = stack(s["da"][at, lanes])
            low = s["pc"][slot, pair]
            ds = score_grad(low, mm_nt(da, keys("v2", slot, lanes)))
            s["dq"][at, lanes] = unstack(mm(ds, keys("k2", slot, lanes)), scale).astype(BF16)
            shape = (members, chunk, LANES)
            s["dk2"][slot, :, :, lanes] = mm_tn(ds, stack(s["q2"][at, lanes], scale)).astype(BF16).reshape(shape)
            s["dv2"][slot, :, :, lanes] = mm_tn(low, da).astype(BF16).reshape(shape)
            return carry
        lax.fori_loop(0, pairs, body, 0)

    def memory_grad(slot):
        def body(part, carry):
            value = mm_nt(s["dk2"][slot, part], weight(CK)) + mm_nt(s["dv2"][slot, part], weight(CV))
            s["gmem"][slot, part] = value.astype(BF16)
            return carry
        lax.fori_loop(0, members, body, 0)

    def send_memory_grad(slot):
        mine = gmem_ref.at[place.mem * slots + slot]
        local_waits.append(local_copy(s["gmem"].at[slot, place.mem], mine))
        for hop, other in zip(range(1, members), others):
            sender = lax.rem(place.mem + members - hop, members)
            grad_waits.append(
                links.copy(
                    s["gmem"].at[slot, other], mine, gmem_ref.at[sender * slots + slot], (place.bucket, other)
                )
            )

    local_waits, grad_waits = [], []

    def cross_query_grad():
        dq = s["dq"][...]
        s["rows_grad"][3:4, :] = column_sum(dq)
        put_grad(CQ, mm_tn(s["h1b"][...], dq))

    def memory_weight_grad():
        for name, number in (("dk2", CK), ("dv2", CV)):
            s["acc"][...] = jnp.zeros_like(s["acc"])

            def body(part, carry, name=name):
                for slot in range(slots):
                    s["acc"][...] += mm_tn(s["mem"][slot, part], s[name][slot, part])
                return carry
            lax.fori_loop(0, members, body, 0)
            put_grad(number, s["acc"][...])
        total = jnp.zeros((1, width), F32)
        for slot in range(slots):
            for part in range(members):
                total += column_sum(s["dv2"][slot, part])
        s["rows_grad"][4:5, :] = total

    def self_open():
        dh1 = s["dr"][...] + mm_nt(s["dq"][...], weight(CQ))
        dr1 = norm_back(dh1, s["n1"][...], s["d1"][...], 0)
        s["dr"][...] = dr1
        e1 = dr1.astype(BF16)
        s["rows_grad"][2:3, :] = column_sum(e1)
        put_grad(SO, mm_tn(s["a"][...], e1))
        s["da"][...] = mm_nt(e1, weight(SO)).astype(BF16)

    def self_back():
        for slot in range(slots):
            at = slice(slot * span, (slot + 1) * span)
            for pair in range(pairs):
                lanes = slice(pair * LANES, (pair + 1) * LANES)
                da = stack(s["da"][at, lanes])
                low = s["ps"][slot, pair]
                ds = score_grad(low, mm_nt(da, s["v"][at, lanes]))
                s["dq"][at, lanes] = unstack(mm(ds, s["k"][at, lanes]), scale).astype(BF16)
                s["dk"][at, lanes] = mm_tn(ds, stack(s["q"][at, lanes], scale)).astype(BF16)
                s["dv"][at, lanes] = mm_tn(low, da).astype(BF16)

    def self_grads():
        x = x_ref[...].reshape(rows, width)
        put_grad(SV, mm_tn(x, s["dv"][...]))
        put_grad(SQ, mm_tn(x, s["dq"][...]))
        put_grad(SK, mm_tn(x, s["dk"][...]))
        s["rows_grad"][0:1, :] = column_sum(s["dq"][...])
        s["rows_grad"][1:2, :] = column_sum(s["dv"][...])

    def input_grad():
        total = s["dr"][...] + mm_nt(s["dq"][...], weight(SQ))
        total += mm_nt(s["dk"][...], weight(SK)) + mm_nt(s["dv"][...], weight(SV))
        s["dx"][...] = total.astype(BF16).reshape(x_ref.shape)
        local_waits.append(local_copy(s["dx"], dx_hbm))

    def turned(value, lanes):
        return value if lanes == 0 else pltpu.roll(value, LANES - lanes, 1)

    def pack_small():
        row = lax.broadcasted_iota(jnp.int32, (ROWS, LANES), 0)
        for number in range(places):
            at = number // group * LANES
            base = turned(s["rows_grad"][:, at : at + LANES], number % group * ROWS)
            at = number // pieces * LANES
            extra = turned(s["ebias_grad"][:, at : at + LANES], number % pieces * share)
            index, rest = [], number
            for axis in reversed(AXES):
                index.insert(0, rest % grid[axis])
                rest //= grid[axis]
            s["gsmall"][tuple(index)] = jnp.where(row == 13, extra, base).astype(BF16)

    targets = dict(block_parts(grad_in_hbm, grad_out_hbm, grad_expand_hbm, grad_reduce_hbm))

    def emit_weight(low, high):
        def emit(total):
            s["stage"][low:high] = total / s["tokens"][0:1, 0:1]
            for number in range(low, high):
                local_waits.append(local_copy(s["stage"].at[number], targets[number]))
        return emit

    def emit_small(total):
        value = total / s["tokens"][0:1, 0:1]
        grad_bias_ref[...] = value[0:6, 0:ROWS]
        grad_gain_ref[...] = value[6:9, 0:ROWS]
        grad_shift_ref[...] = value[9:12, 0:ROWS]
        grad_reduce_bias_ref[...] = value[12:13, 0:ROWS]
        grad_expand_bias_ref[...] = value[13:14, 0:share]

    scatters = []
    for number, (low, high, order) in enumerate(SCATTER_CHUNKS):
        parts, landings, emit = [(s["gw"], (slice(low, high),))], [s["land"][number]], [emit_weight(low, high)]
        if number == len(SCATTER_CHUNKS) - 1:
            parts.append((s["gsmall"], ()))
            landings.append(s["land_small"])
            emit.append(emit_small)
        scatters.append(Scatter(links, place, grid, order, parts, landings, emit))

    def gather(*numbers):
        for number in numbers:
            gathers[number].step()

    def need(*numbers):
        for number in numbers:
            while not gathers[number].over:
                gathers[number].step()

    def scatter(*numbers):
        for number in numbers:
            scatters[number].step()

    def arrived(copies):
        for copy in copies:
            copy.wait()

    def arrived_memory(slot):
        for wait in memory_waits[slot]:
            wait.wait_recv()

    s["rows_grad"][...] = jnp.zeros_like(s["rows_grad"])
    gather(0, 1, 2, 3, 4, 5, 6, 7)
    send_memory(0, 0)
    gather(0, 1, 3, 4, 2, 5, 7)
    send_memory(0, 1)
    gather(6, 2, 7, 0, 6, 1, 0, 2)
    send_memory(1, 0)
    gather(0)
    need(0)
    unpack_small()
    gather(3, 2, 1, 6)
    send_memory(1, 1)
    gather(1)
    need(1)
    arrived(own_rows)
    self_project()
    gather(4)
    self_attend()
    gather(3, 6)
    self_close()
    need(2)
    arrived([own_memory])
    arrived_memory(0)
    cross_memory(0)
    gather(5, 3)
    need(3)
    cross_query()
    cross_attend(0)
    gather(4)
    arrived_memory(1)
    cross_memory(1)
    cross_attend(1)
    gather(5, 4)
    cross_close()
    need(4)
    ff_up(0)
    gather(7)
    ff_up(1)
    gather(5)
    need(5)
    ff_up(2)
    ff_up(3)
    need(6)
    ff_down(0)
    ff_down(1)
    gather(7)
    need(7)
    ff_down(2)
    ff_down(3)
    close()
    reduce_grad(3)
    reduce_grad(2)
    scatter(0)
    reduce_grad(1)
    reduce_grad(0)
    scatter(1)
    ff_back(3)
    ff_back(2)
    scatter(2)
    ff_back(1)
    ff_back(0)
    scatter(0, 3, 1)
    cross_open()
    scatter(2)
    cross_back(0)
    scatter(3)
    memory_grad(0)
    send_memory_grad(0)
    scatter(0)
    cross_back(1)
    scatter(1)
    memory_grad(1)
    send_memory_grad(1)
    scatter(2)
    cross_query_grad()
    scatter(4)
    memory_weight_grad()
    scatter(4, 5, 3, 0, 2)
    self_open()
    self_back()
    scatter(5, 1)
    self_grads()
    pack_small()
    scatter(6, 4, 7)
    input_grad()
    scatter(3, 6, 7, 0, 2, 1, 5, 3, 4, 6, 7, 4, 5, 7, 5, 6, 7, 6)
    for work in scatters:
        while not work.over:
            work.step()
    for wait in grad_waits:
        wait.wait_recv()
    for wait in local_waits:
        wait.wait()
    links.finish()


def copy_count(grid, members, slots):
    count = 0
    for index, (_, _, order) in enumerate(GATHER_CHUNKS):
        count += sum(grid[axis] - 1 for axis in order) * (2 if index == 0 else 1)
    for index, (_, _, order) in enumerate(SCATTER_CHUNKS):
        count += sum(grid[axis] - 1 for axis in order) * (2 if index == len(SCATTER_CHUNKS) - 1 else 1)
    return count + (members - 1) * (2 * slots + slots)


def run_layer(sizes, grid, scalars, small, large):
    x, memory = large[0], large[-1]
    slots, span, width = x.shape
    rows = slots * span
    members = sizes["x"] * sizes["c"]
    chunk = memory.shape[1]
    pairs = width // HD // 2
    ff_blocks = (BLOCKS - EXPAND) // 2
    place = tuple(grid[axis] for axis in AXES)
    mem_shape = (slots, members, chunk, width)
    count = copy_count(grid, members, slots)
    scratch = {
        "w": pltpu.VMEM((BLOCKS,) + place + (ROWS, width), BF16),
        "small": pltpu.VMEM(place + (ROWS, LANES), BF16),
        "packet": pltpu.VMEM((ROWS, LANES), F32),
        "gw": pltpu.VMEM((BLOCKS,) + place + (ROWS, width), BF16),
        "gsmall": pltpu.VMEM(place + (ROWS, LANES), BF16),
        "stage": pltpu.VMEM((BLOCKS, ROWS, width), F32),
        "land": [
            landing_shapes(grid, order, (high - low,), (ROWS, width)) for low, high, order in SCATTER_CHUNKS
        ],
        "land_small": landing_shapes(grid, SCATTER_CHUNKS[-1][2], (), (ROWS, LANES)),
        "pc": pltpu.VMEM((slots, pairs, 2 * span, members * chunk), BF16),
        "ps": pltpu.VMEM((slots, pairs, 2 * span, span), BF16),
        "f": pltpu.VMEM((ff_blocks, rows, width), BF16),
        "slope": pltpu.VMEM((ff_blocks, rows, width), F32),
        "rows": pltpu.VMEM((ROWS, width), F32),
        "rows_grad": pltpu.VMEM((ROWS, width), F32),
        "ebias": pltpu.VMEM((1, width * ff_blocks), F32),
        "ebias_grad": pltpu.VMEM((1, width * ff_blocks), F32),
        "tokens": pltpu.VMEM((8, LANES), F32),
        "acc": pltpu.VMEM((width, width), F32),
        "d1": pltpu.VMEM((rows, 1), F32),
        "d2": pltpu.VMEM((rows, 1), F32),
        "send": pltpu.SemaphoreType.DMA((count,)),
        "recv": pltpu.SemaphoreType.DMA((count,)),
        "local": pltpu.SemaphoreType.DMA((2 * BLOCKS + 5 + slots,)),
    }
    for name in ("mem", "k2", "v2", "dk2", "dv2", "gmem"):
        scratch[name] = pltpu.VMEM(mem_shape, BF16)
    for name in ("q", "k", "v", "a", "h1b", "q2", "a2", "h2b", "e", "da", "dq", "dk", "dv"):
        scratch[name] = pltpu.VMEM((rows, width), BF16)
    for name in ("n1", "n2", "h1", "r3", "dr"):
        scratch[name] = pltpu.VMEM((rows, width), F32)
    for name in ("x", "dy", "y", "dx"):
        scratch[name] = pltpu.VMEM(x.shape, BF16)
    leaves, tree = jax.tree.flatten(scratch)

    def kernel(*refs):
        fixed = refs[: len(refs) - len(leaves)]
        layer_kernel(sizes, grid, *fixed, jax.tree.unflatten(tree, refs[len(fixed) :]))

    vmem, smem = pl.BlockSpec(memory_space=pltpu.VMEM), pl.BlockSpec(memory_space=pltpu.SMEM)
    anywhere = pl.BlockSpec(memory_space=pl.ANY)
    outs = [(part.shape, F32) for part in small]
    outs += [(x.shape, BF16), (x.shape, BF16)] + [(part.shape, F32) for part in large[2:6]] + [(memory.shape, BF16)]
    return pl.pallas_call(
        kernel,
        out_shape=tuple(jax.ShapeDtypeStruct(shape, dtype) for shape, dtype in outs),
        in_specs=[smem] * len(scalars) + [vmem] * len(small) + [anywhere] * len(large),
        out_specs=[vmem] * len(small) + [anywhere] * len(large),
        scratch_shapes=leaves,
        compiler_params=pltpu.CompilerParams(
            collective_id=0, has_side_effects=True, vmem_limit_bytes=62 << 20
        ),
    )(*scalars, *small, *large)


def copy_kernel(*refs):
    count = (len(refs) - 1) // 3
    sources, targets, held, sems = refs[:count], refs[count : 2 * count], refs[2 * count : -1], refs[-1]
    inward = [pltpu.make_async_copy(sources[n], held[n], sems.at[0, n]) for n in range(count)]
    outward = [pltpu.make_async_copy(held[n], targets[n], sems.at[1, n]) for n in range(count)]
    for copy in inward:
        copy.start()
    for came, goes in zip(inward, outward):
        came.wait()
        goes.start()
    for copy in outward:
        copy.wait()


def handed_out(results):
    anywhere = pl.BlockSpec(memory_space=pl.ANY)
    return pl.pallas_call(
        copy_kernel,
        out_shape=tuple(jax.ShapeDtypeStruct(part.shape, part.dtype) for part in results),
        in_specs=[anywhere] * len(results),
        out_specs=[anywhere] * len(results),
        scratch_shapes=[pltpu.VMEM(part.shape, part.dtype) for part in results]
        + [pltpu.SemaphoreType.DMA((2, len(results)))],
        compiler_params=pltpu.CompilerParams(vmem_limit_bytes=62 << 20),
    )(*results)


def shards(
    sizes,
    decoder_in, memory, grad_out, decoder_lengths, memory_lengths, item_route,
    in_projection, out_projection, attention_bias, expand_weight, expand_bias,
    reduce_weight, reduce_bias, norm_gain, norm_bias,
):
    joined = in_projection.shape[1] < ROWS
    small = [attention_bias, norm_gain, norm_bias, reduce_bias[None], expand_bias[None]]
    weights = [in_projection, out_projection, expand_weight, reduce_weight.T]
    along = (1, 1, 0, 0)
    lengths, routes = decoder_lengths, item_route
    grid = dict(sizes)
    if joined:
        grid.update(x=1, c=1)
        small = [lax.all_gather(part, "mem", axis=1, tiled=True) for part in small]
        weights = [lax.all_gather(part, "mem", axis=axis, tiled=True) for part, axis in zip(weights, along)]
        lengths = lax.all_gather(lengths, "mem", tiled=True)
        routes = lax.all_gather(routes, "mem", tiled=True)
    results = run_layer(
        sizes, grid, (decoder_lengths, memory_lengths, item_route, lengths, routes), small,
        [decoder_in, grad_out] + weights + [memory],
    )
    if joined:
        results = list(results)
        for number in range(5):
            results[number] = lax.psum_scatter(results[number], "mem", scatter_dimension=1, tiled=True)
        for number, axis in zip(range(7, 11), along):
            results[number] = lax.psum_scatter(results[number], "mem", scatter_dimension=axis, tiled=True)
    else:
        results = handed_out(results)
    bias, gain, shift, reduce_shift, expand_shift, out, dx, g_in, g_out, g_expand, g_reduce, g_memory = results
    return (
        out, dx, g_memory, g_in, g_out, bias, g_expand, expand_shift[0], g_reduce.T, reduce_shift[0], gain, shift,
    )


def solution(mesh):
    both = ("bucket", "mem")
    buckets, members = mesh.shape["bucket"], mesh.shape["mem"]
    cores = 2
    across = members // cores
    sizes = {"z": buckets // across, "y": across, "x": across, "c": cores}
    in_specs = (
        P(both, None, None), P("bucket", "mem", None), P(both, None, None), P(both), P(both), P(both),
        P(None, both, None), P(None, both, None), P(None, both), P(both, None), P(both),
        P(None, both), P(both), P(None, both), P(None, both),
    )
    out_specs = (
        P(both, None, None), P(both, None, None), P("bucket", "mem", None),
        P(None, both, None), P(None, both, None), P(None, both), P(both, None), P(both),
        P(None, both), P(both), P(None, both), P(None, both),
    )
    return jax.shard_map(
        functools.partial(shards, sizes), mesh=mesh, in_specs=in_specs, out_specs=out_specs, check_vma=False
    )
```

```python
import functools

import jax
import jax.numpy as jnp
from jax import lax
from jax.experimental import pallas as pl
from jax.experimental.pallas import tpu as pltpu
from jax.sharding import PartitionSpec as P

HD = 64
EPS = 1e-05
NEG = -1e30
F32 = jnp.float32
BF16 = jnp.bfloat16
MESH = pl.DeviceIdType.MESH
LANES = 128
ROWS = 16

SQ, SK, SV, SO, CK, CV, CQ, CO, EXPAND, REDUCE = 0, 1, 2, 3, 4, 5, 6, 7, 8, 12
BLOCKS = 16
GATHER_CHUNKS = (
    (0, 1, "zxyc"), (6, 8, "xyzc"), (2, 3, "zyxc"), (1, 2, "zxyc"), (8, 10, "xzyc"),
    (12, 14, "xyzc"), (14, 15, "zxyc"), (3, 4, "zxyc"), (4, 6, "zxyc"), (10, 12, "zxyc"),
    (15, 16, "zxyc"),
)
SCATTER_CHUNKS = (
    (15, 16, "cxyz"), (14, 15, "czyx"), (12, 14, "cyzx"), (10, 12, "cxyz"), (8, 10, "cyzx"),
    (7, 8, "czxy"), (6, 7, "cyzx"), (4, 6, "cyxz"), (3, 4, "cyzx"), (0, 1, "cyxz"),
    (1, 2, "cyxz"), (2, 3, "czyx"),
)
AXES = "zyxc"


def mm(left, right):
    return lax.dot_general(left, right, (((1,), (0,)), ((), ())), preferred_element_type=F32)


def mm_nt(left, right):
    return lax.dot_general(left, right, (((1,), (1,)), ((), ())), preferred_element_type=F32)


def mm_tn(left, right):
    return lax.dot_general(left, right, (((0,), (0,)), ((), ())), preferred_element_type=F32)


class Links:
    def __init__(self, send_sems, recv_sems):
        self.send_sems, self.recv_sems, self.used, self.sent = send_sems, recv_sems, 0, []

    def pair(self):
        self.used += 1
        return self.send_sems.at[self.used - 1], self.recv_sems.at[self.used - 1]

    def copy(self, source, target, landing, device):
        send, recv = self.pair()
        out = pltpu.make_async_remote_copy(
            src_ref=source, dst_ref=target, send_sem=send, recv_sem=recv,
            device_id=device, device_id_type=MESH,
        )
        out.start()
        self.sent.append(out)
        return pltpu.make_async_remote_copy(
            src_ref=source, dst_ref=landing, send_sem=send, recv_sem=recv,
            device_id=device, device_id_type=MESH,
        )

    def finish(self):
        for out in self.sent:
            out.wait_send()


class Place:
    def __init__(self, sizes):
        self.sizes = sizes
        bucket, mem = lax.axis_index("bucket"), lax.axis_index("mem")
        self.bucket, self.mem = bucket, mem
        self.at = {
            "z": bucket // sizes["y"], "y": bucket % sizes["y"],
            "x": mem // sizes["c"], "c": mem % sizes["c"],
        }

    def shifted(self, axis, step):
        size = self.sizes[axis]
        return lax.rem(self.at[axis] + (step % size), size)

    def device(self, axis, step):
        at = dict(self.at)
        at[axis] = self.shifted(axis, step)
        return (at["z"] * self.sizes["y"] + at["y"], at["x"] * self.sizes["c"] + at["c"])


def block_view(ref, lead, index):
    return ref.at[tuple(lead) + tuple(index[axis] for axis in AXES)]


class Gather:
    def __init__(self, links, place, grid, order, parts):
        self.links, self.place, self.parts = links, place, parts
        self.order = [axis for axis in order if grid[axis] > 1]
        self.grid, self.waits, self.done = grid, [], 0

    @property
    def over(self):
        return self.done > len(self.order)

    def step(self):
        if self.over:
            return
        for wait in self.waits:
            wait.wait_recv()
        self.waits = []
        if self.done < len(self.order):
            axis = self.order[self.done]
            known = self.order[: self.done]
            for hop in range(1, self.grid[axis]):
                mine, theirs = {}, {}
                for other in AXES:
                    if other in known:
                        mine[other] = theirs[other] = slice(None)
                    else:
                        at = self.place.at[other] if self.grid[other] > 1 else 0
                        mine[other] = theirs[other] = at
                theirs[axis] = self.place.shifted(axis, -hop)
                for ref, lead in self.parts:
                    self.waits.append(
                        self.links.copy(
                            block_view(ref, lead, mine), block_view(ref, lead, mine),
                            block_view(ref, lead, theirs), self.place.device(axis, hop),
                        )
                    )
        self.done += 1


class Scatter:
    def __init__(self, links, place, grid, order, parts, landings, emit):
        self.links, self.place, self.parts, self.landings = links, place, parts, landings
        self.order = [axis for axis in order if grid[axis] > 1]
        self.grid, self.waits, self.done, self.emit = grid, [], 0, emit

    def index(self, known):
        return {
            axis: (self.place.at[axis] if self.grid[axis] > 1 else 0) if axis in known or self.grid[axis] == 1
            else slice(None)
            for axis in AXES
        }

    @property
    def over(self):
        return self.done > len(self.order)

    def step(self):
        if self.over:
            return
        for wait in self.waits:
            wait.wait_recv()
        self.waits = []
        if self.done > 0:
            axis = self.order[self.done - 1]
            last = self.done == len(self.order)
            index = self.index(self.order[: self.done])
            for number, (ref, lead) in enumerate(self.parts):
                where = tuple(lead) + tuple(index[name] for name in AXES)
                landed = self.landings[number][self.done - 1]
                if self.grid[axis] == 2 and not last:
                    ref[where] = ref[where] + landed[0]
                    continue
                total = ref[where].astype(F32)
                for hop in range(1, self.grid[axis]):
                    total += landed[hop - 1].astype(F32)
                if last:
                    self.emit[number](total)
                else:
                    ref[where] = total.astype(ref.dtype)
        if self.done < len(self.order):
            axis = self.order[self.done]
            known = self.order[: self.done]
            for hop in range(1, self.grid[axis]):
                theirs = self.index(known)
                theirs[axis] = self.place.shifted(axis, hop)
                for number, (ref, lead) in enumerate(self.parts):
                    landing = self.landings[number][self.done].at[hop - 1]
                    self.waits.append(
                        self.links.copy(
                            block_view(ref, lead, theirs), landing, landing, self.place.device(axis, hop)
                        )
                    )
        self.done += 1


def landing_shapes(grid, order, lead_shape, tail_shape):
    shapes, left = [], {axis: grid[axis] for axis in AXES}
    for axis in order:
        if grid[axis] == 1:
            continue
        left[axis] = 1
        kept = tuple(left[name] for name in AXES if left[name] > 1)
        shapes.append(pltpu.VMEM((grid[axis] - 1,) + lead_shape + kept + tail_shape, BF16))
    return shapes


def layer_kernel(
    sizes, grid,
    lengths_ref, reaches_ref, routes_ref, all_lengths_ref, all_routes_ref,
    attention_bias_ref, gain_ref, shift_ref, reduce_bias_ref, expand_bias_ref,
    x_hbm, dy_hbm, in_hbm, out_hbm, expand_hbm, reduce_hbm, memory_ref,
    grad_bias_ref, grad_gain_ref, grad_shift_ref, grad_reduce_bias_ref, grad_expand_bias_ref,
    y_hbm, dx_hbm, grad_in_hbm, grad_out_hbm, grad_expand_hbm, grad_reduce_hbm, gmem_ref,
    scratch,
):
    s = scratch
    place = Place(sizes)
    links = Links(s["send"], s["recv"])
    x_ref, dy_ref = s["x"], s["dy"]
    slots, span, width = x_ref.shape
    rows = slots * span
    members, chunk = s["mem"].shape[1], s["mem"].shape[2]
    reach_span = members * chunk
    heads = width // HD
    pairs = heads // 2
    ff_blocks = (BLOCKS - EXPAND) // 2
    places = width // ROWS
    locals_used = [0]

    def local_copy(source, target):
        locals_used[0] += 1
        copy = pltpu.make_async_copy(source, target, s["local"].at[locals_used[0] - 1])
        copy.start()
        return copy

    barrier = pltpu.get_barrier_semaphore()
    peers = []
    for axis in "zy":
        peers += [place.device(axis, hop) for hop in range(1, sizes[axis])]
    others = [lax.rem(place.mem + hop, members) for hop in range(1, members)]
    peers += [(place.bucket, other) for other in others]
    for peer in peers:
        pl.semaphore_signal(barrier, inc=1, device_id=peer, device_id_type=MESH)

    here = tuple(place.at[axis] if grid[axis] > 1 else 0 for axis in AXES)

    def block_parts(in_ref, out_ref, expand_ref, reduce_ref):
        parts = [(SQ + k, in_ref.at[k]) for k in range(3)] + [(CQ, in_ref.at[3]), (CK, in_ref.at[4])]
        parts += [(CV, in_ref.at[5]), (SO, out_ref.at[0]), (CO, out_ref.at[1])]
        for k in range(ff_blocks):
            lanes = pl.ds(k * width, width)
            parts += [(EXPAND + k, expand_ref.at[:, lanes]), (REDUCE + k, reduce_ref.at[:, lanes])]
        return sorted(parts, key=lambda part: part[0])

    own = [
        local_copy(part, s["w"].at[(number,) + here])
        for number, part in block_parts(in_hbm, out_hbm, expand_hbm, reduce_hbm)
    ]
    own_rows = [local_copy(x_hbm, x_ref), local_copy(dy_hbm, dy_ref)]
    own_memory = local_copy(memory_ref.at[pl.ds(place.mem * slots, slots)], s["mem"].at[:, place.mem])

    spot = here[0]
    for axis, at in zip(AXES[1:], here[1:]):
        spot = spot * grid[axis] + at
    share = expand_bias_ref.shape[1]
    group, pieces = LANES // ROWS, LANES // share
    packet = s["packet"]
    packet[...] = jnp.zeros_like(packet)
    packet[0:6, 0:ROWS] = attention_bias_ref[...].astype(F32)
    packet[6:9, 0:ROWS] = gain_ref[...].astype(F32)
    packet[9:12, 0:ROWS] = shift_ref[...].astype(F32)
    packet[12:13, 0:ROWS] = reduce_bias_ref[...].astype(F32)
    packet[13:14, 0:share] = expand_bias_ref[...].astype(F32)
    narrow = pltpu.roll(packet[...], lax.rem(spot, group) * ROWS, 1)
    wide = pltpu.roll(packet[...], lax.rem(spot, pieces) * share, 1)
    row = lax.broadcasted_iota(jnp.int32, (ROWS, LANES), 0)
    lane = lax.broadcasted_iota(jnp.int32, (ROWS, LANES), 1)
    live = jnp.zeros((ROWS, LANES), jnp.int32)
    for slot in range(all_lengths_ref.shape[0]):
        count = jnp.where(all_routes_ref[slot] >= 0, all_lengths_ref[slot], 0)
        live = jnp.where(lane == slot, count, live)
    value = jnp.where(row == 13, wide, jnp.where(row == 14, live.astype(F32), narrow))
    s["small"][here] = value.astype(BF16)
    for copy in own:
        copy.wait()
    pl.semaphore_wait(barrier, len(peers))

    gathers = []
    for low, high, order in GATHER_CHUNKS:
        parts = [(s["w"], (slice(low, high),))]
        if low == 0:
            parts.append((s["small"], ()))
        gathers.append(Gather(links, place, grid, order, parts))
    memory_waits = [[] for _ in range(slots)]
    half = chunk // 2

    def send_memory(slot, part):
        at = pl.ds(part * half, half)
        for hop, other in zip(range(1, members), others):
            sender = lax.rem(place.mem + members - hop, members)
            memory_waits[slot].append(
                links.copy(
                    memory_ref.at[other * slots + slot, at], s["mem"].at[slot, place.mem, at],
                    s["mem"].at[slot, sender, at], (place.bucket, other),
                )
            )

    def weight(number):
        return s["w"][number].reshape(width, width)

    def put_grad(number, value):
        ref = s["gw"]
        ref[number] = value.astype(BF16).reshape(ref.shape[1:])

    even_lanes = lax.broadcasted_iota(jnp.int32, (1, LANES), 1) < HD
    even = jnp.where(even_lanes, 1.0, 0.0)
    odd = 1.0 - even
    scale = HD ** (-0.5)

    def stack(value, factor=1.0):
        return jnp.concatenate([value * (even * factor).astype(BF16), value * (odd * factor).astype(BF16)], axis=0)

    def unstack(value, factor=1.0):
        return value[:span] * (even * factor) + value[span:] * (odd * factor)

    def normed(value):
        centered = value - jnp.mean(value, axis=-1, keepdims=True)
        rstd = lax.rsqrt(jnp.mean(centered * centered, axis=-1, keepdims=True) + EPS)
        return centered * rstd, rstd

    def norm_back(grad, unit, rstd, number):
        s["rows_grad"][6 + number : 7 + number, :] = jnp.sum(grad * unit, axis=0, keepdims=True)
        s["rows_grad"][9 + number : 10 + number, :] = jnp.sum(grad, axis=0, keepdims=True)
        scaled = grad * s["rows"][6 + number : 7 + number, :]
        return (
            scaled - jnp.mean(scaled, axis=-1, keepdims=True)
            - unit * jnp.mean(scaled * unit, axis=-1, keepdims=True)
        ) * rstd

    def column_sum(value):
        return jnp.sum(value.astype(F32), axis=0, keepdims=True)

    def bias(number):
        return s["rows"][number : number + 1, :]

    def unpack_small():
        every = s["small"][...].reshape(places, ROWS, LANES).astype(F32)
        columns = [jnp.sum(every[g * group : (g + 1) * group], axis=0) for g in range(places // group)]
        s["rows"][...] = jnp.concatenate(columns, axis=1)
        columns = [
            jnp.sum(every[g * pieces : (g + 1) * pieces, 13], axis=0, keepdims=True) for g in range(places // pieces)
        ]
        s["ebias"][...] = jnp.concatenate(columns, axis=1)
        tokens = jnp.sum(jnp.sum(every[:, 14], axis=0, keepdims=True), axis=1, keepdims=True)
        s["tokens"][...] = jnp.broadcast_to(tokens, s["tokens"].shape)

    def self_project():
        x = x_ref[...].reshape(rows, width)
        s["q"][...] = (mm(x, weight(SQ)) + bias(0)).astype(BF16)
        s["k"][...] = mm(x, weight(SK)).astype(BF16)
        s["v"][...] = (mm(x, weight(SV)) + bias(1)).astype(BF16)

    def attend(low_ref, share_ref, mixed_ref, queries, keys_in, values_in, keep, at, lanes):
        scores = jnp.where(keep, mm_nt(stack(queries, scale), keys_in), NEG)
        weights = jnp.exp(scores - jnp.max(scores, axis=-1, keepdims=True))
        part = 1.0 / jnp.sum(weights, axis=-1, keepdims=True)
        low = weights.astype(BF16)
        low_ref[...] = low
        share_ref[...] = part
        mixed_ref[at, lanes] = unstack(mm(low, values_in) * part)

    def attend_back(low_ref, share_ref, mixed, da, queries, keys_in, values_in):
        low, part = low_ref[...], share_ref[...]
        da = stack(da).astype(F32) * part
        delta = jnp.sum(da * jnp.concatenate([mixed, mixed], axis=0), axis=-1, keepdims=True)
        da = da.astype(BF16)
        ds = (low.astype(F32) * (mm_nt(da, values_in) - delta)).astype(BF16)
        return (
            unstack(mm(ds, keys_in), scale).astype(BF16),
            mm_tn(ds, stack(queries, scale)).astype(BF16),
            mm_tn(low, da).astype(BF16),
        )

    def self_attend():
        row = lax.broadcasted_iota(jnp.int32, (2 * span, span), 0) % span
        col = lax.broadcasted_iota(jnp.int32, (2 * span, span), 1)
        for slot in range(slots):
            keep = (col <= row) & (col < lengths_ref[slot])
            at = slice(slot * span, (slot + 1) * span)
            for pair in range(pairs):
                lanes = slice(pair * LANES, (pair + 1) * LANES)
                attend(
                    s["ps"].at[slot, pair], s["share"].at[slot, pair], s["af"],
                    s["q"][at, lanes], s["k"][at, lanes], s["v"][at, lanes], keep, at, lanes,
                )
        s["a"][...] = s["af"][...].astype(BF16)

    def self_close():
        x = x_ref[...].reshape(rows, width).astype(F32)
        unit, rstd = normed(x + mm(s["a"][...], weight(SO)) + bias(2))
        s["n1"][...], s["d1"][...] = unit, rstd
        h1 = unit * bias(6) + bias(9)
        s["h1"][...] = h1
        s["h1b"][...] = h1.astype(BF16)

    def cross_query():
        s["q2"][...] = (mm(s["h1b"][...], weight(CQ)) + bias(3)).astype(BF16)

    def cross_memory(slot):
        items = s["mem"][slot].reshape(reach_span, width)
        s["k2"][slot] = mm(items, weight(CK)).astype(BF16).reshape(members, chunk, width)
        s["v2"][slot] = (mm(items, weight(CV)) + bias(4)).astype(BF16).reshape(members, chunk, width)

    def keys(name, slot, lanes):
        return s[name][slot, :, :, lanes].reshape(reach_span, LANES)

    def cross_attend(slot):
        col = lax.broadcasted_iota(jnp.int32, (1, reach_span), 1)
        keep = col < reaches_ref[slot]
        at = slice(slot * span, (slot + 1) * span)

        def body(pair, carry):
            lanes = pl.ds(pl.multiple_of(pair * LANES, LANES), LANES)
            attend(
                s["pc"].at[slot, pair], s["share2"].at[slot, pair], s["a2f"],
                s["q2"][at, lanes], keys("k2", slot, lanes), keys("v2", slot, lanes), keep, at, lanes,
            )
            return carry
        lax.fori_loop(0, pairs, body, 0)

    def cross_close():
        s["a2"][...] = s["a2f"][...].astype(BF16)
        unit, rstd = normed(s["h1"][...] + mm(s["a2"][...], weight(CO)) + bias(5))
        s["n2"][...], s["d2"][...] = unit, rstd
        h2 = unit * bias(7) + bias(10)
        s["h2b"][...] = h2.astype(BF16)
        s["r3"][...] = h2 + bias(12)

    def ff_up(block):
        lanes = slice(block * width, (block + 1) * width)
        u = mm(s["h2b"][...], weight(EXPAND + block)) + s["ebias"][:, lanes]
        sig = 1.0 / (1.0 + jnp.exp(-u))
        s["f"][block] = (u * sig).astype(BF16)
        s["slope"][block] = sig * (1.0 + u * (1.0 - sig))

    def ff_down(block):
        s["r3"][...] += mm_nt(s["f"][block], weight(REDUCE + block))

    def live_rows(each):
        row = lax.broadcasted_iota(jnp.int32, (rows, 1), 0)
        count = jnp.zeros((rows, 1), jnp.int32)
        for slot in range(slots):
            here_count = jnp.where(routes_ref[slot] >= 0, each(slot), 0)
            count = jnp.where((row >= slot * span) & (row < (slot + 1) * span), here_count + slot * span, count)
        return row < count

    def close():
        unit, rstd = normed(s["r3"][...])
        y = unit * bias(8) + bias(11)
        y = jnp.where(live_rows(lambda slot: span), y, 0.0)
        s["y"][...] = y.astype(BF16).reshape(x_ref.shape)
        local_waits.append(local_copy(s["y"], y_hbm))
        dy = dy_ref[...].reshape(rows, width).astype(F32)
        dy = jnp.where(live_rows(lambda slot: lengths_ref[slot]), dy, 0.0)
        dr3 = norm_back(dy, unit, rstd, 2)
        s["dr"][...] = dr3
        s["e"][...] = dr3.astype(BF16)
        s["rows_grad"][12:13, :] = column_sum(s["e"][...])

    def reduce_grad(block):
        put_grad(REDUCE + block, mm_tn(s["e"][...], s["f"][block]))

    def ff_back(block):
        lanes = slice(block * width, (block + 1) * width)
        du = (mm(s["e"][...], weight(REDUCE + block)) * s["slope"][block]).astype(BF16)
        s["ebias_grad"][:, lanes] = column_sum(du)
        put_grad(EXPAND + block, mm_tn(s["h2b"][...], du))
        s["dr"][...] += mm_nt(du, weight(EXPAND + block))

    def cross_open():
        dr2 = norm_back(s["dr"][...], s["n2"][...], s["d2"][...], 1)
        s["dr"][...] = dr2
        e2 = dr2.astype(BF16)
        s["rows_grad"][5:6, :] = column_sum(e2)
        put_grad(CO, mm_tn(s["a2"][...], e2))
        s["da"][...] = mm_nt(e2, weight(CO)).astype(BF16)

    def cross_back(slot):
        at = slice(slot * span, (slot + 1) * span)

        def body(pair, carry):
            lanes = pl.ds(pl.multiple_of(pair * LANES, LANES), LANES)
            shape = (members, chunk, LANES)
            dq, dk, dv = attend_back(
                s["pc"].at[slot, pair], s["share2"].at[slot, pair], s["a2f"][at, lanes], s["da"][at, lanes],
                s["q2"][at, lanes], keys("k2", slot, lanes), keys("v2", slot, lanes),
            )
            s["dq"][at, lanes] = dq
            s["dk2"][slot, :, :, lanes] = dk.reshape(shape)
            s["dv2"][slot, :, :, lanes] = dv.reshape(shape)
            return carry
        lax.fori_loop(0, pairs, body, 0)

    def memory_grad(slot):
        value = mm_nt(s["dk2"][slot].reshape(reach_span, width), weight(CK))
        value += mm_nt(s["dv2"][slot].reshape(reach_span, width), weight(CV))
        s["gmem"][slot] = value.astype(BF16).reshape(members, chunk, width)

    def send_memory_grad(slot):
        mine = gmem_ref.at[place.mem * slots + slot]
        local_waits.append(local_copy(s["gmem"].at[slot, place.mem], mine))
        for hop, other in zip(range(1, members), others):
            sender = lax.rem(place.mem + members - hop, members)
            grad_waits.append(
                links.copy(
                    s["gmem"].at[slot, other], mine, gmem_ref.at[sender * slots + slot], (place.bucket, other)
                )
            )

    local_waits, grad_waits = [], []

    def cross_query_grad():
        dq = s["dq"][...]
        s["rows_grad"][3:4, :] = column_sum(dq)
        put_grad(CQ, mm_tn(s["h1b"][...], dq))

    def memory_weight_grad():
        items = s["mem"][...].reshape(slots * reach_span, width)
        put_grad(CK, mm_tn(items, s["dk2"][...].reshape(slots * reach_span, width)))
        dv = s["dv2"][...].reshape(slots * reach_span, width)
        put_grad(CV, mm_tn(items, dv))
        s["rows_grad"][4:5, :] = column_sum(dv)

    def self_open():
        dh1 = s["dr"][...] + mm_nt(s["dq"][...], weight(CQ))
        dr1 = norm_back(dh1, s["n1"][...], s["d1"][...], 0)
        s["dr"][...] = dr1
        e1 = dr1.astype(BF16)
        s["rows_grad"][2:3, :] = column_sum(e1)
        put_grad(SO, mm_tn(s["a"][...], e1))
        s["da"][...] = mm_nt(e1, weight(SO)).astype(BF16)

    def self_back():
        for slot in range(slots):
            at = slice(slot * span, (slot + 1) * span)
            for pair in range(pairs):
                lanes = slice(pair * LANES, (pair + 1) * LANES)
                s["dq"][at, lanes], s["dk"][at, lanes], s["dv"][at, lanes] = attend_back(
                    s["ps"].at[slot, pair], s["share"].at[slot, pair], s["af"][at, lanes], s["da"][at, lanes],
                    s["q"][at, lanes], s["k"][at, lanes], s["v"][at, lanes],
                )

    def self_grads():
        x = x_ref[...].reshape(rows, width)
        put_grad(SV, mm_tn(x, s["dv"][...]))
        put_grad(SQ, mm_tn(x, s["dq"][...]))
        put_grad(SK, mm_tn(x, s["dk"][...]))
        s["rows_grad"][0:1, :] = column_sum(s["dq"][...])
        s["rows_grad"][1:2, :] = column_sum(s["dv"][...])

    def input_grad():
        total = s["dr"][...] + mm_nt(s["dq"][...], weight(SQ))
        total += mm_nt(s["dk"][...], weight(SK)) + mm_nt(s["dv"][...], weight(SV))
        s["dx"][...] = total.astype(BF16).reshape(x_ref.shape)
        local_waits.append(local_copy(s["dx"], dx_hbm))

    def turned(value, lanes):
        return value if lanes == 0 else pltpu.roll(value, LANES - lanes, 1)

    def pack_small():
        row = lax.broadcasted_iota(jnp.int32, (ROWS, LANES), 0)
        for number in range(places):
            at = number // group * LANES
            base = turned(s["rows_grad"][:, at : at + LANES], number % group * ROWS)
            at = number // pieces * LANES
            extra = turned(s["ebias_grad"][:, at : at + LANES], number % pieces * share)
            index, rest = [], number
            for axis in reversed(AXES):
                index.insert(0, rest % grid[axis])
                rest //= grid[axis]
            s["gsmall"][tuple(index)] = jnp.where(row == 13, extra, base).astype(BF16)

    targets = dict(block_parts(grad_in_hbm, grad_out_hbm, grad_expand_hbm, grad_reduce_hbm))

    def emit_weight(low, high):
        def emit(total):
            s["stage"][low:high] = total / s["tokens"][0:1, 0:1]
            for number in range(low, high):
                local_waits.append(local_copy(s["stage"].at[number], targets[number]))
        return emit

    def emit_small(total):
        value = total / s["tokens"][0:1, 0:1]
        grad_bias_ref[...] = value[0:6, 0:ROWS]
        grad_gain_ref[...] = value[6:9, 0:ROWS]
        grad_shift_ref[...] = value[9:12, 0:ROWS]
        grad_reduce_bias_ref[...] = value[12:13, 0:ROWS]
        grad_expand_bias_ref[...] = value[13:14, 0:share]

    scatters = []
    for number, (low, high, order) in enumerate(SCATTER_CHUNKS):
        parts, landings, emit = [(s["gw"], (slice(low, high),))], [s["land"][number]], [emit_weight(low, high)]
        if number == len(SCATTER_CHUNKS) - 1:
            parts.append((s["gsmall"], ()))
            landings.append(s["land_small"])
            emit.append(emit_small)
        scatters.append(Scatter(links, place, grid, order, parts, landings, emit))

    def gather(*numbers):
        for number in numbers:
            gathers[number].step()

    def need(*numbers):
        for number in numbers:
            while not gathers[number].over:
                gathers[number].step()

    def scatter(*numbers):
        for number in numbers:
            scatters[number].step()

    def arrived(copies):
        for copy in copies:
            copy.wait()

    def arrived_memory(slot):
        for wait in memory_waits[slot]:
            wait.wait_recv()

    s["rows_grad"][...] = jnp.zeros_like(s["rows_grad"])
    gather(0, 1, 2, 3, 4, 5, 6, 7, 8, 9, 10)
    send_memory(0, 0)
    gather(1, 4, 5, 0, 2, 1, 3, 5, 6, 7, 2, 0, 3, 8, 6, 7, 9, 0, 10, 2, 0)
    need(0)
    unpack_small()
    gather(3, 2, 8)
    send_memory(0, 1)
    gather(3)
    need(2, 3)
    arrived(own_rows)
    self_project()
    gather(6, 4)
    self_attend()
    gather(9, 6, 7, 10)
    send_memory(1, 0)
    gather(7)
    need(7)
    self_close()
    gather(8)
    send_memory(1, 1)
    gather(8, 1, 4, 1)
    need(1)
    cross_query()
    need(8)
    arrived([own_memory])
    arrived_memory(0)
    cross_memory(0)
    cross_attend(0)
    gather(4)
    arrived_memory(1)
    cross_memory(1)
    gather(9)
    cross_attend(1)
    gather(5, 10, 9)
    cross_close()
    need(4)
    ff_up(0)
    ff_up(1)
    need(9)
    ff_up(2)
    ff_up(3)
    gather(5)
    need(5)
    ff_down(0)
    gather(10)
    ff_down(1)
    need(6)
    ff_down(2)
    need(10)
    ff_down(3)
    close()
    reduce_grad(3)
    scatter(0)
    reduce_grad(2)
    scatter(1)
    reduce_grad(1)
    reduce_grad(0)
    scatter(2)
    ff_back(3)
    ff_back(2)
    scatter(0, 1, 3)
    ff_back(1)
    scatter(2)
    ff_back(0)
    scatter(4)
    cross_open()
    scatter(3, 5)
    cross_back(0)
    scatter(5, 0, 4)
    memory_grad(0)
    send_memory_grad(0)
    scatter(2, 1)
    cross_back(1)
    scatter(3, 0)
    memory_grad(1)
    send_memory_grad(1)
    cross_query_grad()
    scatter(6)
    memory_weight_grad()
    scatter(7, 6, 4, 1, 5)
    self_open()
    scatter(8, 3, 7)
    self_back()
    scatter(8, 2, 0, 6)
    self_grads()
    pack_small()
    scatter(9, 10, 11)
    input_grad()
    scatter(9, 10, 4, 11, 7, 3, 8, 6, 1, 5, 9, 2, 4, 10, 5, 7, 6, 11, 9, 10, 8, 11, 8, 7, 11, 9, 10)
    for work in scatters:
        while not work.over:
            work.step()
    for wait in grad_waits:
        wait.wait_recv()
    for wait in local_waits:
        wait.wait()
    links.finish()


def copy_count(grid, members, slots):
    count = 0
    for low, _, order in GATHER_CHUNKS:
        count += sum(grid[axis] - 1 for axis in order) * (2 if low == 0 else 1)
    for index, (_, _, order) in enumerate(SCATTER_CHUNKS):
        count += sum(grid[axis] - 1 for axis in order) * (2 if index == len(SCATTER_CHUNKS) - 1 else 1)
    return count + (members - 1) * (2 * slots + slots)


def run_layer(sizes, grid, scalars, small, large):
    x, memory = large[0], large[-1]
    slots, span, width = x.shape
    rows = slots * span
    members = sizes["x"] * sizes["c"]
    chunk = memory.shape[1]
    pairs = width // HD // 2
    ff_blocks = (BLOCKS - EXPAND) // 2
    place = tuple(grid[axis] for axis in AXES)
    mem_shape = (slots, members, chunk, width)
    count = copy_count(grid, members, slots)
    scratch = {
        "w": pltpu.VMEM((BLOCKS,) + place + (ROWS, width), BF16),
        "small": pltpu.VMEM(place + (ROWS, LANES), BF16),
        "packet": pltpu.VMEM((ROWS, LANES), F32),
        "gw": pltpu.VMEM((BLOCKS,) + place + (ROWS, width), BF16),
        "gsmall": pltpu.VMEM(place + (ROWS, LANES), BF16),
        "stage": pltpu.VMEM((BLOCKS, ROWS, width), F32),
        "land": [
            landing_shapes(grid, order, (high - low,), (ROWS, width)) for low, high, order in SCATTER_CHUNKS
        ],
        "land_small": landing_shapes(grid, SCATTER_CHUNKS[-1][2], (), (ROWS, LANES)),
        "pc": pltpu.VMEM((slots, pairs, 2 * span, members * chunk), BF16),
        "ps": pltpu.VMEM((slots, pairs, 2 * span, span), BF16),
        "share": pltpu.VMEM((slots, pairs, 2 * span, 1), F32),
        "share2": pltpu.VMEM((slots, pairs, 2 * span, 1), F32),
        "f": pltpu.VMEM((ff_blocks, rows, width), BF16),
        "slope": pltpu.VMEM((ff_blocks, rows, width), F32),
        "rows": pltpu.VMEM((ROWS, width), F32),
        "rows_grad": pltpu.VMEM((ROWS, width), F32),
        "ebias": pltpu.VMEM((1, width * ff_blocks), F32),
        "ebias_grad": pltpu.VMEM((1, width * ff_blocks), F32),
        "tokens": pltpu.VMEM((8, LANES), F32),
        "d1": pltpu.VMEM((rows, 1), F32),
        "d2": pltpu.VMEM((rows, 1), F32),
        "send": pltpu.SemaphoreType.DMA((count,)),
        "recv": pltpu.SemaphoreType.DMA((count,)),
        "local": pltpu.SemaphoreType.DMA((2 * BLOCKS + 5 + slots,)),
    }
    for name in ("mem", "k2", "v2", "dk2", "dv2", "gmem"):
        scratch[name] = pltpu.VMEM(mem_shape, BF16)
    for name in ("q", "k", "v", "a", "h1b", "q2", "a2", "h2b", "e", "da", "dq", "dk", "dv"):
        scratch[name] = pltpu.VMEM((rows, width), BF16)
    for name in ("n1", "n2", "h1", "r3", "dr", "af", "a2f"):
        scratch[name] = pltpu.VMEM((rows, width), F32)
    for name in ("x", "dy", "y", "dx"):
        scratch[name] = pltpu.VMEM(x.shape, BF16)
    leaves, tree = jax.tree.flatten(scratch)

    def kernel(*refs):
        fixed = refs[: len(refs) - len(leaves)]
        layer_kernel(sizes, grid, *fixed, jax.tree.unflatten(tree, refs[len(fixed) :]))

    vmem, smem = pl.BlockSpec(memory_space=pltpu.VMEM), pl.BlockSpec(memory_space=pltpu.SMEM)
    anywhere = pl.BlockSpec(memory_space=pl.ANY)
    outs = [(part.shape, F32) for part in small]
    outs += [(x.shape, BF16), (x.shape, BF16)] + [(part.shape, F32) for part in large[2:6]] + [(memory.shape, BF16)]
    return pl.pallas_call(
        kernel,
        out_shape=tuple(jax.ShapeDtypeStruct(shape, dtype) for shape, dtype in outs),
        in_specs=[smem] * len(scalars) + [vmem] * len(small) + [anywhere] * len(large),
        out_specs=[vmem] * len(small) + [anywhere] * len(large),
        scratch_shapes=leaves,
        compiler_params=pltpu.CompilerParams(
            collective_id=0, has_side_effects=True, vmem_limit_bytes=62 << 20
        ),
    )(*scalars, *small, *large)


def copy_kernel(*refs):
    count = (len(refs) - 1) // 3
    sources, targets, held, sems = refs[:count], refs[count : 2 * count], refs[2 * count : -1], refs[-1]
    inward = [pltpu.make_async_copy(sources[n], held[n], sems.at[0, n]) for n in range(count)]
    outward = [pltpu.make_async_copy(held[n], targets[n], sems.at[1, n]) for n in range(count)]
    for copy in inward:
        copy.start()
    for came, goes in zip(inward, outward):
        came.wait()
        goes.start()
    for copy in outward:
        copy.wait()


def handed_out(results):
    anywhere = pl.BlockSpec(memory_space=pl.ANY)
    return pl.pallas_call(
        copy_kernel,
        out_shape=tuple(jax.ShapeDtypeStruct(part.shape, part.dtype) for part in results),
        in_specs=[anywhere] * len(results),
        out_specs=[anywhere] * len(results),
        scratch_shapes=[pltpu.VMEM(part.shape, part.dtype) for part in results]
        + [pltpu.SemaphoreType.DMA((2, len(results)))],
        compiler_params=pltpu.CompilerParams(vmem_limit_bytes=62 << 20),
    )(*results)


def shards(
    sizes,
    decoder_in, memory, grad_out, decoder_lengths, memory_lengths, item_route,
    in_projection, out_projection, attention_bias, expand_weight, expand_bias,
    reduce_weight, reduce_bias, norm_gain, norm_bias,
):
    joined = in_projection.shape[1] < ROWS
    small = [attention_bias, norm_gain, norm_bias, reduce_bias[None], expand_bias[None]]
    weights = [in_projection, out_projection, expand_weight, reduce_weight.T]
    along = (1, 1, 0, 0)
    lengths, routes = decoder_lengths, item_route
    grid = dict(sizes)
    if joined:
        grid.update(x=1, c=1)
        small = [lax.all_gather(part, "mem", axis=1, tiled=True) for part in small]
        weights = [lax.all_gather(part, "mem", axis=axis, tiled=True) for part, axis in zip(weights, along)]
        lengths = lax.all_gather(lengths, "mem", tiled=True)
        routes = lax.all_gather(routes, "mem", tiled=True)
    results = run_layer(
        sizes, grid, (decoder_lengths, memory_lengths, item_route, lengths, routes), small,
        [decoder_in, grad_out] + weights + [memory],
    )
    if joined:
        results = list(results)
        for number in range(5):
            results[number] = lax.psum_scatter(results[number], "mem", scatter_dimension=1, tiled=True)
        for number, axis in zip(range(7, 11), along):
            results[number] = lax.psum_scatter(results[number], "mem", scatter_dimension=axis, tiled=True)
    else:
        results = handed_out(results)
    bias, gain, shift, reduce_shift, expand_shift, out, dx, g_in, g_out, g_expand, g_reduce, g_memory = results
    return (
        out, dx, g_memory, g_in, g_out, bias, g_expand, expand_shift[0], g_reduce.T, reduce_shift[0], gain, shift,
    )


def solution(mesh):
    both = ("bucket", "mem")
    buckets, members = mesh.shape["bucket"], mesh.shape["mem"]
    cores = 2
    across = members // cores
    sizes = {"z": buckets // across, "y": across, "x": across, "c": cores}
    in_specs = (
        P(both, None, None), P("bucket", "mem", None), P(both, None, None), P(both), P(both), P(both),
        P(None, both, None), P(None, both, None), P(None, both), P(both, None), P(both),
        P(None, both), P(both), P(None, both), P(None, both),
    )
    out_specs = (
        P(both, None, None), P(both, None, None), P("bucket", "mem", None),
        P(None, both, None), P(None, both, None), P(None, both), P(both, None), P(both),
        P(None, both), P(both), P(None, both), P(None, both),
    )
    return jax.shard_map(
        functools.partial(shards, sizes), mesh=mesh, in_specs=in_specs, out_specs=out_specs, check_vma=False
    )
```

```python
import functools

import jax
import jax.numpy as jnp
from jax import lax
from jax.experimental import pallas as pl
from jax.experimental.pallas import tpu as pltpu
from jax.sharding import PartitionSpec as P

HD = 64
EPS = 1e-05
NEG = -1e30
F32 = jnp.float32
BF16 = jnp.bfloat16
MESH = pl.DeviceIdType.MESH
LANES = 128
ROWS = 16

SQ, SK, SV, SO, CK, CV, CQ, CO, EXPAND, REDUCE = 0, 1, 2, 3, 4, 5, 6, 7, 8, 12
BLOCKS = 16
GATHER_CHUNKS = (
    (0, 1, "zxyc"), (6, 8, "xyzc"), (2, 3, "zyxc"), (1, 2, "zxyc"), (8, 10, "xzyc"),
    (12, 14, "xyzc"), (14, 15, "zxyc"), (3, 4, "zxyc"), (4, 6, "zxyc"), (10, 12, "zxyc"),
    (15, 16, "zxyc"),
)
SCATTER_CHUNKS = (
    (15, 16, "cxyz"), (14, 15, "czyx"), (12, 14, "cyzx"), (10, 12, "cxyz"), (8, 10, "cyzx"),
    (7, 8, "czxy"), (6, 7, "cyzx"), (4, 6, "cyxz"), (3, 4, "cyzx"), (0, 1, "cyxz"),
    (1, 2, "cyxz"), (2, 3, "czyx"),
)
AXES = "zyxc"


def mm(left, right):
    return lax.dot_general(left, right, (((1,), (0,)), ((), ())), preferred_element_type=F32)


def mm_nt(left, right):
    return lax.dot_general(left, right, (((1,), (1,)), ((), ())), preferred_element_type=F32)


def mm_tn(left, right):
    return lax.dot_general(left, right, (((0,), (0,)), ((), ())), preferred_element_type=F32)


class Links:
    def __init__(self, send_sems, recv_sems):
        self.send_sems, self.recv_sems, self.used, self.sent = send_sems, recv_sems, 0, []

    def pair(self):
        self.used += 1
        return self.send_sems.at[self.used - 1], self.recv_sems.at[self.used - 1]

    def copy(self, source, target, landing, device):
        send, recv = self.pair()
        out = pltpu.make_async_remote_copy(
            src_ref=source, dst_ref=target, send_sem=send, recv_sem=recv,
            device_id=device, device_id_type=MESH,
        )
        out.start()
        self.sent.append(out)
        return pltpu.make_async_remote_copy(
            src_ref=source, dst_ref=landing, send_sem=send, recv_sem=recv,
            device_id=device, device_id_type=MESH,
        )

    def finish(self):
        for out in self.sent:
            out.wait_send()


class Place:
    def __init__(self, sizes):
        self.sizes = sizes
        bucket, mem = lax.axis_index("bucket"), lax.axis_index("mem")
        self.bucket, self.mem = bucket, mem
        self.at = {
            "z": bucket // sizes["y"], "y": bucket % sizes["y"],
            "x": mem // sizes["c"], "c": mem % sizes["c"],
        }

    def shifted(self, axis, step):
        size = self.sizes[axis]
        return lax.rem(self.at[axis] + (step % size), size)

    def device(self, axis, step):
        at = dict(self.at)
        at[axis] = self.shifted(axis, step)
        return (at["z"] * self.sizes["y"] + at["y"], at["x"] * self.sizes["c"] + at["c"])


def block_view(ref, lead, index):
    return ref.at[tuple(lead) + tuple(index[axis] for axis in AXES)]


class Gather:
    def __init__(self, links, place, grid, order, parts):
        self.links, self.place, self.parts = links, place, parts
        self.order = [axis for axis in order if grid[axis] > 1]
        self.grid, self.waits, self.done = grid, [], 0

    @property
    def over(self):
        return self.done > len(self.order)

    def step(self):
        if self.over:
            return
        for wait in self.waits:
            wait.wait_recv()
        self.waits = []
        if self.done < len(self.order):
            axis = self.order[self.done]
            known = self.order[: self.done]
            for hop in range(1, self.grid[axis]):
                mine, theirs = {}, {}
                for other in AXES:
                    if other in known:
                        mine[other] = theirs[other] = slice(None)
                    else:
                        at = self.place.at[other] if self.grid[other] > 1 else 0
                        mine[other] = theirs[other] = at
                theirs[axis] = self.place.shifted(axis, -hop)
                for ref, lead in self.parts:
                    self.waits.append(
                        self.links.copy(
                            block_view(ref, lead, mine), block_view(ref, lead, mine),
                            block_view(ref, lead, theirs), self.place.device(axis, hop),
                        )
                    )
        self.done += 1


class Scatter:
    def __init__(self, links, place, grid, order, parts, landings, emit):
        self.links, self.place, self.parts, self.landings = links, place, parts, landings
        self.order = [axis for axis in order if grid[axis] > 1]
        self.grid, self.waits, self.done, self.emit = grid, [], 0, emit

    def index(self, known):
        return {
            axis: (self.place.at[axis] if self.grid[axis] > 1 else 0) if axis in known or self.grid[axis] == 1
            else slice(None)
            for axis in AXES
        }

    @property
    def over(self):
        return self.done > len(self.order)

    def step(self):
        if self.over:
            return
        for wait in self.waits:
            wait.wait_recv()
        self.waits = []
        if self.done > 0:
            axis = self.order[self.done - 1]
            last = self.done == len(self.order)
            index = self.index(self.order[: self.done])
            for number, (ref, lead) in enumerate(self.parts):
                where = tuple(lead) + tuple(index[name] for name in AXES)
                landed = self.landings[number][self.done - 1]
                if self.grid[axis] == 2 and not last:
                    ref[where] = ref[where] + landed[0]
                    continue
                total = ref[where].astype(F32)
                for hop in range(1, self.grid[axis]):
                    total += landed[hop - 1].astype(F32)
                if last:
                    self.emit[number](total)
                else:
                    ref[where] = total.astype(ref.dtype)
        if self.done < len(self.order):
            axis = self.order[self.done]
            known = self.order[: self.done]
            for hop in range(1, self.grid[axis]):
                theirs = self.index(known)
                theirs[axis] = self.place.shifted(axis, hop)
                for number, (ref, lead) in enumerate(self.parts):
                    landing = self.landings[number][self.done].at[hop - 1]
                    self.waits.append(
                        self.links.copy(
                            block_view(ref, lead, theirs), landing, landing, self.place.device(axis, hop)
                        )
                    )
        self.done += 1


def landing_shapes(grid, order, lead_shape, tail_shape):
    shapes, left = [], {axis: grid[axis] for axis in AXES}
    for axis in order:
        if grid[axis] == 1:
            continue
        left[axis] = 1
        kept = tuple(left[name] for name in AXES if left[name] > 1)
        shapes.append(pltpu.VMEM((grid[axis] - 1,) + lead_shape + kept + tail_shape, BF16))
    return shapes


def layer_kernel(
    sizes, grid,
    scalars_hbm, small_hbm,
    x_hbm, dy_hbm, in_hbm, out_hbm, expand_hbm, reduce_hbm, memory_ref,
    grad_small_refs,
    y_ref, dx_ref, grad_in_ref, grad_out_ref, grad_expand_ref, grad_reduce_ref, gmem_ref,
    scratch,
):
    s = scratch
    place = Place(sizes)
    links = Links(s["send"], s["recv"])
    x_ref, dy_ref = s["x"], s["dy"]
    slots, span, width = x_ref.shape
    rows = slots * span
    members, chunk = s["mem"].shape[1], s["mem"].shape[2]
    reach_span = members * chunk
    heads = width // HD
    pairs = heads // 2
    ff_blocks = (BLOCKS - EXPAND) // 2
    places = width // ROWS
    locals_used = [0]

    def local_copy(source, target):
        locals_used[0] += 1
        copy = pltpu.make_async_copy(source, target, s["local"].at[locals_used[0] - 1])
        copy.start()
        return copy

    barrier = pltpu.get_barrier_semaphore()
    lengths_ref, reaches_ref, routes_ref, all_lengths_ref, all_routes_ref = s["scalars"]
    attention_bias_ref, gain_ref, shift_ref, reduce_bias_ref, expand_bias_ref = s["params"]
    peers = []
    for axis in "zy":
        peers += [place.device(axis, hop) for hop in range(1, sizes[axis])]
    others = [lax.rem(place.mem + hop, members) for hop in range(1, members)]
    peers += [(place.bucket, other) for other in others]
    for peer in peers:
        pl.semaphore_signal(barrier, inc=1, device_id=peer, device_id_type=MESH)

    here = tuple(place.at[axis] if grid[axis] > 1 else 0 for axis in AXES)

    def block_parts(in_ref, out_ref, expand_ref, reduce_ref):
        parts = [(SQ + k, in_ref.at[k]) for k in range(3)] + [(CQ, in_ref.at[3]), (CK, in_ref.at[4])]
        parts += [(CV, in_ref.at[5]), (SO, out_ref.at[0]), (CO, out_ref.at[1])]
        for k in range(ff_blocks):
            lanes = pl.ds(k * width, width)
            parts += [(EXPAND + k, expand_ref.at[:, lanes]), (REDUCE + k, reduce_ref.at[:, lanes])]
        return sorted(parts, key=lambda part: part[0])

    own_small = [local_copy(source, target) for source, target in zip(small_hbm, s["params"])]
    own_small += [local_copy(source, target) for source, target in zip(scalars_hbm, s["scalars"])]
    own = [
        local_copy(part, s["w"].at[(number,) + here])
        for number, part in block_parts(in_hbm, out_hbm, expand_hbm, reduce_hbm)
    ]
    own_rows = [local_copy(x_hbm, x_ref), local_copy(dy_hbm, dy_ref)]
    own_memory = local_copy(memory_ref.at[pl.ds(place.mem * slots, slots)], s["mem"].at[:, place.mem])

    spot = here[0]
    for axis, at in zip(AXES[1:], here[1:]):
        spot = spot * grid[axis] + at
    share = expand_bias_ref.shape[1]
    group, pieces = LANES // ROWS, LANES // share
    for copy in own_small:
        copy.wait()
    packet = s["packet"]
    packet[...] = jnp.zeros_like(packet)
    packet[0:6, 0:ROWS] = attention_bias_ref[...].astype(F32)
    packet[6:9, 0:ROWS] = gain_ref[...].astype(F32)
    packet[9:12, 0:ROWS] = shift_ref[...].astype(F32)
    packet[12:13, 0:ROWS] = reduce_bias_ref[...].astype(F32)
    packet[13:14, 0:share] = expand_bias_ref[...].astype(F32)
    narrow = pltpu.roll(packet[...], lax.rem(spot, group) * ROWS, 1)
    wide = pltpu.roll(packet[...], lax.rem(spot, pieces) * share, 1)
    row = lax.broadcasted_iota(jnp.int32, (ROWS, LANES), 0)
    lane = lax.broadcasted_iota(jnp.int32, (ROWS, LANES), 1)
    live = jnp.zeros((ROWS, LANES), jnp.int32)
    for slot in range(all_lengths_ref.shape[0]):
        count = jnp.where(all_routes_ref[slot] >= 0, all_lengths_ref[slot], 0)
        live = jnp.where(lane == slot, count, live)
    value = jnp.where(row == 13, wide, jnp.where(row == 14, live.astype(F32), narrow))
    s["small"][here] = value.astype(BF16)
    for copy in own:
        copy.wait()
    pl.semaphore_wait(barrier, len(peers))

    gathers = []
    for low, high, order in GATHER_CHUNKS:
        parts = [(s["w"], (slice(low, high),))]
        if low == 0:
            parts.append((s["small"], ()))
        gathers.append(Gather(links, place, grid, order, parts))
    memory_waits = [[] for _ in range(slots)]
    half = chunk // 2

    def send_memory(slot, part):
        at = pl.ds(part * half, half)
        for hop, other in zip(range(1, members), others):
            sender = lax.rem(place.mem + members - hop, members)
            memory_waits[slot].append(
                links.copy(
                    memory_ref.at[other * slots + slot, at], s["mem"].at[slot, place.mem, at],
                    s["mem"].at[slot, sender, at], (place.bucket, other),
                )
            )

    def weight(number):
        return s["w"][number].reshape(width, width)

    def put_grad(number, value):
        ref = s["gw"]
        ref[number] = value.astype(BF16).reshape(ref.shape[1:])

    even_lanes = lax.broadcasted_iota(jnp.int32, (1, LANES), 1) < HD
    even = jnp.where(even_lanes, 1.0, 0.0)
    odd = 1.0 - even
    scale = HD ** (-0.5)

    def stack(value, factor=1.0):
        return jnp.concatenate([value * (even * factor).astype(BF16), value * (odd * factor).astype(BF16)], axis=0)

    def unstack(value, factor=1.0):
        return value[:span] * (even * factor) + value[span:] * (odd * factor)

    def normed(value):
        centered = value - jnp.mean(value, axis=-1, keepdims=True)
        rstd = lax.rsqrt(jnp.mean(centered * centered, axis=-1, keepdims=True) + EPS)
        return centered * rstd, rstd

    def norm_back(grad, unit, rstd, number):
        s["rows_grad"][6 + number : 7 + number, :] = jnp.sum(grad * unit, axis=0, keepdims=True)
        s["rows_grad"][9 + number : 10 + number, :] = jnp.sum(grad, axis=0, keepdims=True)
        scaled = grad * s["rows"][6 + number : 7 + number, :]
        return (
            scaled - jnp.mean(scaled, axis=-1, keepdims=True)
            - unit * jnp.mean(scaled * unit, axis=-1, keepdims=True)
        ) * rstd

    def column_sum(value):
        return jnp.sum(value.astype(F32), axis=0, keepdims=True)

    def bias(number):
        return s["rows"][number : number + 1, :]

    def unpack_small():
        every = s["small"][...].reshape(places, ROWS, LANES).astype(F32)
        columns = [jnp.sum(every[g * group : (g + 1) * group], axis=0) for g in range(places // group)]
        s["rows"][...] = jnp.concatenate(columns, axis=1)
        columns = [
            jnp.sum(every[g * pieces : (g + 1) * pieces, 13], axis=0, keepdims=True) for g in range(places // pieces)
        ]
        s["ebias"][...] = jnp.concatenate(columns, axis=1)
        tokens = jnp.sum(jnp.sum(every[:, 14], axis=0, keepdims=True), axis=1, keepdims=True)
        s["tokens"][...] = jnp.broadcast_to(tokens, s["tokens"].shape)

    def self_project():
        x = x_ref[...].reshape(rows, width)
        s["q"][...] = (mm(x, weight(SQ)) + bias(0)).astype(BF16)
        s["k"][...] = mm(x, weight(SK)).astype(BF16)
        s["v"][...] = (mm(x, weight(SV)) + bias(1)).astype(BF16)

    def attend(low_ref, share_ref, mixed_ref, queries, keys_in, values_in, keep, at, lanes):
        scores = jnp.where(keep, mm_nt(stack(queries, scale), keys_in), NEG)
        weights = jnp.exp(scores - jnp.max(scores, axis=-1, keepdims=True))
        part = 1.0 / jnp.sum(weights, axis=-1, keepdims=True)
        low = weights.astype(BF16)
        low_ref[...] = low
        share_ref[...] = part
        mixed_ref[at, lanes] = unstack(mm(low, values_in) * part)

    def attend_back(low_ref, share_ref, mixed, da, queries, keys_in, values_in):
        low, part = low_ref[...], share_ref[...]
        da = stack(da).astype(F32) * part
        delta = jnp.sum(da * jnp.concatenate([mixed, mixed], axis=0), axis=-1, keepdims=True)
        da = da.astype(BF16)
        ds = (low.astype(F32) * (mm_nt(da, values_in) - delta)).astype(BF16)
        return (
            unstack(mm(ds, keys_in), scale).astype(BF16),
            mm_tn(ds, stack(queries, scale)).astype(BF16),
            mm_tn(low, da).astype(BF16),
        )

    def self_attend():
        row = lax.broadcasted_iota(jnp.int32, (2 * span, span), 0) % span
        col = lax.broadcasted_iota(jnp.int32, (2 * span, span), 1)
        for slot in range(slots):
            keep = (col <= row) & (col < lengths_ref[slot])
            at = slice(slot * span, (slot + 1) * span)
            for pair in range(pairs):
                lanes = slice(pair * LANES, (pair + 1) * LANES)
                attend(
                    s["ps"].at[slot, pair], s["share"].at[slot, pair], s["af"],
                    s["q"][at, lanes], s["k"][at, lanes], s["v"][at, lanes], keep, at, lanes,
                )
        s["a"][...] = s["af"][...].astype(BF16)

    def self_close():
        x = x_ref[...].reshape(rows, width).astype(F32)
        unit, rstd = normed(x + mm(s["a"][...], weight(SO)) + bias(2))
        s["n1"][...], s["d1"][...] = unit, rstd
        h1 = unit * bias(6) + bias(9)
        s["h1"][...] = h1
        s["h1b"][...] = h1.astype(BF16)

    def cross_query():
        s["q2"][...] = (mm(s["h1b"][...], weight(CQ)) + bias(3)).astype(BF16)

    def cross_memory(slot):
        items = s["mem"][slot].reshape(reach_span, width)
        s["k2"][slot] = mm(items, weight(CK)).astype(BF16).reshape(members, chunk, width)
        s["v2"][slot] = (mm(items, weight(CV)) + bias(4)).astype(BF16).reshape(members, chunk, width)

    def keys(name, slot, lanes):
        return s[name][slot, :, :, lanes].reshape(reach_span, LANES)

    def cross_attend(slot):
        col = lax.broadcasted_iota(jnp.int32, (1, reach_span), 1)
        keep = col < reaches_ref[slot]
        at = slice(slot * span, (slot + 1) * span)

        def body(pair, carry):
            lanes = pl.ds(pl.multiple_of(pair * LANES, LANES), LANES)
            attend(
                s["pc"].at[slot, pair], s["share2"].at[slot, pair], s["a2f"],
                s["q2"][at, lanes], keys("k2", slot, lanes), keys("v2", slot, lanes), keep, at, lanes,
            )
            return carry
        lax.fori_loop(0, pairs, body, 0)

    def cross_close():
        s["a2"][...] = s["a2f"][...].astype(BF16)
        unit, rstd = normed(s["h1"][...] + mm(s["a2"][...], weight(CO)) + bias(5))
        s["n2"][...], s["d2"][...] = unit, rstd
        h2 = unit * bias(7) + bias(10)
        s["h2b"][...] = h2.astype(BF16)
        s["r3"][...] = h2 + bias(12)

    def ff_up(block):
        lanes = slice(block * width, (block + 1) * width)
        u = mm(s["h2b"][...], weight(EXPAND + block)) + s["ebias"][:, lanes]
        sig = 1.0 / (1.0 + jnp.exp(-u))
        s["f"][block] = (u * sig).astype(BF16)
        s["slope"][block] = sig * (1.0 + u * (1.0 - sig))

    def ff_down(block):
        s["r3"][...] += mm_nt(s["f"][block], weight(REDUCE + block))

    def live_rows(each):
        row = lax.broadcasted_iota(jnp.int32, (rows, 1), 0)
        count = jnp.zeros((rows, 1), jnp.int32)
        for slot in range(slots):
            here_count = jnp.where(routes_ref[slot] >= 0, each(slot), 0)
            count = jnp.where((row >= slot * span) & (row < (slot + 1) * span), here_count + slot * span, count)
        return row < count

    def close():
        unit, rstd = normed(s["r3"][...])
        y = unit * bias(8) + bias(11)
        y = jnp.where(live_rows(lambda slot: span), y, 0.0)
        y_ref[...] = y.astype(BF16).reshape(x_ref.shape)
        dy = dy_ref[...].reshape(rows, width).astype(F32)
        dy = jnp.where(live_rows(lambda slot: lengths_ref[slot]), dy, 0.0)
        dr3 = norm_back(dy, unit, rstd, 2)
        s["dr"][...] = dr3
        s["e"][...] = dr3.astype(BF16)
        s["rows_grad"][12:13, :] = column_sum(s["e"][...])

    def reduce_grad(block):
        put_grad(REDUCE + block, mm_tn(s["e"][...], s["f"][block]))

    def ff_back(block):
        lanes = slice(block * width, (block + 1) * width)
        du = (mm(s["e"][...], weight(REDUCE + block)) * s["slope"][block]).astype(BF16)
        s["ebias_grad"][:, lanes] = column_sum(du)
        put_grad(EXPAND + block, mm_tn(s["h2b"][...], du))
        s["dr"][...] += mm_nt(du, weight(EXPAND + block))

    def cross_open():
        dr2 = norm_back(s["dr"][...], s["n2"][...], s["d2"][...], 1)
        s["dr"][...] = dr2
        e2 = dr2.astype(BF16)
        s["rows_grad"][5:6, :] = column_sum(e2)
        put_grad(CO, mm_tn(s["a2"][...], e2))
        s["da"][...] = mm_nt(e2, weight(CO)).astype(BF16)

    def cross_back(slot):
        at = slice(slot * span, (slot + 1) * span)

        def body(pair, carry):
            lanes = pl.ds(pl.multiple_of(pair * LANES, LANES), LANES)
            shape = (members, chunk, LANES)
            dq, dk, dv = attend_back(
                s["pc"].at[slot, pair], s["share2"].at[slot, pair], s["a2f"][at, lanes], s["da"][at, lanes],
                s["q2"][at, lanes], keys("k2", slot, lanes), keys("v2", slot, lanes),
            )
            s["dq"][at, lanes] = dq
            s["dk2"][slot, :, :, lanes] = dk.reshape(shape)
            s["dv2"][slot, :, :, lanes] = dv.reshape(shape)
            return carry
        lax.fori_loop(0, pairs, body, 0)

    def memory_grad(slot):
        value = mm_nt(s["dk2"][slot].reshape(reach_span, width), weight(CK))
        value += mm_nt(s["dv2"][slot].reshape(reach_span, width), weight(CV))
        s["gmem"][slot] = value.astype(BF16).reshape(members, chunk, width)

    def send_memory_grad(slot):
        mine = gmem_ref.at[place.mem * slots + slot]
        local_waits.append(local_copy(s["gmem"].at[slot, place.mem], mine))
        for hop, other in zip(range(1, members), others):
            sender = lax.rem(place.mem + members - hop, members)
            grad_waits.append(
                links.copy(
                    s["gmem"].at[slot, other], mine, gmem_ref.at[sender * slots + slot], (place.bucket, other)
                )
            )

    local_waits, grad_waits = [], []

    def cross_query_grad():
        dq = s["dq"][...]
        s["rows_grad"][3:4, :] = column_sum(dq)
        put_grad(CQ, mm_tn(s["h1b"][...], dq))

    def memory_weight_grad():
        items = s["mem"][...].reshape(slots * reach_span, width)
        put_grad(CK, mm_tn(items, s["dk2"][...].reshape(slots * reach_span, width)))
        dv = s["dv2"][...].reshape(slots * reach_span, width)
        put_grad(CV, mm_tn(items, dv))
        s["rows_grad"][4:5, :] = column_sum(dv)

    def self_open():
        dh1 = s["dr"][...] + mm_nt(s["dq"][...], weight(CQ))
        dr1 = norm_back(dh1, s["n1"][...], s["d1"][...], 0)
        s["dr"][...] = dr1
        e1 = dr1.astype(BF16)
        s["rows_grad"][2:3, :] = column_sum(e1)
        put_grad(SO, mm_tn(s["a"][...], e1))
        s["da"][...] = mm_nt(e1, weight(SO)).astype(BF16)

    def self_back():
        for slot in range(slots):
            at = slice(slot * span, (slot + 1) * span)
            for pair in range(pairs):
                lanes = slice(pair * LANES, (pair + 1) * LANES)
                s["dq"][at, lanes], s["dk"][at, lanes], s["dv"][at, lanes] = attend_back(
                    s["ps"].at[slot, pair], s["share"].at[slot, pair], s["af"][at, lanes], s["da"][at, lanes],
                    s["q"][at, lanes], s["k"][at, lanes], s["v"][at, lanes],
                )

    def self_grads():
        x = x_ref[...].reshape(rows, width)
        put_grad(SV, mm_tn(x, s["dv"][...]))
        put_grad(SQ, mm_tn(x, s["dq"][...]))
        put_grad(SK, mm_tn(x, s["dk"][...]))
        s["rows_grad"][0:1, :] = column_sum(s["dq"][...])
        s["rows_grad"][1:2, :] = column_sum(s["dv"][...])

    def input_grad():
        total = s["dr"][...] + mm_nt(s["dq"][...], weight(SQ))
        total += mm_nt(s["dk"][...], weight(SK)) + mm_nt(s["dv"][...], weight(SV))
        dx_ref[...] = total.astype(BF16).reshape(x_ref.shape)

    def turned(value, lanes):
        return value if lanes == 0 else pltpu.roll(value, LANES - lanes, 1)

    def pack_small():
        row = lax.broadcasted_iota(jnp.int32, (ROWS, LANES), 0)
        for number in range(places):
            at = number // group * LANES
            base = turned(s["rows_grad"][:, at : at + LANES], number % group * ROWS)
            at = number // pieces * LANES
            extra = turned(s["ebias_grad"][:, at : at + LANES], number % pieces * share)
            index, rest = [], number
            for axis in reversed(AXES):
                index.insert(0, rest % grid[axis])
                rest //= grid[axis]
            s["gsmall"][tuple(index)] = jnp.where(row == 13, extra, base).astype(BF16)

    targets = dict(block_parts(grad_in_ref, grad_out_ref, grad_expand_ref, grad_reduce_ref))

    def emit_weight(low, high):
        def emit(total):
            for number in range(low, high):
                targets[number][...] = total[number - low] / s["tokens"][0:1, 0:1]
        return emit

    def emit_small(total):
        value = total / s["tokens"][0:1, 0:1]
        first = 0
        for target in grad_small_refs:
            target[...] = value[first : first + target.shape[0], 0 : target.shape[1]]
            first += target.shape[0]

    scatters = []
    for number, (low, high, order) in enumerate(SCATTER_CHUNKS):
        parts, landings, emit = [(s["gw"], (slice(low, high),))], [s["land"][number]], [emit_weight(low, high)]
        if number == len(SCATTER_CHUNKS) - 1:
            parts.append((s["gsmall"], ()))
            landings.append(s["land_small"])
            emit.append(emit_small)
        scatters.append(Scatter(links, place, grid, order, parts, landings, emit))

    def gather(*numbers):
        for number in numbers:
            gathers[number].step()

    def need(*numbers):
        for number in numbers:
            while not gathers[number].over:
                gathers[number].step()

    def scatter(*numbers):
        for number in numbers:
            scatters[number].step()

    def arrived(copies):
        for copy in copies:
            copy.wait()

    def arrived_memory(slot):
        for wait in memory_waits[slot]:
            wait.wait_recv()

    s["rows_grad"][...] = jnp.zeros_like(s["rows_grad"])
    gather(0, 1, 2, 3, 4, 5, 6, 7, 8, 9, 10)
    send_memory(0, 0)
    gather(1, 4, 5, 0, 2, 1, 3, 5, 6, 7, 2, 0, 3, 8, 6, 7, 9, 0, 10, 2, 0)
    need(0)
    unpack_small()
    gather(3, 2, 8)
    send_memory(0, 1)
    gather(3)
    need(2, 3)
    arrived(own_rows)
    self_project()
    gather(6, 4)
    self_attend()
    gather(9, 6, 7, 10)
    send_memory(1, 0)
    gather(7)
    need(7)
    self_close()
    gather(8)
    send_memory(1, 1)
    gather(8, 1, 4, 1)
    need(1)
    cross_query()
    need(8)
    arrived([own_memory])
    arrived_memory(0)
    cross_memory(0)
    cross_attend(0)
    gather(4)
    arrived_memory(1)
    cross_memory(1)
    gather(9)
    cross_attend(1)
    gather(5, 10, 9)
    cross_close()
    need(4)
    ff_up(0)
    ff_up(1)
    need(9)
    ff_up(2)
    ff_up(3)
    gather(5)
    need(5)
    ff_down(0)
    gather(10)
    ff_down(1)
    need(6)
    ff_down(2)
    need(10)
    ff_down(3)
    close()
    reduce_grad(3)
    scatter(0)
    reduce_grad(2)
    scatter(1)
    reduce_grad(1)
    reduce_grad(0)
    scatter(2)
    ff_back(3)
    ff_back(2)
    scatter(0, 1, 3)
    ff_back(1)
    scatter(2)
    ff_back(0)
    scatter(4)
    cross_open()
    scatter(3, 5)
    cross_back(0)
    scatter(5, 0, 4)
    memory_grad(0)
    send_memory_grad(0)
    scatter(2, 1)
    cross_back(1)
    scatter(3, 0)
    memory_grad(1)
    send_memory_grad(1)
    cross_query_grad()
    scatter(6)
    memory_weight_grad()
    scatter(7, 6, 4, 1, 5)
    self_open()
    scatter(8, 3, 7)
    self_back()
    scatter(8, 2, 0, 6)
    self_grads()
    pack_small()
    scatter(9, 10, 11)
    input_grad()
    scatter(9, 10, 4, 11, 7, 3, 8, 6, 1, 5, 9, 2, 4, 10, 5, 7, 6, 11, 9, 10, 8, 11, 8, 7, 11, 9, 10)
    for work in scatters:
        while not work.over:
            work.step()
    for wait in grad_waits:
        wait.wait_recv()
    for wait in local_waits:
        wait.wait()
    links.finish()


def copy_count(grid, members, slots):
    count = 0
    for low, _, order in GATHER_CHUNKS:
        count += sum(grid[axis] - 1 for axis in order) * (2 if low == 0 else 1)
    for index, (_, _, order) in enumerate(SCATTER_CHUNKS):
        count += sum(grid[axis] - 1 for axis in order) * (2 if index == len(SCATTER_CHUNKS) - 1 else 1)
    return count + (members - 1) * (2 * slots + slots)


def run_layer(sizes, grid, scalars, small, large):
    x, memory = large[0], large[-1]
    slots, span, width = x.shape
    rows = slots * span
    members = sizes["x"] * sizes["c"]
    chunk = memory.shape[1]
    pairs = width // HD // 2
    ff_blocks = (BLOCKS - EXPAND) // 2
    place = tuple(grid[axis] for axis in AXES)
    mem_shape = (slots, members, chunk, width)
    count = copy_count(grid, members, slots)
    scratch = {
        "w": pltpu.VMEM((BLOCKS,) + place + (ROWS, width), BF16),
        "small": pltpu.VMEM(place + (ROWS, LANES), BF16),
        "packet": pltpu.VMEM((ROWS, LANES), F32),
        "gw": pltpu.VMEM((BLOCKS,) + place + (ROWS, width), BF16),
        "gsmall": pltpu.VMEM(place + (ROWS, LANES), BF16),
        "land": [
            landing_shapes(grid, order, (high - low,), (ROWS, width)) for low, high, order in SCATTER_CHUNKS
        ],
        "land_small": landing_shapes(grid, SCATTER_CHUNKS[-1][2], (), (ROWS, LANES)),
        "pc": pltpu.VMEM((slots, pairs, 2 * span, members * chunk), BF16),
        "ps": pltpu.VMEM((slots, pairs, 2 * span, span), BF16),
        "share": pltpu.VMEM((slots, pairs, 2 * span, 1), F32),
        "share2": pltpu.VMEM((slots, pairs, 2 * span, 1), F32),
        "f": pltpu.VMEM((ff_blocks, rows, width), BF16),
        "slope": pltpu.VMEM((ff_blocks, rows, width), F32),
        "rows": pltpu.VMEM((ROWS, width), F32),
        "rows_grad": pltpu.VMEM((ROWS, width), F32),
        "ebias": pltpu.VMEM((1, width * ff_blocks), F32),
        "ebias_grad": pltpu.VMEM((1, width * ff_blocks), F32),
        "tokens": pltpu.VMEM((8, LANES), F32),
        "d1": pltpu.VMEM((rows, 1), F32),
        "d2": pltpu.VMEM((rows, 1), F32),
        "send": pltpu.SemaphoreType.DMA((count,)),
        "recv": pltpu.SemaphoreType.DMA((count,)),
        "local": pltpu.SemaphoreType.DMA((BLOCKS + 3 + slots + len(small) + len(scalars),)),
        "scalars": [pltpu.SMEM(part.shape, part.dtype) for part in scalars],
        "params": [pltpu.VMEM(part.shape, BF16) for part in small],
    }
    for name in ("mem", "k2", "v2", "dk2", "dv2", "gmem"):
        scratch[name] = pltpu.VMEM(mem_shape, BF16)
    for name in ("q", "k", "v", "a", "h1b", "q2", "a2", "h2b", "e", "da", "dq", "dk", "dv"):
        scratch[name] = pltpu.VMEM((rows, width), BF16)
    for name in ("n1", "n2", "h1", "r3", "dr", "af", "a2f"):
        scratch[name] = pltpu.VMEM((rows, width), F32)
    for name in ("x", "dy"):
        scratch[name] = pltpu.VMEM(x.shape, BF16)
    leaves, tree = jax.tree.flatten(scratch)

    counts = (len(scalars), len(small), len(large), len(small), len(large))

    def kernel(*refs):
        groups, at = [], 0
        for size in counts:
            groups.append(refs[at : at + size])
            at += size
        layer_kernel(
            sizes, grid, groups[0], groups[1], *groups[2], groups[3], *groups[4],
            jax.tree.unflatten(tree, refs[at:]),
        )

    anywhere, vmem = pl.BlockSpec(memory_space=pl.ANY), pl.BlockSpec(memory_space=pltpu.VMEM)
    outs = [(part.shape, F32) for part in small]
    outs += [(x.shape, BF16), (x.shape, BF16)] + [(part.shape, F32) for part in large[2:6]] + [(memory.shape, BF16)]
    return pl.pallas_call(
        kernel,
        out_shape=tuple(pltpu.VMEM(shape, dtype) for shape, dtype in outs),
        in_specs=[anywhere] * sum(counts[:3]),
        out_specs=[vmem] * sum(counts[3:]),
        scratch_shapes=leaves,
        compiler_params=pltpu.CompilerParams(
            collective_id=0, has_side_effects=True, vmem_limit_bytes=58 << 20
        ),
    )(*scalars, *small, *large)


def copy_kernel(*refs):
    count, sems = len(refs) // 2, refs[-1]
    copies = [pltpu.make_async_copy(refs[n], refs[count + n], sems.at[n]) for n in range(count)]
    for copy in copies:
        copy.start()
    for copy in copies:
        copy.wait()


def handed_out(results):
    anywhere, vmem = pl.BlockSpec(memory_space=pl.ANY), pl.BlockSpec(memory_space=pltpu.VMEM)
    return pl.pallas_call(
        copy_kernel,
        out_shape=tuple(pltpu.HBM(part.shape, part.dtype) for part in results),
        in_specs=[vmem] * len(results),
        out_specs=[anywhere] * len(results),
        scratch_shapes=[pltpu.SemaphoreType.DMA((len(results),))],
        compiler_params=pltpu.CompilerParams(vmem_limit_bytes=32 << 20),
    )(*(pltpu.with_memory_space_constraint(part, pltpu.VMEM) for part in results))


def shards(
    sizes,
    decoder_in, memory, grad_out, decoder_lengths, memory_lengths, item_route,
    in_projection, out_projection, attention_bias, expand_weight, expand_bias,
    reduce_weight, reduce_bias, norm_gain, norm_bias,
):
    joined = in_projection.shape[1] < ROWS
    small = [attention_bias, norm_gain, norm_bias, reduce_bias[None], expand_bias[None]]
    weights = [in_projection, out_projection, expand_weight, reduce_weight.T]
    along = (1, 1, 0, 0)
    lengths, routes = decoder_lengths, item_route
    grid = dict(sizes)
    if joined:
        grid.update(x=1, c=1)
        small = [lax.all_gather(part, "mem", axis=1, tiled=True) for part in small]
        weights = [lax.all_gather(part, "mem", axis=axis, tiled=True) for part, axis in zip(weights, along)]
        lengths = lax.all_gather(lengths, "mem", tiled=True)
        routes = lax.all_gather(routes, "mem", tiled=True)
    results = run_layer(
        sizes, grid, (decoder_lengths, memory_lengths, item_route, lengths, routes), small,
        [decoder_in, grad_out] + weights + [memory],
    )
    if joined:
        results = list(results)
        for number in range(5):
            results[number] = lax.psum_scatter(results[number], "mem", scatter_dimension=1, tiled=True)
        for number, axis in zip(range(7, 11), along):
            results[number] = lax.psum_scatter(results[number], "mem", scatter_dimension=axis, tiled=True)
    else:
        results = handed_out(results)
    bias, gain, shift, reduce_shift, expand_shift, out, dx, g_in, g_out, g_expand, g_reduce, g_memory = results
    return (
        out, dx, g_memory, g_in, g_out, bias, g_expand, expand_shift[0], g_reduce.T, reduce_shift[0], gain, shift,
    )


def solution(mesh):
    both = ("bucket", "mem")
    buckets, members = mesh.shape["bucket"], mesh.shape["mem"]
    cores = 2
    across = members // cores
    sizes = {"z": buckets // across, "y": across, "x": across, "c": cores}
    in_specs = (
        P(both, None, None), P("bucket", "mem", None), P(both, None, None), P(both), P(both), P(both),
        P(None, both, None), P(None, both, None), P(None, both), P(both, None), P(both),
        P(None, both), P(both), P(None, both), P(None, both),
    )
    out_specs = (
        P(both, None, None), P(both, None, None), P("bucket", "mem", None),
        P(None, both, None), P(None, both, None), P(None, both), P(both, None), P(both),
        P(None, both), P(both), P(None, both), P(None, both),
    )
    return jax.shard_map(
        functools.partial(shards, sizes), mesh=mesh, in_specs=in_specs, out_specs=out_specs, check_vma=False
    )
```

```python
import functools

import jax
import jax.numpy as jnp
from jax import lax
from jax.experimental import pallas as pl
from jax.experimental.pallas import tpu as pltpu
from jax.sharding import PartitionSpec as P

HD = 64
EPS = 1e-05
NEG = -1e30
F32 = jnp.float32
BF16 = jnp.bfloat16
MESH = pl.DeviceIdType.MESH
LANES = 128
ROWS = 16

SQ, SK, SV, SO, CK, CV, CQ, CO, EXPAND, REDUCE = 0, 1, 2, 3, 4, 5, 6, 7, 8, 12
BLOCKS = 16
GATHER_CHUNKS = (
    (2, 3, "xzyc"), (0, 1, "zxyc"), (1, 2, "zxyc"), (6, 8, "zyxc"), (3, 4, "zxyc"),
    (4, 6, "xzyc"), (10, 12, "xzyc"), (12, 13, "xzyc"), (15, 16, "yxzc"), (8, 10, "zyxc"),
    (14, 15, "zxyc"), (13, 14, "xyzc"),
)
SCATTER_CHUNKS = (
    (15, 16, "cyzx"), (14, 15, "czyx"), (13, 14, "cyzx"), (12, 13, "cxzy"), (10, 12, "cxyz"),
    (8, 10, "cyzx"), (7, 8, "cyzx"), (6, 7, "cyzx"), (5, 6, "cyxz"), (4, 5, "cyxz"),
    (3, 4, "cyxz"), (0, 1, "cyxz"), (1, 2, "czyx"), (2, 3, "cyzx"),
)
AXES = "zyxc"


def mm(left, right):
    return lax.dot_general(left, right, (((1,), (0,)), ((), ())), preferred_element_type=F32)


def mm_nt(left, right):
    return lax.dot_general(left, right, (((1,), (1,)), ((), ())), preferred_element_type=F32)


def mm_tn(left, right):
    return lax.dot_general(left, right, (((0,), (0,)), ((), ())), preferred_element_type=F32)


class Links:
    def __init__(self, send_sems, recv_sems):
        self.send_sems, self.recv_sems, self.used, self.sent = send_sems, recv_sems, 0, []

    def pair(self):
        self.used += 1
        return self.send_sems.at[self.used - 1], self.recv_sems.at[self.used - 1]

    def copy(self, source, target, landing, device):
        send, recv = self.pair()
        out = pltpu.make_async_remote_copy(
            src_ref=source, dst_ref=target, send_sem=send, recv_sem=recv,
            device_id=device, device_id_type=MESH,
        )
        out.start()
        self.sent.append(out)
        return pltpu.make_async_remote_copy(
            src_ref=source, dst_ref=landing, send_sem=send, recv_sem=recv,
            device_id=device, device_id_type=MESH,
        )

    def finish(self):
        for out in self.sent:
            out.wait_send()


class Place:
    def __init__(self, sizes):
        self.sizes = sizes
        bucket, mem = lax.axis_index("bucket"), lax.axis_index("mem")
        self.bucket, self.mem = bucket, mem
        self.at = {
            "z": bucket // sizes["y"], "y": bucket % sizes["y"],
            "x": mem // sizes["c"], "c": mem % sizes["c"],
        }

    def shifted(self, axis, step):
        size = self.sizes[axis]
        return lax.rem(self.at[axis] + (step % size), size)

    def device(self, axis, step):
        at = dict(self.at)
        at[axis] = self.shifted(axis, step)
        return (at["z"] * self.sizes["y"] + at["y"], at["x"] * self.sizes["c"] + at["c"])


def block_view(ref, lead, index):
    return ref.at[tuple(lead) + tuple(index[axis] for axis in AXES)]


class Gather:
    def __init__(self, links, place, grid, order, parts):
        self.links, self.place, self.parts = links, place, parts
        self.order = [axis for axis in order if grid[axis] > 1]
        self.grid, self.waits, self.done = grid, [], 0

    @property
    def over(self):
        return self.done > len(self.order)

    def step(self):
        if self.over:
            return
        for wait in self.waits:
            wait.wait_recv()
        self.waits = []
        if self.done < len(self.order):
            axis = self.order[self.done]
            known = self.order[: self.done]
            for hop in range(1, self.grid[axis]):
                mine, theirs = {}, {}
                for other in AXES:
                    if other in known:
                        mine[other] = theirs[other] = slice(None)
                    else:
                        at = self.place.at[other] if self.grid[other] > 1 else 0
                        mine[other] = theirs[other] = at
                theirs[axis] = self.place.shifted(axis, -hop)
                for ref, lead in self.parts:
                    self.waits.append(
                        self.links.copy(
                            block_view(ref, lead, mine), block_view(ref, lead, mine),
                            block_view(ref, lead, theirs), self.place.device(axis, hop),
                        )
                    )
        self.done += 1


class Scatter:
    def __init__(self, links, place, grid, order, parts, landings, emit):
        self.links, self.place, self.parts, self.landings = links, place, parts, landings
        self.order = [axis for axis in order if grid[axis] > 1]
        self.grid, self.waits, self.done, self.emit = grid, [], 0, emit

    def index(self, known):
        return {
            axis: (self.place.at[axis] if self.grid[axis] > 1 else 0) if axis in known or self.grid[axis] == 1
            else slice(None)
            for axis in AXES
        }

    @property
    def over(self):
        return self.done > len(self.order)

    def step(self):
        if self.over:
            return
        for wait in self.waits:
            wait.wait_recv()
        self.waits = []
        if self.done > 0:
            axis = self.order[self.done - 1]
            last = self.done == len(self.order)
            index = self.index(self.order[: self.done])
            for number, (ref, lead) in enumerate(self.parts):
                where = tuple(lead) + tuple(index[name] for name in AXES)
                landed = self.landings[number][self.done - 1]
                if self.grid[axis] == 2 and not last:
                    ref[where] = ref[where] + landed[0]
                    continue
                total = ref[where].astype(F32)
                for hop in range(1, self.grid[axis]):
                    total += landed[hop - 1].astype(F32)
                if last:
                    self.emit[number](total)
                else:
                    ref[where] = total.astype(ref.dtype)
        if self.done < len(self.order):
            axis = self.order[self.done]
            known = self.order[: self.done]
            for hop in range(1, self.grid[axis]):
                theirs = self.index(known)
                theirs[axis] = self.place.shifted(axis, hop)
                for number, (ref, lead) in enumerate(self.parts):
                    landing = self.landings[number][self.done].at[hop - 1]
                    self.waits.append(
                        self.links.copy(
                            block_view(ref, lead, theirs), landing, landing, self.place.device(axis, hop)
                        )
                    )
        self.done += 1


def landing_shapes(grid, order, lead_shape, tail_shape):
    shapes, left = [], {axis: grid[axis] for axis in AXES}
    for axis in order:
        if grid[axis] == 1:
            continue
        left[axis] = 1
        kept = tuple(left[name] for name in AXES if left[name] > 1)
        shapes.append(pltpu.VMEM((grid[axis] - 1,) + lead_shape + kept + tail_shape, BF16))
    return shapes


def layer_kernel(
    sizes, grid,
    scalars_hbm, small_hbm,
    x_hbm, dy_hbm, in_hbm, out_hbm, expand_hbm, reduce_hbm, memory_ref,
    grad_small_refs,
    y_ref, dx_ref, grad_in_ref, grad_out_ref, grad_expand_ref, grad_reduce_ref, gmem_ref,
    scratch,
):
    s = scratch
    place = Place(sizes)
    links = Links(s["send"], s["recv"])
    x_ref, dy_ref = s["x"], s["dy"]
    slots, span, width = x_ref.shape
    rows = slots * span
    members, chunk = s["mem"].shape[1], s["mem"].shape[2]
    reach_span = members * chunk
    heads = width // HD
    pairs = heads // 2
    ff_blocks = (BLOCKS - EXPAND) // 2
    places = width // ROWS
    locals_used = [0]

    def local_copy(source, target):
        locals_used[0] += 1
        copy = pltpu.make_async_copy(source, target, s["local"].at[locals_used[0] - 1])
        copy.start()
        return copy

    barrier = pltpu.get_barrier_semaphore()
    lengths_ref, reaches_ref, routes_ref, all_lengths_ref, all_routes_ref = s["scalars"]
    attention_bias_ref, gain_ref, shift_ref, reduce_bias_ref, expand_bias_ref = s["params"]
    peers = []
    for axis in "zy":
        peers += [place.device(axis, hop) for hop in range(1, sizes[axis])]
    others = [lax.rem(place.mem + hop, members) for hop in range(1, members)]
    peers += [(place.bucket, other) for other in others]
    for peer in peers:
        pl.semaphore_signal(barrier, inc=1, device_id=peer, device_id_type=MESH)

    here = tuple(place.at[axis] if grid[axis] > 1 else 0 for axis in AXES)

    def block_parts(in_ref, out_ref, expand_ref, reduce_ref):
        parts = [(SQ + k, in_ref.at[k]) for k in range(3)] + [(CQ, in_ref.at[3]), (CK, in_ref.at[4])]
        parts += [(CV, in_ref.at[5]), (SO, out_ref.at[0]), (CO, out_ref.at[1])]
        for k in range(ff_blocks):
            lanes = pl.ds(k * width, width)
            parts += [(EXPAND + k, expand_ref.at[:, lanes]), (REDUCE + k, reduce_ref.at[:, lanes])]
        return sorted(parts, key=lambda part: part[0])

    own_small = [local_copy(source, target) for source, target in zip(small_hbm, s["params"])]
    own_small += [local_copy(source, target) for source, target in zip(scalars_hbm, s["scalars"])]
    own = [
        local_copy(part, s["w"].at[(number,) + here])
        for number, part in block_parts(in_hbm, out_hbm, expand_hbm, reduce_hbm)
    ]
    own_rows = [local_copy(x_hbm, x_ref), local_copy(dy_hbm, dy_ref)]
    own_memory = local_copy(memory_ref.at[pl.ds(place.mem * slots, slots)], s["mem"].at[:, place.mem])

    spot = here[0]
    for axis, at in zip(AXES[1:], here[1:]):
        spot = spot * grid[axis] + at
    share = expand_bias_ref.shape[1]
    group, pieces = LANES // ROWS, LANES // share
    for copy in own_small:
        copy.wait()
    packet = s["packet"]
    packet[...] = jnp.zeros_like(packet)
    packet[0:6, 0:ROWS] = attention_bias_ref[...].astype(F32)
    packet[6:9, 0:ROWS] = gain_ref[...].astype(F32)
    packet[9:12, 0:ROWS] = shift_ref[...].astype(F32)
    packet[12:13, 0:ROWS] = reduce_bias_ref[...].astype(F32)
    packet[13:14, 0:share] = expand_bias_ref[...].astype(F32)
    narrow = pltpu.roll(packet[...], lax.rem(spot, group) * ROWS, 1)
    wide = pltpu.roll(packet[...], lax.rem(spot, pieces) * share, 1)
    row = lax.broadcasted_iota(jnp.int32, (ROWS, LANES), 0)
    lane = lax.broadcasted_iota(jnp.int32, (ROWS, LANES), 1)
    live = jnp.zeros((ROWS, LANES), jnp.int32)
    for slot in range(all_lengths_ref.shape[0]):
        count = jnp.where(all_routes_ref[slot] >= 0, all_lengths_ref[slot], 0)
        live = jnp.where(lane == slot, count, live)
    value = jnp.where(row == 13, wide, jnp.where(row == 14, live.astype(F32), narrow))
    s["small"][here] = value.astype(BF16)
    for copy in own:
        copy.wait()
    pl.semaphore_wait(barrier, len(peers))

    gathers = []
    for low, high, order in GATHER_CHUNKS:
        parts = [(s["w"], (slice(low, high),))]
        if low == 0:
            parts.append((s["small"], ()))
        gathers.append(Gather(links, place, grid, order, parts))
    memory_waits = [[] for _ in range(slots)]
    half = chunk // 2

    def send_memory(slot, part):
        at = pl.ds(part * half, half)
        for hop, other in zip(range(1, members), others):
            sender = lax.rem(place.mem + members - hop, members)
            memory_waits[slot].append(
                links.copy(
                    memory_ref.at[other * slots + slot, at], s["mem"].at[slot, place.mem, at],
                    s["mem"].at[slot, sender, at], (place.bucket, other),
                )
            )

    def weight(number):
        return s["w"][number].reshape(width, width)

    def put_grad(number, value):
        ref = s["gw"]
        ref[number] = value.astype(BF16).reshape(ref.shape[1:])

    even_lanes = lax.broadcasted_iota(jnp.int32, (1, LANES), 1) < HD
    even = jnp.where(even_lanes, 1.0, 0.0)
    odd = 1.0 - even
    scale = HD ** (-0.5)

    def stack(value, factor=1.0):
        return jnp.concatenate([value * (even * factor).astype(BF16), value * (odd * factor).astype(BF16)], axis=0)

    def unstack(value, factor=1.0):
        return value[:span] * (even * factor) + value[span:] * (odd * factor)

    def normed(value):
        centered = value - jnp.mean(value, axis=-1, keepdims=True)
        rstd = lax.rsqrt(jnp.mean(centered * centered, axis=-1, keepdims=True) + EPS)
        return centered * rstd, rstd

    def norm_back(grad, unit, rstd, number):
        s["rows_grad"][6 + number : 7 + number, :] = jnp.sum(grad * unit, axis=0, keepdims=True)
        s["rows_grad"][9 + number : 10 + number, :] = jnp.sum(grad, axis=0, keepdims=True)
        scaled = grad * s["rows"][6 + number : 7 + number, :]
        return (
            scaled - jnp.mean(scaled, axis=-1, keepdims=True)
            - unit * jnp.mean(scaled * unit, axis=-1, keepdims=True)
        ) * rstd

    def column_sum(value):
        return jnp.sum(value.astype(F32), axis=0, keepdims=True)

    def bias(number):
        return s["rows"][number : number + 1, :]

    def unpack_small():
        every = s["small"][...].reshape(places, ROWS, LANES).astype(F32)
        columns = [jnp.sum(every[g * group : (g + 1) * group], axis=0) for g in range(places // group)]
        s["rows"][...] = jnp.concatenate(columns, axis=1)
        columns = [
            jnp.sum(every[g * pieces : (g + 1) * pieces, 13], axis=0, keepdims=True) for g in range(places // pieces)
        ]
        s["ebias"][...] = jnp.concatenate(columns, axis=1)
        tokens = jnp.sum(jnp.sum(every[:, 14], axis=0, keepdims=True), axis=1, keepdims=True)
        s["tokens"][...] = jnp.broadcast_to(tokens, s["tokens"].shape)

    def self_project():
        x = x_ref[...].reshape(rows, width)
        s["q"][...] = (mm(x, weight(SQ)) + bias(0)).astype(BF16)
        s["k"][...] = mm(x, weight(SK)).astype(BF16)
        s["v"][...] = (mm(x, weight(SV)) + bias(1)).astype(BF16)

    def attend(low_ref, share_ref, mixed_ref, queries, keys_in, values_in, keep, at, lanes):
        scores = jnp.where(keep, mm_nt(stack(queries, scale), keys_in), NEG)
        weights = jnp.exp(scores - jnp.max(scores, axis=-1, keepdims=True))
        part = 1.0 / jnp.sum(weights, axis=-1, keepdims=True)
        low = weights.astype(BF16)
        low_ref[...] = low
        share_ref[...] = part
        mixed_ref[at, lanes] = unstack(mm(low, values_in) * part)

    def attend_back(low_ref, share_ref, mixed, da, queries, keys_in, values_in):
        low, part = low_ref[...], share_ref[...]
        da = stack(da).astype(F32) * part
        delta = jnp.sum(da * jnp.concatenate([mixed, mixed], axis=0), axis=-1, keepdims=True)
        da = da.astype(BF16)
        ds = (low.astype(F32) * (mm_nt(da, values_in) - delta)).astype(BF16)
        return (
            unstack(mm(ds, keys_in), scale).astype(BF16),
            mm_tn(ds, stack(queries, scale)).astype(BF16),
            mm_tn(low, da).astype(BF16),
        )

    def self_attend():
        row = lax.broadcasted_iota(jnp.int32, (2 * span, span), 0) % span
        col = lax.broadcasted_iota(jnp.int32, (2 * span, span), 1)
        for slot in range(slots):
            keep = (col <= row) & (col < lengths_ref[slot])
            at = slice(slot * span, (slot + 1) * span)
            for pair in range(pairs):
                lanes = slice(pair * LANES, (pair + 1) * LANES)
                attend(
                    s["ps"].at[slot, pair], s["share"].at[slot, pair], s["af"],
                    s["q"][at, lanes], s["k"][at, lanes], s["v"][at, lanes], keep, at, lanes,
                )
        s["a"][...] = s["af"][...].astype(BF16)

    def self_close():
        x = x_ref[...].reshape(rows, width).astype(F32)
        unit, rstd = normed(x + mm(s["a"][...], weight(SO)) + bias(2))
        s["n1"][...], s["d1"][...] = unit, rstd
        h1 = unit * bias(6) + bias(9)
        s["h1"][...] = h1
        s["h1b"][...] = h1.astype(BF16)

    def cross_query():
        s["q2"][...] = (mm(s["h1b"][...], weight(CQ)) + bias(3)).astype(BF16)

    def cross_memory(slot):
        items = s["mem"][slot].reshape(reach_span, width)
        s["k2"][slot] = mm(items, weight(CK)).astype(BF16).reshape(members, chunk, width)
        s["v2"][slot] = (mm(items, weight(CV)) + bias(4)).astype(BF16).reshape(members, chunk, width)

    def keys(name, slot, lanes):
        return s[name][slot, :, :, lanes].reshape(reach_span, LANES)

    def cross_attend(slot):
        col = lax.broadcasted_iota(jnp.int32, (1, reach_span), 1)
        keep = col < reaches_ref[slot]
        at = slice(slot * span, (slot + 1) * span)

        def body(pair, carry):
            lanes = pl.ds(pl.multiple_of(pair * LANES, LANES), LANES)
            attend(
                s["pc"].at[slot, pair], s["share2"].at[slot, pair], s["a2f"],
                s["q2"][at, lanes], keys("k2", slot, lanes), keys("v2", slot, lanes), keep, at, lanes,
            )
            return carry
        lax.fori_loop(0, pairs, body, 0, unroll=4)

    def cross_close():
        s["a2"][...] = s["a2f"][...].astype(BF16)
        unit, rstd = normed(s["h1"][...] + mm(s["a2"][...], weight(CO)) + bias(5))
        s["n2"][...], s["d2"][...] = unit, rstd
        h2 = unit * bias(7) + bias(10)
        s["h2b"][...] = h2.astype(BF16)
        s["r3"][...] = h2 + bias(12)

    def ff_up(block):
        lanes = slice(block * width, (block + 1) * width)
        u = mm(s["h2b"][...], weight(EXPAND + block)) + s["ebias"][:, lanes]
        sig = 1.0 / (1.0 + jnp.exp(-u))
        s["f"][block] = (u * sig).astype(BF16)
        s["slope"][block] = sig * (1.0 + u * (1.0 - sig))

    def ff_down(block):
        s["r3"][...] += mm_nt(s["f"][block], weight(REDUCE + block))

    def live_rows(each):
        row = lax.broadcasted_iota(jnp.int32, (rows, 1), 0)
        count = jnp.zeros((rows, 1), jnp.int32)
        for slot in range(slots):
            here_count = jnp.where(routes_ref[slot] >= 0, each(slot), 0)
            count = jnp.where((row >= slot * span) & (row < (slot + 1) * span), here_count + slot * span, count)
        return row < count

    def close():
        unit, rstd = normed(s["r3"][...])
        y = unit * bias(8) + bias(11)
        y = jnp.where(live_rows(lambda slot: span), y, 0.0)
        y_ref[...] = y.astype(BF16).reshape(x_ref.shape)
        dy = dy_ref[...].reshape(rows, width).astype(F32)
        dy = jnp.where(live_rows(lambda slot: lengths_ref[slot]), dy, 0.0)
        dr3 = norm_back(dy, unit, rstd, 2)
        s["dr"][...] = dr3
        s["e"][...] = dr3.astype(BF16)
        s["rows_grad"][12:13, :] = column_sum(s["e"][...])

    def reduce_grad(block):
        put_grad(REDUCE + block, mm_tn(s["e"][...], s["f"][block]))

    def ff_back(block):
        lanes = slice(block * width, (block + 1) * width)
        du = (mm(s["e"][...], weight(REDUCE + block)) * s["slope"][block]).astype(BF16)
        s["ebias_grad"][:, lanes] = column_sum(du)
        put_grad(EXPAND + block, mm_tn(s["h2b"][...], du))
        s["dr"][...] += mm_nt(du, weight(EXPAND + block))

    def cross_open():
        dr2 = norm_back(s["dr"][...], s["n2"][...], s["d2"][...], 1)
        s["dr"][...] = dr2
        e2 = dr2.astype(BF16)
        s["rows_grad"][5:6, :] = column_sum(e2)
        put_grad(CO, mm_tn(s["a2"][...], e2))
        s["da"][...] = mm_nt(e2, weight(CO)).astype(BF16)

    def cross_back(slot):
        at = slice(slot * span, (slot + 1) * span)

        def body(pair, carry):
            lanes = pl.ds(pl.multiple_of(pair * LANES, LANES), LANES)
            shape = (members, chunk, LANES)
            dq, dk, dv = attend_back(
                s["pc"].at[slot, pair], s["share2"].at[slot, pair], s["a2f"][at, lanes], s["da"][at, lanes],
                s["q2"][at, lanes], keys("k2", slot, lanes), keys("v2", slot, lanes),
            )
            s["dq"][at, lanes] = dq
            s["dk2"][slot, :, :, lanes] = dk.reshape(shape)
            s["dv2"][slot, :, :, lanes] = dv.reshape(shape)
            return carry
        lax.fori_loop(0, pairs, body, 0, unroll=4)

    def memory_grad(slot):
        value = mm_nt(s["dk2"][slot].reshape(reach_span, width), weight(CK))
        value += mm_nt(s["dv2"][slot].reshape(reach_span, width), weight(CV))
        s["gmem"][slot] = value.astype(BF16).reshape(members, chunk, width)

    def send_memory_grad(slot):
        mine = gmem_ref.at[place.mem * slots + slot]
        local_waits.append(local_copy(s["gmem"].at[slot, place.mem], mine))
        for hop, other in zip(range(1, members), others):
            sender = lax.rem(place.mem + members - hop, members)
            grad_waits.append(
                links.copy(
                    s["gmem"].at[slot, other], mine, gmem_ref.at[sender * slots + slot], (place.bucket, other)
                )
            )

    local_waits, grad_waits = [], []

    def cross_query_grad():
        dq = s["dq"][...]
        s["rows_grad"][3:4, :] = column_sum(dq)
        put_grad(CQ, mm_tn(s["h1b"][...], dq))

    def memory_weight_grad():
        items = s["mem"][...].reshape(slots * reach_span, width)
        put_grad(CK, mm_tn(items, s["dk2"][...].reshape(slots * reach_span, width)))
        dv = s["dv2"][...].reshape(slots * reach_span, width)
        put_grad(CV, mm_tn(items, dv))
        s["rows_grad"][4:5, :] = column_sum(dv)

    def self_open():
        dh1 = s["dr"][...] + mm_nt(s["dq"][...], weight(CQ))
        dr1 = norm_back(dh1, s["n1"][...], s["d1"][...], 0)
        s["dr"][...] = dr1
        e1 = dr1.astype(BF16)
        s["rows_grad"][2:3, :] = column_sum(e1)
        put_grad(SO, mm_tn(s["a"][...], e1))
        s["da"][...] = mm_nt(e1, weight(SO)).astype(BF16)

    def self_back():
        for slot in range(slots):
            at = slice(slot * span, (slot + 1) * span)
            for pair in range(pairs):
                lanes = slice(pair * LANES, (pair + 1) * LANES)
                s["dq"][at, lanes], s["dk"][at, lanes], s["dv"][at, lanes] = attend_back(
                    s["ps"].at[slot, pair], s["share"].at[slot, pair], s["af"][at, lanes], s["da"][at, lanes],
                    s["q"][at, lanes], s["k"][at, lanes], s["v"][at, lanes],
                )

    def self_grads():
        x = x_ref[...].reshape(rows, width)
        put_grad(SV, mm_tn(x, s["dv"][...]))
        put_grad(SQ, mm_tn(x, s["dq"][...]))
        put_grad(SK, mm_tn(x, s["dk"][...]))
        s["rows_grad"][0:1, :] = column_sum(s["dq"][...])
        s["rows_grad"][1:2, :] = column_sum(s["dv"][...])

    def input_grad():
        total = s["dr"][...] + mm_nt(s["dq"][...], weight(SQ))
        total += mm_nt(s["dk"][...], weight(SK)) + mm_nt(s["dv"][...], weight(SV))
        dx_ref[...] = total.astype(BF16).reshape(x_ref.shape)

    def turned(value, lanes):
        return value if lanes == 0 else pltpu.roll(value, LANES - lanes, 1)

    def pack_small():
        row = lax.broadcasted_iota(jnp.int32, (ROWS, LANES), 0)
        for number in range(places):
            at = number // group * LANES
            base = turned(s["rows_grad"][:, at : at + LANES], number % group * ROWS)
            at = number // pieces * LANES
            extra = turned(s["ebias_grad"][:, at : at + LANES], number % pieces * share)
            index, rest = [], number
            for axis in reversed(AXES):
                index.insert(0, rest % grid[axis])
                rest //= grid[axis]
            s["gsmall"][tuple(index)] = jnp.where(row == 13, extra, base).astype(BF16)

    targets = dict(block_parts(grad_in_ref, grad_out_ref, grad_expand_ref, grad_reduce_ref))

    def emit_weight(low, high):
        def emit(total):
            for number in range(low, high):
                targets[number][...] = total[number - low] / s["tokens"][0:1, 0:1]
        return emit

    def emit_small(total):
        value = total / s["tokens"][0:1, 0:1]
        first = 0
        for target in grad_small_refs:
            target[...] = value[first : first + target.shape[0], 0 : target.shape[1]]
            first += target.shape[0]

    scatters = []
    for number, (low, high, order) in enumerate(SCATTER_CHUNKS):
        parts, landings, emit = [(s["gw"], (slice(low, high),))], [s["land"][number]], [emit_weight(low, high)]
        if number == len(SCATTER_CHUNKS) - 1:
            parts.append((s["gsmall"], ()))
            landings.append(s["land_small"])
            emit.append(emit_small)
        scatters.append(Scatter(links, place, grid, order, parts, landings, emit))

    def gather(*numbers):
        for number in numbers:
            gathers[number].step()

    def need(*numbers):
        for number in numbers:
            while not gathers[number].over:
                gathers[number].step()

    def scatter(*numbers):
        for number in numbers:
            scatters[number].step()

    def arrived(copies):
        for copy in copies:
            copy.wait()

    def arrived_memory(slot):
        for wait in memory_waits[slot]:
            wait.wait_recv()

    s["rows_grad"][...] = jnp.zeros_like(s["rows_grad"])
    gather(1, 0, 2, 11, 6, 3)
    send_memory(0, 0)
    gather(11, 1, 2, 4, 7, 0, 5, 8, 3)
    send_memory(0, 1)
    gather(1, 10, 5, 2, 4, 0, 10, 9, 8, 3, 7, 1, 6, 4)
    send_memory(1, 0)
    send_memory(1, 1)
    gather(5, 1)
    need(1)
    unpack_small()
    gather(2, 0, 0, 2, 8, 4, 9, 3, 10, 4)
    need(0, 2)
    arrived(own_rows)
    self_project()
    gather(5, 3)
    self_attend()
    gather(11)
    need(4)
    self_close()
    gather(7)
    need(3)
    cross_query()
    gather(9, 5)
    need(5)
    arrived([own_memory])
    arrived_memory(0)
    cross_memory(0)
    gather(6)
    cross_attend(0)
    gather(10)
    arrived_memory(1)
    cross_memory(1)
    gather(7, 8)
    cross_attend(1)
    gather(9, 10, 6, 7)
    cross_close()
    gather(11, 8, 9)
    need(9)
    ff_up(0)
    ff_up(1)
    gather(6)
    need(6)
    ff_up(2)
    ff_up(3)
    need(7)
    ff_down(0)
    gather(11)
    need(11)
    ff_down(1)
    need(10)
    ff_down(2)
    need(8)
    ff_down(3)
    close()
    reduce_grad(3)
    reduce_grad(2)
    reduce_grad(1)
    reduce_grad(0)
    scatter(3, 1, 2)
    ff_back(3)
    ff_back(2)
    scatter(4, 0, 3, 1)
    ff_back(1)
    scatter(2)
    ff_back(0)
    cross_open()
    scatter(5, 6, 0, 4)
    cross_back(0)
    scatter(6, 2)
    memory_grad(0)
    send_memory_grad(0)
    scatter(5, 3)
    cross_back(1)
    scatter(0, 4)
    memory_grad(1)
    send_memory_grad(1)
    cross_query_grad()
    scatter(7, 6, 1)
    memory_weight_grad()
    scatter(8, 7, 5)
    self_open()
    scatter(10, 8)
    self_back()
    self_grads()
    pack_small()
    scatter(12, 10, 7, 13, 9, 1, 2, 12, 6, 13, 11, 11, 9, 10, 0, 4, 8, 3, 11, 13, 1, 10, 8, 12, 6, 9)
    input_grad()
    scatter(11, 5, 12, 4, 9, 13, 0, 7, 10, 3, 8, 5, 7, 11, 2, 12, 13, 9)
    for work in scatters:
        while not work.over:
            work.step()
    for wait in grad_waits:
        wait.wait_recv()
    for wait in local_waits:
        wait.wait()
    links.finish()


def copy_count(grid, members, slots):
    count = 0
    for low, _, order in GATHER_CHUNKS:
        count += sum(grid[axis] - 1 for axis in order) * (2 if low == 0 else 1)
    for index, (_, _, order) in enumerate(SCATTER_CHUNKS):
        count += sum(grid[axis] - 1 for axis in order) * (2 if index == len(SCATTER_CHUNKS) - 1 else 1)
    return count + (members - 1) * (2 * slots + slots)


def run_layer(sizes, grid, scalars, small, large):
    x, memory = large[0], large[-1]
    slots, span, width = x.shape
    rows = slots * span
    members = sizes["x"] * sizes["c"]
    chunk = memory.shape[1]
    pairs = width // HD // 2
    ff_blocks = (BLOCKS - EXPAND) // 2
    place = tuple(grid[axis] for axis in AXES)
    mem_shape = (slots, members, chunk, width)
    count = copy_count(grid, members, slots)
    scratch = {
        "w": pltpu.VMEM((BLOCKS,) + place + (ROWS, width), BF16),
        "small": pltpu.VMEM(place + (ROWS, LANES), BF16),
        "packet": pltpu.VMEM((ROWS, LANES), F32),
        "gw": pltpu.VMEM((BLOCKS,) + place + (ROWS, width), BF16),
        "gsmall": pltpu.VMEM(place + (ROWS, LANES), BF16),
        "land": [
            landing_shapes(grid, order, (high - low,), (ROWS, width)) for low, high, order in SCATTER_CHUNKS
        ],
        "land_small": landing_shapes(grid, SCATTER_CHUNKS[-1][2], (), (ROWS, LANES)),
        "pc": pltpu.VMEM((slots, pairs, 2 * span, members * chunk), BF16),
        "ps": pltpu.VMEM((slots, pairs, 2 * span, span), BF16),
        "share": pltpu.VMEM((slots, pairs, 2 * span, 1), F32),
        "share2": pltpu.VMEM((slots, pairs, 2 * span, 1), F32),
        "f": pltpu.VMEM((ff_blocks, rows, width), BF16),
        "slope": pltpu.VMEM((ff_blocks, rows, width), F32),
        "rows": pltpu.VMEM((ROWS, width), F32),
        "rows_grad": pltpu.VMEM((ROWS, width), F32),
        "ebias": pltpu.VMEM((1, width * ff_blocks), F32),
        "ebias_grad": pltpu.VMEM((1, width * ff_blocks), F32),
        "tokens": pltpu.VMEM((8, LANES), F32),
        "d1": pltpu.VMEM((rows, 1), F32),
        "d2": pltpu.VMEM((rows, 1), F32),
        "send": pltpu.SemaphoreType.DMA((count,)),
        "recv": pltpu.SemaphoreType.DMA((count,)),
        "local": pltpu.SemaphoreType.DMA((BLOCKS + 3 + slots + len(small) + len(scalars),)),
        "scalars": [pltpu.SMEM(part.shape, part.dtype) for part in scalars],
        "params": [pltpu.VMEM(part.shape, BF16) for part in small],
    }
    for name in ("mem", "k2", "v2", "dk2", "dv2", "gmem"):
        scratch[name] = pltpu.VMEM(mem_shape, BF16)
    for name in ("q", "k", "v", "a", "h1b", "q2", "a2", "h2b", "e", "da", "dq", "dk", "dv"):
        scratch[name] = pltpu.VMEM((rows, width), BF16)
    for name in ("n1", "n2", "h1", "r3", "dr", "af", "a2f"):
        scratch[name] = pltpu.VMEM((rows, width), F32)
    for name in ("x", "dy"):
        scratch[name] = pltpu.VMEM(x.shape, BF16)
    leaves, tree = jax.tree.flatten(scratch)

    counts = (len(scalars), len(small), len(large), len(small), len(large))

    def kernel(*refs):
        groups, at = [], 0
        for size in counts:
            groups.append(refs[at : at + size])
            at += size
        layer_kernel(
            sizes, grid, groups[0], groups[1], *groups[2], groups[3], *groups[4],
            jax.tree.unflatten(tree, refs[at:]),
        )

    anywhere, vmem = pl.BlockSpec(memory_space=pl.ANY), pl.BlockSpec(memory_space=pltpu.VMEM)
    outs = [(part.shape, F32) for part in small]
    outs += [(x.shape, BF16), (x.shape, BF16)] + [(part.shape, F32) for part in large[2:6]] + [(memory.shape, BF16)]
    return pl.pallas_call(
        kernel,
        out_shape=tuple(pltpu.VMEM(shape, dtype) for shape, dtype in outs),
        in_specs=[anywhere] * sum(counts[:3]),
        out_specs=[vmem] * sum(counts[3:]),
        scratch_shapes=leaves,
        compiler_params=pltpu.CompilerParams(
            collective_id=0, has_side_effects=True, vmem_limit_bytes=58 << 20
        ),
    )(*scalars, *small, *large)


def copy_kernel(*refs):
    count, sems = len(refs) // 2, refs[-1]
    copies = [pltpu.make_async_copy(refs[n], refs[count + n], sems.at[n]) for n in range(count)]
    for copy in copies:
        copy.start()
    for copy in copies:
        copy.wait()


def handed_out(results):
    anywhere, vmem = pl.BlockSpec(memory_space=pl.ANY), pl.BlockSpec(memory_space=pltpu.VMEM)
    return pl.pallas_call(
        copy_kernel,
        out_shape=tuple(pltpu.HBM(part.shape, part.dtype) for part in results),
        in_specs=[vmem] * len(results),
        out_specs=[anywhere] * len(results),
        scratch_shapes=[pltpu.SemaphoreType.DMA((len(results),))],
        compiler_params=pltpu.CompilerParams(vmem_limit_bytes=32 << 20),
    )(*(pltpu.with_memory_space_constraint(part, pltpu.VMEM) for part in results))


def shards(
    sizes,
    decoder_in, memory, grad_out, decoder_lengths, memory_lengths, item_route,
    in_projection, out_projection, attention_bias, expand_weight, expand_bias,
    reduce_weight, reduce_bias, norm_gain, norm_bias,
):
    joined = in_projection.shape[1] < ROWS
    small = [attention_bias, norm_gain, norm_bias, reduce_bias[None], expand_bias[None]]
    weights = [in_projection, out_projection, expand_weight, reduce_weight.T]
    along = (1, 1, 0, 0)
    lengths, routes = decoder_lengths, item_route
    grid = dict(sizes)
    if joined:
        grid.update(x=1, c=1)
        small = [lax.all_gather(part, "mem", axis=1, tiled=True) for part in small]
        weights = [lax.all_gather(part, "mem", axis=axis, tiled=True) for part, axis in zip(weights, along)]
        lengths = lax.all_gather(lengths, "mem", tiled=True)
        routes = lax.all_gather(routes, "mem", tiled=True)
    results = run_layer(
        sizes, grid, (decoder_lengths, memory_lengths, item_route, lengths, routes), small,
        [decoder_in, grad_out] + weights + [memory],
    )
    if joined:
        results = list(results)
        for number in range(5):
            results[number] = lax.psum_scatter(results[number], "mem", scatter_dimension=1, tiled=True)
        for number, axis in zip(range(7, 11), along):
            results[number] = lax.psum_scatter(results[number], "mem", scatter_dimension=axis, tiled=True)
    else:
        results = handed_out(results)
    bias, gain, shift, reduce_shift, expand_shift, out, dx, g_in, g_out, g_expand, g_reduce, g_memory = results
    return (
        out, dx, g_memory, g_in, g_out, bias, g_expand, expand_shift[0], g_reduce.T, reduce_shift[0], gain, shift,
    )


def solution(mesh):
    both = ("bucket", "mem")
    buckets, members = mesh.shape["bucket"], mesh.shape["mem"]
    cores = 2
    across = members // cores
    sizes = {"z": buckets // across, "y": across, "x": across, "c": cores}
    in_specs = (
        P(both, None, None), P("bucket", "mem", None), P(both, None, None), P(both), P(both), P(both),
        P(None, both, None), P(None, both, None), P(None, both), P(both, None), P(both),
        P(None, both), P(both), P(None, both), P(None, both),
    )
    out_specs = (
        P(both, None, None), P(both, None, None), P("bucket", "mem", None),
        P(None, both, None), P(None, both, None), P(None, both), P(both, None), P(both),
        P(None, both), P(both), P(None, both), P(None, both),
    )
    return jax.shard_map(
        functools.partial(shards, sizes), mesh=mesh, in_specs=in_specs, out_specs=out_specs, check_vma=False
    )
```

```python
import functools

import jax
import jax.numpy as jnp
from jax import lax
from jax.experimental import pallas as pl
from jax.experimental.pallas import tpu as pltpu
from jax.sharding import PartitionSpec as P

HD = 64
EPS = 1e-05
NEG = -1e30
F32 = jnp.float32
BF16 = jnp.bfloat16
MESH = pl.DeviceIdType.MESH
LANES = 128
ROWS = 16

SQ, SK, SV, SO, CK, CV, CQ, CO, EXPAND, REDUCE = 0, 1, 2, 3, 4, 5, 6, 7, 8, 12
BLOCKS = 16
GATHER_CHUNKS = (
    (1, 2, "zxyc"), (3, 4, "xyzc"), (0, 1, "xzyc"), (2, 3, "zxyc"), (12, 14, "zyxc"),
    (4, 6, "xyzc"), (15, 16, "xzyc"), (6, 8, "zxyc"), (10, 12, "zxyc"), (14, 15, "xyzc"),
    (8, 10, "xyzc"),
)
SCATTER_CHUNKS = (
    (15, 16, "czyx"), (14, 15, "czyx"), (12, 14, "cxyz"), (10, 12, "czyx"), (8, 10, "cyzx"),
    (7, 8, "cyxz"), (6, 7, "cyzx"), (4, 6, "cyxz"), (3, 4, "czxy"), (0, 1, "cyxz"),
    (1, 2, "czyx"), (2, 3, "cyxz"),
)
AXES = "zyxc"


def mm(left, right):
    return lax.dot_general(left, right, (((1,), (0,)), ((), ())), preferred_element_type=F32)


def mm_nt(left, right):
    return lax.dot_general(left, right, (((1,), (1,)), ((), ())), preferred_element_type=F32)


def mm_tn(left, right):
    return lax.dot_general(left, right, (((0,), (0,)), ((), ())), preferred_element_type=F32)


def only_if(condition, action):
    if condition is None:
        action()
    else:
        pl.when(condition)(action)


class Landing:
    def __init__(self, copy, lands):
        self.copy, self.lands = copy, lands

    def wait_recv(self):
        only_if(self.lands, self.copy.wait_recv)


def steps_of(grid, order):
    steps = []
    for axis in order:
        if axis == "z" and grid["z"] == 4:
            steps += ["z", "Z"]
        elif grid[axis] > 1:
            steps.append(axis)
    return steps


class Links:
    def __init__(self, send_sems, recv_sems):
        self.send_sems, self.recv_sems, self.used, self.sent = send_sems, recv_sems, 0, []

    def pair(self):
        self.used += 1
        return self.send_sems.at[self.used - 1], self.recv_sems.at[self.used - 1]

    def copy(self, source, target, landing, device, sends=None, lands=None):
        send, recv = self.pair()
        out = pltpu.make_async_remote_copy(
            src_ref=source, dst_ref=target, send_sem=send, recv_sem=recv,
            device_id=device, device_id_type=MESH,
        )
        only_if(sends, out.start)
        self.sent.append((sends, out))
        return Landing(
            pltpu.make_async_remote_copy(
                src_ref=source, dst_ref=landing, send_sem=send, recv_sem=recv,
                device_id=device, device_id_type=MESH,
            ),
            lands,
        )

    def finish(self):
        for sends, out in self.sent:
            only_if(sends, out.wait_send)


class Place:
    def __init__(self, sizes):
        self.sizes = sizes
        bucket, mem = lax.axis_index("bucket"), lax.axis_index("mem")
        self.bucket, self.mem = bucket, mem
        self.at = {
            "z": bucket // sizes["y"], "y": bucket % sizes["y"],
            "x": mem // sizes["c"], "c": mem % sizes["c"],
        }

    def on_line(self):
        z = self.at["z"]
        side = z // 2
        middle = (z == 1) | (z == 2)
        return middle, jnp.logical_not(middle), z + 1 - 2 * (z % 2), 2 - side, 3 * (1 - side), 2 * (1 - side)

    def at_z(self, z):
        return (z * self.sizes["y"] + self.at["y"], self.mem)

    def shifted(self, axis, step):
        size = self.sizes[axis]
        return lax.rem(self.at[axis] + (step % size), size)

    def device(self, axis, step):
        at = dict(self.at)
        at[axis] = self.shifted(axis, step)
        return (at["z"] * self.sizes["y"] + at["y"], at["x"] * self.sizes["c"] + at["c"])


def block_view(ref, lead, index):
    return ref.at[tuple(lead) + tuple(index[axis] for axis in AXES)]


class Gather:
    def index(self, known):
        return {
            axis: slice(None) if axis in known else (self.place.at[axis] if self.grid[axis] > 1 else 0)
            for axis in AXES
        }

    def line_step(self, axis, known):
        middle, end, pair, far_middle, far_end, far_first = self.place.on_line()

        def send(source_z, landing_z, target_z, sends, lands):
            source, landing = self.index(known), self.index(known)
            source["z"], landing["z"] = source_z, landing_z
            for ref, lead in self.parts:
                here = block_view(ref, lead, source)
                self.waits.append(
                    self.links.copy(
                        here, here, block_view(ref, lead, landing), self.place.at_z(target_z), sends, lands
                    )
                )

        z = self.place.at["z"]
        if axis == "z":
            send(z, far_end, far_middle, end, middle)
            send(z, far_middle, far_middle, middle, middle)
            send(z, pair, pair, None, None)
        else:
            both = pl.ds(far_first, 2)
            send(both, both, pair, middle, end)

    def __init__(self, links, place, grid, order, parts):
        self.links, self.place, self.parts = links, place, parts
        self.order = steps_of(grid, order)
        self.grid, self.waits, self.done = grid, [], 0

    @property
    def over(self):
        return self.done > len(self.order)

    def step(self):
        if self.over:
            return
        for wait in self.waits:
            wait.wait_recv()
        self.waits = []
        if self.done < len(self.order):
            axis = self.order[self.done]
            known = self.order[: self.done]
            if axis in "zZ" and "Z" in self.order:
                self.line_step(axis, known)
                self.done += 1
                return
            for hop in range(1, self.grid[axis]):
                mine, theirs = self.index(known), self.index(known)
                theirs[axis] = self.place.shifted(axis, -hop)
                for ref, lead in self.parts:
                    self.waits.append(
                        self.links.copy(
                            block_view(ref, lead, mine), block_view(ref, lead, mine),
                            block_view(ref, lead, theirs), self.place.device(axis, hop),
                        )
                    )
        self.done += 1


class Scatter:
    def __init__(self, links, place, grid, order, parts, landings, emit):
        self.links, self.place, self.parts, self.landings = links, place, parts, landings
        self.order = steps_of(grid, order)
        self.grid, self.waits, self.done, self.emit = grid, [], 0, emit

    def index(self, known):
        return {
            axis: (self.place.at[axis] if self.grid[axis] > 1 else 0) if axis in known or self.grid[axis] == 1
            else slice(None)
            for axis in AXES
        }

    @property
    def over(self):
        return self.done > len(self.order)

    def step(self):
        if self.over:
            return
        for wait in self.waits:
            wait.wait_recv()
        self.waits = []
        if self.done > 0 and self.order[self.done - 1] == "z" and "Z" in self.order:
            self.line_add()
        elif self.done > 0:
            axis = self.order[self.done - 1]
            last = self.done == len(self.order)
            index = self.index(self.order[: self.done])
            for number, (ref, lead) in enumerate(self.parts):
                where = tuple(lead) + tuple(index[name] for name in AXES)
                landed = self.landings[number][self.done - 1]
                if landed.shape[0] == 1 and not last:
                    ref[where] = ref[where] + landed[0]
                    continue
                total = ref[where].astype(F32)
                for hop in range(landed.shape[0]):
                    total += landed[hop].astype(F32)
                if last:
                    self.emit[number](total)
                else:
                    ref[where] = total.astype(ref.dtype)
        if self.done < len(self.order):
            axis = self.order[self.done]
            known = self.order[: self.done]
            if axis in "zZ" and "Z" in self.order:
                self.line_step(axis, known)
                self.done += 1
                return
            for hop in range(1, self.grid[axis]):
                theirs = self.index(known)
                theirs[axis] = self.place.shifted(axis, hop)
                for number, (ref, lead) in enumerate(self.parts):
                    landing = self.landings[number][self.done].at[hop - 1]
                    self.waits.append(
                        self.links.copy(
                            block_view(ref, lead, theirs), landing, landing, self.place.device(axis, hop)
                        )
                    )
        self.done += 1


    def line_step(self, axis, known):
        middle, end, pair, far_middle, far_end, far_first = self.place.on_line()
        known = [name for name in known if name != "z"]

        def send(source_z, landing, target_z, sends, lands):
            source = self.index(known)
            source["z"] = source_z
            for number, (ref, lead) in enumerate(self.parts):
                held = landing(self.landings[number])
                self.waits.append(
                    self.links.copy(
                        block_view(ref, lead, source), held, held, self.place.at_z(target_z), sends, lands
                    )
                )

        first = self.order.index("z")
        if axis == "z":
            send(pl.ds(far_first, 2), lambda held: held[first], pair, end, middle)
            self.pair_waits = []
            waits, self.waits = self.waits, []
            send(pair, lambda held: held[first + 1].at[0], pair, None, None)
            self.pair_waits, self.waits = self.waits, waits
        else:
            send(far_middle, lambda held: held[first + 1].at[1], far_middle, middle, middle)
            send(far_end, lambda held: held[first + 1].at[1], far_end, middle, end)
            self.waits += self.pair_waits

    def line_add(self):
        middle, _, _, _, _, far_first = self.place.on_line()
        first = self.order.index("z")
        index = self.index(self.order[:first])
        index["z"] = pl.ds(far_first, 2)

        @pl.when(middle)
        def _():
            for number, (ref, lead) in enumerate(self.parts):
                where = tuple(lead) + tuple(index[name] for name in AXES)
                ref[where] = ref[where] + self.landings[number][first][...]


def landing_shapes(grid, order, lead_shape, tail_shape):
    shapes, left = [], {axis: grid[axis] for axis in AXES}
    steps = steps_of(grid, order)
    for axis in steps:
        left[axis.lower()] = 1
        kept = tuple(left[name] for name in AXES if left[name] > 1)
        if axis == "z" and "Z" in steps:
            shape = lead_shape + (2,) + kept + tail_shape
        else:
            shape = (2 if axis == "Z" else grid[axis] - 1,) + lead_shape + kept + tail_shape
        shapes.append(pltpu.VMEM(shape, BF16))
    return shapes


def layer_kernel(
    sizes, grid,
    scalars_hbm, small_hbm,
    x_hbm, dy_hbm, in_hbm, out_hbm, expand_hbm, reduce_hbm, memory_ref,
    grad_small_refs,
    y_ref, dx_ref, grad_in_ref, grad_out_ref, grad_expand_ref, grad_reduce_ref, gmem_ref,
    scratch,
):
    s = scratch
    place = Place(sizes)
    links = Links(s["send"], s["recv"])
    x_ref, dy_ref = s["x"], s["dy"]
    slots, span, width = x_ref.shape
    rows = slots * span
    members, chunk = s["mem"].shape[1], s["mem"].shape[2]
    reach_span = members * chunk
    heads = width // HD
    pairs = heads // 2
    ff_blocks = (BLOCKS - EXPAND) // 2
    places = width // ROWS
    locals_used = [0]

    def local_copy(source, target):
        locals_used[0] += 1
        copy = pltpu.make_async_copy(source, target, s["local"].at[locals_used[0] - 1])
        copy.start()
        return copy

    barrier = pltpu.get_barrier_semaphore()
    lengths_ref, reaches_ref, routes_ref, all_lengths_ref, all_routes_ref = s["scalars"]
    attention_bias_ref, gain_ref, shift_ref, reduce_bias_ref, expand_bias_ref = s["params"]
    peers = []
    for axis in "zy":
        peers += [place.device(axis, hop) for hop in range(1, sizes[axis])]
    others = [lax.rem(place.mem + hop, members) for hop in range(1, members)]
    peers += [(place.bucket, other) for other in others]
    for peer in peers:
        pl.semaphore_signal(barrier, inc=1, device_id=peer, device_id_type=MESH)

    here = tuple(place.at[axis] if grid[axis] > 1 else 0 for axis in AXES)

    def block_parts(in_ref, out_ref, expand_ref, reduce_ref):
        parts = [(SQ + k, in_ref.at[k]) for k in range(3)] + [(CQ, in_ref.at[3]), (CK, in_ref.at[4])]
        parts += [(CV, in_ref.at[5]), (SO, out_ref.at[0]), (CO, out_ref.at[1])]
        for k in range(ff_blocks):
            lanes = pl.ds(k * width, width)
            parts += [(EXPAND + k, expand_ref.at[:, lanes]), (REDUCE + k, reduce_ref.at[:, lanes])]
        return sorted(parts, key=lambda part: part[0])

    own_small = [local_copy(source, target) for source, target in zip(small_hbm, s["params"])]
    own_small += [local_copy(source, target) for source, target in zip(scalars_hbm, s["scalars"])]
    own = [
        local_copy(part, s["w"].at[(number,) + here])
        for number, part in block_parts(in_hbm, out_hbm, expand_hbm, reduce_hbm)
    ]
    own_rows = [local_copy(x_hbm, x_ref), local_copy(dy_hbm, dy_ref)]
    own_memory = local_copy(memory_ref.at[pl.ds(place.mem * slots, slots)], s["mem"].at[:, place.mem])

    spot = here[0]
    for axis, at in zip(AXES[1:], here[1:]):
        spot = spot * grid[axis] + at
    share = expand_bias_ref.shape[1]
    group, pieces = LANES // ROWS, LANES // share
    for copy in own_small:
        copy.wait()
    packet = s["packet"]
    packet[...] = jnp.zeros_like(packet)
    packet[0:6, 0:ROWS] = attention_bias_ref[...].astype(F32)
    packet[6:9, 0:ROWS] = gain_ref[...].astype(F32)
    packet[9:12, 0:ROWS] = shift_ref[...].astype(F32)
    packet[12:13, 0:ROWS] = reduce_bias_ref[...].astype(F32)
    packet[13:14, 0:share] = expand_bias_ref[...].astype(F32)
    narrow = pltpu.roll(packet[...], lax.rem(spot, group) * ROWS, 1)
    wide = pltpu.roll(packet[...], lax.rem(spot, pieces) * share, 1)
    row = lax.broadcasted_iota(jnp.int32, (ROWS, LANES), 0)
    lane = lax.broadcasted_iota(jnp.int32, (ROWS, LANES), 1)
    live = jnp.zeros((ROWS, LANES), jnp.int32)
    for slot in range(all_lengths_ref.shape[0]):
        count = jnp.where(all_routes_ref[slot] >= 0, all_lengths_ref[slot], 0)
        live = jnp.where(lane == slot, count, live)
    value = jnp.where(row == 13, wide, jnp.where(row == 14, live.astype(F32), narrow))
    s["small"][here] = value.astype(BF16)
    for copy in own:
        copy.wait()
    pl.semaphore_wait(barrier, len(peers))

    gathers = []
    for low, high, order in GATHER_CHUNKS:
        parts = [(s["w"], (slice(low, high),))]
        if low == 0:
            parts.append((s["small"], ()))
        gathers.append(Gather(links, place, grid, order, parts))
    memory_waits = [[] for _ in range(slots)]
    half = chunk // 2

    def send_memory(slot, part):
        at = pl.ds(part * half, half)
        for hop, other in zip(range(1, members), others):
            sender = lax.rem(place.mem + members - hop, members)
            memory_waits[slot].append(
                links.copy(
                    memory_ref.at[other * slots + slot, at], s["mem"].at[slot, place.mem, at],
                    s["mem"].at[slot, sender, at], (place.bucket, other),
                )
            )

    def weight(number):
        return s["w"][number].reshape(width, width)

    def put_grad(number, value):
        ref = s["gw"]
        ref[number] = value.astype(BF16).reshape(ref.shape[1:])

    even_lanes = lax.broadcasted_iota(jnp.int32, (1, LANES), 1) < HD
    even = jnp.where(even_lanes, 1.0, 0.0)
    odd = 1.0 - even
    scale = HD ** (-0.5)

    def stack(value, factor=1.0):
        return jnp.concatenate([value * (even * factor).astype(BF16), value * (odd * factor).astype(BF16)], axis=0)

    def unstack(value, factor=1.0):
        return value[:span] * (even * factor) + value[span:] * (odd * factor)

    def normed(value):
        centered = value - jnp.mean(value, axis=-1, keepdims=True)
        rstd = lax.rsqrt(jnp.mean(centered * centered, axis=-1, keepdims=True) + EPS)
        return centered * rstd, rstd

    def norm_back(grad, unit, rstd, number):
        s["rows_grad"][6 + number : 7 + number, :] = jnp.sum(grad * unit, axis=0, keepdims=True)
        s["rows_grad"][9 + number : 10 + number, :] = jnp.sum(grad, axis=0, keepdims=True)
        scaled = grad * s["rows"][6 + number : 7 + number, :]
        return (
            scaled - jnp.mean(scaled, axis=-1, keepdims=True)
            - unit * jnp.mean(scaled * unit, axis=-1, keepdims=True)
        ) * rstd

    def column_sum(value):
        return jnp.sum(value.astype(F32), axis=0, keepdims=True)

    def bias(number):
        return s["rows"][number : number + 1, :]

    def unpack_small():
        every = s["small"][...].reshape(places, ROWS, LANES).astype(F32)
        columns = [jnp.sum(every[g * group : (g + 1) * group], axis=0) for g in range(places // group)]
        s["rows"][...] = jnp.concatenate(columns, axis=1)
        columns = [
            jnp.sum(every[g * pieces : (g + 1) * pieces, 13], axis=0, keepdims=True) for g in range(places // pieces)
        ]
        s["ebias"][...] = jnp.concatenate(columns, axis=1)
        tokens = jnp.sum(jnp.sum(every[:, 14], axis=0, keepdims=True), axis=1, keepdims=True)
        s["tokens"][...] = jnp.broadcast_to(tokens, s["tokens"].shape)

    def self_project():
        x = x_ref[...].reshape(rows, width)
        s["q"][...] = (mm(x, weight(SQ)) + bias(0)).astype(BF16)
        s["k"][...] = mm(x, weight(SK)).astype(BF16)
        s["v"][...] = (mm(x, weight(SV)) + bias(1)).astype(BF16)

    def attend(low_ref, share_ref, mixed_ref, queries, keys_in, values_in, keep, at, lanes):
        scores = jnp.where(keep, mm_nt(stack(queries, scale), keys_in), NEG)
        weights = jnp.exp(scores - jnp.max(scores, axis=-1, keepdims=True))
        part = 1.0 / jnp.sum(weights, axis=-1, keepdims=True)
        low = weights.astype(BF16)
        low_ref[...] = low
        share_ref[...] = part
        mixed_ref[at, lanes] = unstack(mm(low, values_in) * part)

    def attend_back(low_ref, share_ref, mixed, da, queries, keys_in, values_in):
        low, part = low_ref[...], share_ref[...]
        da = stack(da).astype(F32) * part
        delta = jnp.sum(da * jnp.concatenate([mixed, mixed], axis=0), axis=-1, keepdims=True)
        da = da.astype(BF16)
        ds = (low.astype(F32) * (mm_nt(da, values_in) - delta)).astype(BF16)
        return (
            unstack(mm(ds, keys_in), scale).astype(BF16),
            mm_tn(ds, stack(queries, scale)).astype(BF16),
            mm_tn(low, da).astype(BF16),
        )

    def self_attend():
        row = lax.broadcasted_iota(jnp.int32, (2 * span, span), 0) % span
        col = lax.broadcasted_iota(jnp.int32, (2 * span, span), 1)
        for slot in range(slots):
            keep = (col <= row) & (col < lengths_ref[slot])
            at = slice(slot * span, (slot + 1) * span)
            for pair in range(pairs):
                lanes = slice(pair * LANES, (pair + 1) * LANES)
                attend(
                    s["ps"].at[slot, pair], s["share"].at[slot, pair], s["af"],
                    s["q"][at, lanes], s["k"][at, lanes], s["v"][at, lanes], keep, at, lanes,
                )
        s["a"][...] = s["af"][...].astype(BF16)

    def self_close():
        x = x_ref[...].reshape(rows, width).astype(F32)
        unit, rstd = normed(x + mm(s["a"][...], weight(SO)) + bias(2))
        s["n1"][...], s["d1"][...] = unit, rstd
        h1 = unit * bias(6) + bias(9)
        s["h1"][...] = h1
        s["h1b"][...] = h1.astype(BF16)

    def cross_query():
        s["q2"][...] = (mm(s["h1b"][...], weight(CQ)) + bias(3)).astype(BF16)

    def cross_memory(slot):
        items = s["mem"][slot].reshape(reach_span, width)
        s["k2"][slot] = mm(items, weight(CK)).astype(BF16).reshape(members, chunk, width)
        s["v2"][slot] = (mm(items, weight(CV)) + bias(4)).astype(BF16).reshape(members, chunk, width)

    def keys(name, slot, lanes):
        return s[name][slot, :, :, lanes].reshape(reach_span, LANES)

    def cross_attend(slot):
        col = lax.broadcasted_iota(jnp.int32, (1, reach_span), 1)
        keep = col < reaches_ref[slot]
        at = slice(slot * span, (slot + 1) * span)

        def body(pair, carry):
            lanes = pl.ds(pl.multiple_of(pair * LANES, LANES), LANES)
            attend(
                s["pc"].at[slot, pair], s["share2"].at[slot, pair], s["a2f"],
                s["q2"][at, lanes], keys("k2", slot, lanes), keys("v2", slot, lanes), keep, at, lanes,
            )
            return carry
        lax.fori_loop(0, pairs, body, 0, unroll=4)

    def cross_close():
        s["a2"][...] = s["a2f"][...].astype(BF16)
        unit, rstd = normed(s["h1"][...] + mm(s["a2"][...], weight(CO)) + bias(5))
        s["n2"][...], s["d2"][...] = unit, rstd
        h2 = unit * bias(7) + bias(10)
        s["h2b"][...] = h2.astype(BF16)
        s["r3"][...] = h2 + bias(12)

    def ff_up(block):
        lanes = slice(block * width, (block + 1) * width)
        u = mm(s["h2b"][...], weight(EXPAND + block)) + s["ebias"][:, lanes]
        sig = 1.0 / (1.0 + jnp.exp(-u))
        s["f"][block] = (u * sig).astype(BF16)
        s["slope"][block] = sig * (1.0 + u * (1.0 - sig))

    def ff_down(block):
        s["r3"][...] += mm_nt(s["f"][block], weight(REDUCE + block))

    def live_rows(each):
        row = lax.broadcasted_iota(jnp.int32, (rows, 1), 0)
        count = jnp.zeros((rows, 1), jnp.int32)
        for slot in range(slots):
            here_count = jnp.where(routes_ref[slot] >= 0, each(slot), 0)
            count = jnp.where((row >= slot * span) & (row < (slot + 1) * span), here_count + slot * span, count)
        return row < count

    def close():
        unit, rstd = normed(s["r3"][...])
        y = unit * bias(8) + bias(11)
        y = jnp.where(live_rows(lambda slot: span), y, 0.0)
        y_ref[...] = y.astype(BF16).reshape(x_ref.shape)
        dy = dy_ref[...].reshape(rows, width).astype(F32)
        dy = jnp.where(live_rows(lambda slot: lengths_ref[slot]), dy, 0.0)
        dr3 = norm_back(dy, unit, rstd, 2)
        s["dr"][...] = dr3
        s["e"][...] = dr3.astype(BF16)
        s["rows_grad"][12:13, :] = column_sum(s["e"][...])

    def reduce_grad(block):
        put_grad(REDUCE + block, mm_tn(s["e"][...], s["f"][block]))

    def ff_back(block):
        lanes = slice(block * width, (block + 1) * width)
        du = (mm(s["e"][...], weight(REDUCE + block)) * s["slope"][block]).astype(BF16)
        s["ebias_grad"][:, lanes] = column_sum(du)
        put_grad(EXPAND + block, mm_tn(s["h2b"][...], du))
        s["dr"][...] += mm_nt(du, weight(EXPAND + block))

    def cross_open():
        dr2 = norm_back(s["dr"][...], s["n2"][...], s["d2"][...], 1)
        s["dr"][...] = dr2
        e2 = dr2.astype(BF16)
        s["rows_grad"][5:6, :] = column_sum(e2)
        put_grad(CO, mm_tn(s["a2"][...], e2))
        s["da"][...] = mm_nt(e2, weight(CO)).astype(BF16)

    def cross_back(slot):
        at = slice(slot * span, (slot + 1) * span)

        def body(pair, carry):
            lanes = pl.ds(pl.multiple_of(pair * LANES, LANES), LANES)
            shape = (members, chunk, LANES)
            dq, dk, dv = attend_back(
                s["pc"].at[slot, pair], s["share2"].at[slot, pair], s["a2f"][at, lanes], s["da"][at, lanes],
                s["q2"][at, lanes], keys("k2", slot, lanes), keys("v2", slot, lanes),
            )
            s["dq"][at, lanes] = dq
            s["dk2"][slot, :, :, lanes] = dk.reshape(shape)
            s["dv2"][slot, :, :, lanes] = dv.reshape(shape)
            return carry
        lax.fori_loop(0, pairs, body, 0, unroll=4)

    def memory_grad(slot):
        value = mm_nt(s["dk2"][slot].reshape(reach_span, width), weight(CK))
        value += mm_nt(s["dv2"][slot].reshape(reach_span, width), weight(CV))
        s["gmem"][slot] = value.astype(BF16).reshape(members, chunk, width)

    def send_memory_grad(slot):
        mine = gmem_ref.at[place.mem * slots + slot]
        local_waits.append(local_copy(s["gmem"].at[slot, place.mem], mine))
        for hop, other in zip(range(1, members), others):
            sender = lax.rem(place.mem + members - hop, members)
            grad_waits.append(
                links.copy(
                    s["gmem"].at[slot, other], mine, gmem_ref.at[sender * slots + slot], (place.bucket, other)
                )
            )

    local_waits, grad_waits = [], []

    def cross_query_grad():
        dq = s["dq"][...]
        s["rows_grad"][3:4, :] = column_sum(dq)
        put_grad(CQ, mm_tn(s["h1b"][...], dq))

    def memory_weight_grad():
        items = s["mem"][...].reshape(slots * reach_span, width)
        put_grad(CK, mm_tn(items, s["dk2"][...].reshape(slots * reach_span, width)))
        dv = s["dv2"][...].reshape(slots * reach_span, width)
        put_grad(CV, mm_tn(items, dv))
        s["rows_grad"][4:5, :] = column_sum(dv)

    def self_open():
        dh1 = s["dr"][...] + mm_nt(s["dq"][...], weight(CQ))
        dr1 = norm_back(dh1, s["n1"][...], s["d1"][...], 0)
        s["dr"][...] = dr1
        e1 = dr1.astype(BF16)
        s["rows_grad"][2:3, :] = column_sum(e1)
        put_grad(SO, mm_tn(s["a"][...], e1))
        s["da"][...] = mm_nt(e1, weight(SO)).astype(BF16)

    def self_back():
        for slot in range(slots):
            at = slice(slot * span, (slot + 1) * span)
            for pair in range(pairs):
                lanes = slice(pair * LANES, (pair + 1) * LANES)
                s["dq"][at, lanes], s["dk"][at, lanes], s["dv"][at, lanes] = attend_back(
                    s["ps"].at[slot, pair], s["share"].at[slot, pair], s["af"][at, lanes], s["da"][at, lanes],
                    s["q"][at, lanes], s["k"][at, lanes], s["v"][at, lanes],
                )

    def self_grads():
        x = x_ref[...].reshape(rows, width)
        put_grad(SV, mm_tn(x, s["dv"][...]))
        put_grad(SQ, mm_tn(x, s["dq"][...]))
        put_grad(SK, mm_tn(x, s["dk"][...]))
        s["rows_grad"][0:1, :] = column_sum(s["dq"][...])
        s["rows_grad"][1:2, :] = column_sum(s["dv"][...])

    def input_grad():
        total = s["dr"][...] + mm_nt(s["dq"][...], weight(SQ))
        total += mm_nt(s["dk"][...], weight(SK)) + mm_nt(s["dv"][...], weight(SV))
        dx_ref[...] = total.astype(BF16).reshape(x_ref.shape)

    def turned(value, lanes):
        return value if lanes == 0 else pltpu.roll(value, LANES - lanes, 1)

    def pack_small():
        row = lax.broadcasted_iota(jnp.int32, (ROWS, LANES), 0)
        for number in range(places):
            at = number // group * LANES
            base = turned(s["rows_grad"][:, at : at + LANES], number % group * ROWS)
            at = number // pieces * LANES
            extra = turned(s["ebias_grad"][:, at : at + LANES], number % pieces * share)
            index, rest = [], number
            for axis in reversed(AXES):
                index.insert(0, rest % grid[axis])
                rest //= grid[axis]
            s["gsmall"][tuple(index)] = jnp.where(row == 13, extra, base).astype(BF16)

    targets = dict(block_parts(grad_in_ref, grad_out_ref, grad_expand_ref, grad_reduce_ref))

    def emit_weight(low, high):
        def emit(total):
            for number in range(low, high):
                targets[number][...] = total[number - low] / s["tokens"][0:1, 0:1]
        return emit

    def emit_small(total):
        value = total / s["tokens"][0:1, 0:1]
        first = 0
        for target in grad_small_refs:
            target[...] = value[first : first + target.shape[0], 0 : target.shape[1]]
            first += target.shape[0]

    scatters = []
    for number, (low, high, order) in enumerate(SCATTER_CHUNKS):
        parts, landings, emit = [(s["gw"], (slice(low, high),))], [s["land"][number]], [emit_weight(low, high)]
        if number == len(SCATTER_CHUNKS) - 1:
            parts.append((s["gsmall"], ()))
            landings.append(s["land_small"])
            emit.append(emit_small)
        scatters.append(Scatter(links, place, grid, order, parts, landings, emit))

    def gather(*numbers):
        for number in numbers:
            gathers[number].step()

    def need(*numbers):
        for number in numbers:
            while not gathers[number].over:
                gathers[number].step()

    def scatter(*numbers):
        for number in numbers:
            scatters[number].step()

    def arrived(copies):
        for copy in copies:
            copy.wait()

    def arrived_memory(slot):
        for wait in memory_waits[slot]:
            wait.wait_recv()

    s["rows_grad"][...] = jnp.zeros_like(s["rows_grad"])
    gather(2, 3, 5, 0, 4, 1, 6, 8, 10, 9, 7)
    send_memory(0, 0)
    gather(2, 3, 0, 4, 1, 5, 10, 8, 6, 7, 3, 9, 1, 0, 4, 2, 8, 5, 3, 6, 10, 7, 0, 1)
    send_memory(0, 1)
    gather(2, 7, 6, 5)
    send_memory(1, 0)
    gather(0, 2)
    send_memory(1, 1)
    gather(4, 3, 0, 2, 1, 9, 10, 3, 1, 8)
    need(2)
    unpack_small()
    gather(7)
    need(0, 3)
    arrived(own_rows)
    self_project()
    gather(5)
    self_attend()
    need(1)
    self_close()
    gather(7)
    need(7)
    cross_query()
    gather(6, 5, 9)
    need(5)
    arrived([own_memory])
    arrived_memory(0)
    cross_memory(0)
    cross_attend(0)
    arrived_memory(1)
    cross_memory(1)
    gather(10, 8)
    cross_attend(1)
    gather(9, 6, 4)
    cross_close()
    gather(10)
    need(10)
    ff_up(0)
    gather(8)
    ff_up(1)
    need(8)
    ff_up(2)
    gather(9)
    ff_up(3)
    gather(4)
    need(4)
    ff_down(0)
    ff_down(1)
    need(9)
    ff_down(2)
    need(6)
    ff_down(3)
    close()
    reduce_grad(3)
    scatter(0)
    reduce_grad(2)
    reduce_grad(1)
    reduce_grad(0)
    scatter(2)
    ff_back(3)
    ff_back(2)
    ff_back(1)
    ff_back(0)
    scatter(3, 0, 4, 2)
    cross_open()
    scatter(1)
    cross_back(0)
    scatter(3)
    memory_grad(0)
    send_memory_grad(0)
    scatter(4)
    cross_back(1)
    memory_grad(1)
    send_memory_grad(1)
    scatter(5, 1)
    cross_query_grad()
    scatter(2, 6)
    memory_weight_grad()
    scatter(5, 7)
    self_open()
    scatter(3, 4, 6, 8, 7)
    self_back()
    scatter(8, 0, 1)
    self_grads()
    pack_small()
    scatter(11, 9, 6, 5, 10, 11, 10, 4, 9, 0, 2, 8, 7, 1, 11, 5, 10, 3, 6, 9, 7, 0, 8, 11, 2, 1, 4)
    input_grad()
    scatter(9, 5, 10, 7, 8, 3, 6, 11, 9, 10, 0, 5, 2, 6, 4, 7, 8, 3, 11, 1, 10, 9)
    for work in scatters:
        while not work.over:
            work.step()
    for wait in grad_waits:
        wait.wait_recv()
    for wait in local_waits:
        wait.wait()
    links.finish()


def copy_count(grid, members, slots):
    def copies(order):
        steps = steps_of(grid, order)
        return sum(2 if axis in "zZ" and "Z" in steps else grid[axis] - 1 for axis in steps)

    count = sum(copies(order) * (2 if low == 0 else 1) for low, _, order in GATHER_CHUNKS)
    count += sum(copies(order) for _, _, order in SCATTER_CHUNKS) + copies(SCATTER_CHUNKS[-1][2])
    return count + (members - 1) * (2 * slots + slots)


def run_layer(sizes, grid, scalars, small, large):
    x, memory = large[0], large[-1]
    slots, span, width = x.shape
    rows = slots * span
    members = sizes["x"] * sizes["c"]
    chunk = memory.shape[1]
    pairs = width // HD // 2
    ff_blocks = (BLOCKS - EXPAND) // 2
    place = tuple(grid[axis] for axis in AXES)
    mem_shape = (slots, members, chunk, width)
    count = copy_count(grid, members, slots)
    scratch = {
        "w": pltpu.VMEM((BLOCKS,) + place + (ROWS, width), BF16),
        "small": pltpu.VMEM(place + (ROWS, LANES), BF16),
        "packet": pltpu.VMEM((ROWS, LANES), F32),
        "gw": pltpu.VMEM((BLOCKS,) + place + (ROWS, width), BF16),
        "gsmall": pltpu.VMEM(place + (ROWS, LANES), BF16),
        "land": [
            landing_shapes(grid, order, (high - low,), (ROWS, width)) for low, high, order in SCATTER_CHUNKS
        ],
        "land_small": landing_shapes(grid, SCATTER_CHUNKS[-1][2], (), (ROWS, LANES)),
        "pc": pltpu.VMEM((slots, pairs, 2 * span, members * chunk), BF16),
        "ps": pltpu.VMEM((slots, pairs, 2 * span, span), BF16),
        "share": pltpu.VMEM((slots, pairs, 2 * span, 1), F32),
        "share2": pltpu.VMEM((slots, pairs, 2 * span, 1), F32),
        "f": pltpu.VMEM((ff_blocks, rows, width), BF16),
        "slope": pltpu.VMEM((ff_blocks, rows, width), F32),
        "rows": pltpu.VMEM((ROWS, width), F32),
        "rows_grad": pltpu.VMEM((ROWS, width), F32),
        "ebias": pltpu.VMEM((1, width * ff_blocks), F32),
        "ebias_grad": pltpu.VMEM((1, width * ff_blocks), F32),
        "tokens": pltpu.VMEM((8, LANES), F32),
        "d1": pltpu.VMEM((rows, 1), F32),
        "d2": pltpu.VMEM((rows, 1), F32),
        "send": pltpu.SemaphoreType.DMA((count,)),
        "recv": pltpu.SemaphoreType.DMA((count,)),
        "local": pltpu.SemaphoreType.DMA((BLOCKS + 3 + slots + len(small) + len(scalars),)),
        "scalars": [pltpu.SMEM(part.shape, part.dtype) for part in scalars],
        "params": [pltpu.VMEM(part.shape, BF16) for part in small],
    }
    for name in ("mem", "k2", "v2", "dk2", "dv2", "gmem"):
        scratch[name] = pltpu.VMEM(mem_shape, BF16)
    for name in ("q", "k", "v", "a", "h1b", "q2", "a2", "h2b", "e", "da", "dq", "dk", "dv"):
        scratch[name] = pltpu.VMEM((rows, width), BF16)
    for name in ("n1", "n2", "h1", "r3", "dr", "af", "a2f"):
        scratch[name] = pltpu.VMEM((rows, width), F32)
    for name in ("x", "dy"):
        scratch[name] = pltpu.VMEM(x.shape, BF16)
    leaves, tree = jax.tree.flatten(scratch)

    counts = (len(scalars), len(small), len(large), len(small), len(large))

    def kernel(*refs):
        groups, at = [], 0
        for size in counts:
            groups.append(refs[at : at + size])
            at += size
        layer_kernel(
            sizes, grid, groups[0], groups[1], *groups[2], groups[3], *groups[4],
            jax.tree.unflatten(tree, refs[at:]),
        )

    anywhere, vmem = pl.BlockSpec(memory_space=pl.ANY), pl.BlockSpec(memory_space=pltpu.VMEM)
    outs = [(part.shape, F32) for part in small]
    outs += [(x.shape, BF16), (x.shape, BF16)] + [(part.shape, F32) for part in large[2:6]] + [(memory.shape, BF16)]
    return pl.pallas_call(
        kernel,
        out_shape=tuple(pltpu.VMEM(shape, dtype) for shape, dtype in outs),
        in_specs=[anywhere] * sum(counts[:3]),
        out_specs=[vmem] * sum(counts[3:]),
        scratch_shapes=leaves,
        compiler_params=pltpu.CompilerParams(
            collective_id=0, has_side_effects=True, vmem_limit_bytes=58 << 20
        ),
    )(*scalars, *small, *large)


def copy_kernel(*refs):
    count, sems = len(refs) // 2, refs[-1]
    copies = [pltpu.make_async_copy(refs[n], refs[count + n], sems.at[n]) for n in range(count)]
    for copy in copies:
        copy.start()
    for copy in copies:
        copy.wait()


def handed_out(results):
    anywhere, vmem = pl.BlockSpec(memory_space=pl.ANY), pl.BlockSpec(memory_space=pltpu.VMEM)
    return pl.pallas_call(
        copy_kernel,
        out_shape=tuple(pltpu.HBM(part.shape, part.dtype) for part in results),
        in_specs=[vmem] * len(results),
        out_specs=[anywhere] * len(results),
        scratch_shapes=[pltpu.SemaphoreType.DMA((len(results),))],
        compiler_params=pltpu.CompilerParams(vmem_limit_bytes=32 << 20),
    )(*(pltpu.with_memory_space_constraint(part, pltpu.VMEM) for part in results))


def shards(
    sizes,
    decoder_in, memory, grad_out, decoder_lengths, memory_lengths, item_route,
    in_projection, out_projection, attention_bias, expand_weight, expand_bias,
    reduce_weight, reduce_bias, norm_gain, norm_bias,
):
    joined = in_projection.shape[1] < ROWS
    small = [attention_bias, norm_gain, norm_bias, reduce_bias[None], expand_bias[None]]
    weights = [in_projection, out_projection, expand_weight, reduce_weight.T]
    along = (1, 1, 0, 0)
    lengths, routes = decoder_lengths, item_route
    grid = dict(sizes)
    if joined:
        grid.update(x=1, c=1)
        small = [lax.all_gather(part, "mem", axis=1, tiled=True) for part in small]
        weights = [lax.all_gather(part, "mem", axis=axis, tiled=True) for part, axis in zip(weights, along)]
        lengths = lax.all_gather(lengths, "mem", tiled=True)
        routes = lax.all_gather(routes, "mem", tiled=True)
    results = run_layer(
        sizes, grid, (decoder_lengths, memory_lengths, item_route, lengths, routes), small,
        [decoder_in, grad_out] + weights + [memory],
    )
    if joined:
        results = list(results)
        for number in range(5):
            results[number] = lax.psum_scatter(results[number], "mem", scatter_dimension=1, tiled=True)
        for number, axis in zip(range(7, 11), along):
            results[number] = lax.psum_scatter(results[number], "mem", scatter_dimension=axis, tiled=True)
    else:
        results = handed_out(results)
    bias, gain, shift, reduce_shift, expand_shift, out, dx, g_in, g_out, g_expand, g_reduce, g_memory = results
    return (
        out, dx, g_memory, g_in, g_out, bias, g_expand, expand_shift[0], g_reduce.T, reduce_shift[0], gain, shift,
    )


def solution(mesh):
    both = ("bucket", "mem")
    buckets, members = mesh.shape["bucket"], mesh.shape["mem"]
    cores = 2
    across = members // cores
    sizes = {"z": buckets // across, "y": across, "x": across, "c": cores}
    in_specs = (
        P(both, None, None), P("bucket", "mem", None), P(both, None, None), P(both), P(both), P(both),
        P(None, both, None), P(None, both, None), P(None, both), P(both, None), P(both),
        P(None, both), P(both), P(None, both), P(None, both),
    )
    out_specs = (
        P(both, None, None), P(both, None, None), P("bucket", "mem", None),
        P(None, both, None), P(None, both, None), P(None, both), P(both, None), P(both),
        P(None, both), P(both), P(None, both), P(None, both),
    )
    return jax.shard_map(
        functools.partial(shards, sizes), mesh=mesh, in_specs=in_specs, out_specs=out_specs, check_vma=False
    )
```

```python
import functools

import jax
import jax.numpy as jnp
from jax import lax
from jax.experimental import pallas as pl
from jax.experimental.pallas import tpu as pltpu
from jax.sharding import PartitionSpec as P

HD = 64
EPS = 1e-05
NEG = -1e30
F32 = jnp.float32
BF16 = jnp.bfloat16
MESH = pl.DeviceIdType.MESH
LANES = 128
ROWS = 16

SQ, SK, SV, SO, CK, CV, CQ, CO, EXPAND, REDUCE = 0, 1, 2, 3, 4, 5, 6, 7, 8, 12
BLOCKS = 16
GATHER_CHUNKS = (
    (1, 2, "zxyc"), (3, 4, "xyzc"), (0, 1, "xzyc"), (2, 3, "zxyc"), (12, 14, "zyxc"),
    (4, 6, "xyzc"), (15, 16, "xzyc"), (6, 8, "zxyc"), (10, 12, "zxyc"), (14, 15, "xyzc"),
    (8, 10, "xyzc"),
)
SCATTER_CHUNKS = (
    (15, 16, "cxyz"), (14, 15, "czyx"), (12, 14, "cyzx"), (10, 12, "czyx"), (8, 10, "cyzx"),
    (7, 8, "cyzx"), (6, 7, "cyzx"), (4, 6, "cyxz"), (3, 4, "cyxz"), (0, 1, "cyxz"),
    (1, 2, "cxzy"), (2, 3, "czyx"),
)
AXES = "zyxc"


def mm(left, right):
    return lax.dot_general(left, right, (((1,), (0,)), ((), ())), preferred_element_type=F32)


def mm_nt(left, right):
    return lax.dot_general(left, right, (((1,), (1,)), ((), ())), preferred_element_type=F32)


def mm_tn(left, right):
    return lax.dot_general(left, right, (((0,), (0,)), ((), ())), preferred_element_type=F32)


def only_if(condition, action):
    if condition is None:
        action()
    else:
        pl.when(condition)(action)


class Landing:
    def __init__(self, copy, lands):
        self.copy, self.lands = copy, lands

    def wait_recv(self):
        only_if(self.lands, self.copy.wait_recv)


def steps_of(grid, order):
    steps = []
    for axis in order:
        if axis == "z" and grid["z"] == 4:
            steps += ["z", "Z"]
        elif grid[axis] > 1:
            steps.append(axis)
    return steps


class Links:
    def __init__(self, send_sems, recv_sems):
        self.send_sems, self.recv_sems, self.used, self.sent = send_sems, recv_sems, 0, []

    def pair(self):
        self.used += 1
        return self.send_sems.at[self.used - 1], self.recv_sems.at[self.used - 1]

    def copy(self, source, target, landing, device, sends=None, lands=None):
        send, recv = self.pair()
        out = pltpu.make_async_remote_copy(
            src_ref=source, dst_ref=target, send_sem=send, recv_sem=recv,
            device_id=device, device_id_type=MESH,
        )
        only_if(sends, out.start)
        self.sent.append((sends, out))
        return Landing(
            pltpu.make_async_remote_copy(
                src_ref=source, dst_ref=landing, send_sem=send, recv_sem=recv,
                device_id=device, device_id_type=MESH,
            ),
            lands,
        )

    def finish(self):
        for sends, out in self.sent:
            only_if(sends, out.wait_send)


class Place:
    def __init__(self, sizes):
        self.sizes = sizes
        bucket, mem = lax.axis_index("bucket"), lax.axis_index("mem")
        self.bucket, self.mem = bucket, mem
        self.at = {
            "z": bucket // sizes["y"], "y": bucket % sizes["y"],
            "x": mem // sizes["c"], "c": mem % sizes["c"],
        }

    def on_line(self):
        z = self.at["z"]
        side = z // 2
        middle = (z == 1) | (z == 2)
        return middle, jnp.logical_not(middle), z + 1 - 2 * (z % 2), 2 - side, 3 * (1 - side), 2 * (1 - side)

    def at_z(self, z):
        return (z * self.sizes["y"] + self.at["y"], self.mem)

    def shifted(self, axis, step):
        size = self.sizes[axis]
        return lax.rem(self.at[axis] + (step % size), size)

    def device(self, axis, step):
        at = dict(self.at)
        at[axis] = self.shifted(axis, step)
        return (at["z"] * self.sizes["y"] + at["y"], at["x"] * self.sizes["c"] + at["c"])


def block_view(ref, lead, index):
    return ref.at[tuple(lead) + tuple(index[axis] for axis in AXES)]


class Gather:
    def index(self, known):
        return {
            axis: slice(None) if axis in known else (self.place.at[axis] if self.grid[axis] > 1 else 0)
            for axis in AXES
        }

    def line_step(self, axis, known):
        middle, end, pair, far_middle, far_end, far_first = self.place.on_line()

        def send(source_z, landing_z, target_z, sends, lands):
            source, landing = self.index(known), self.index(known)
            source["z"], landing["z"] = source_z, landing_z
            for ref, lead in self.parts:
                here = block_view(ref, lead, source)
                self.waits.append(
                    self.links.copy(
                        here, here, block_view(ref, lead, landing), self.place.at_z(target_z), sends, lands
                    )
                )

        z = self.place.at["z"]
        if axis == "z":
            send(z, far_end, far_middle, end, middle)
            send(z, far_middle, far_middle, middle, middle)
            send(z, pair, pair, None, None)
        else:
            both = pl.ds(far_first, 2)
            send(both, both, pair, middle, end)

    def __init__(self, links, place, grid, order, parts):
        self.links, self.place, self.parts = links, place, parts
        self.order = steps_of(grid, order)
        self.grid, self.waits, self.done = grid, [], 0

    @property
    def over(self):
        return self.done > len(self.order)

    def step(self):
        if self.over:
            return
        for wait in self.waits:
            wait.wait_recv()
        self.waits = []
        if self.done < len(self.order):
            axis = self.order[self.done]
            known = self.order[: self.done]
            if axis in "zZ" and "Z" in self.order:
                self.line_step(axis, known)
                self.done += 1
                return
            for hop in range(1, self.grid[axis]):
                mine, theirs = self.index(known), self.index(known)
                theirs[axis] = self.place.shifted(axis, -hop)
                for ref, lead in self.parts:
                    self.waits.append(
                        self.links.copy(
                            block_view(ref, lead, mine), block_view(ref, lead, mine),
                            block_view(ref, lead, theirs), self.place.device(axis, hop),
                        )
                    )
        self.done += 1


class Scatter:
    def __init__(self, links, place, grid, order, parts, landings, emit):
        self.links, self.place, self.parts, self.landings = links, place, parts, landings
        self.order = steps_of(grid, order)
        self.grid, self.waits, self.done, self.emit = grid, [], 0, emit

    def index(self, known):
        return {
            axis: (self.place.at[axis] if self.grid[axis] > 1 else 0) if axis in known or self.grid[axis] == 1
            else slice(None)
            for axis in AXES
        }

    @property
    def over(self):
        return self.done > len(self.order)

    def step(self):
        if self.over:
            return
        for wait in self.waits:
            wait.wait_recv()
        self.waits = []
        if self.done > 0 and self.order[self.done - 1] == "z" and "Z" in self.order:
            self.line_add()
        elif self.done > 0:
            axis = self.order[self.done - 1]
            last = self.done == len(self.order)
            index = self.index(self.order[: self.done])
            for number, (ref, lead) in enumerate(self.parts):
                where = tuple(lead) + tuple(index[name] for name in AXES)
                landed = self.landings[number][self.done - 1]
                if landed.shape[0] == 1 and not last:
                    ref[where] = ref[where] + landed[0]
                    continue
                total = ref[where].astype(F32)
                for hop in range(landed.shape[0]):
                    total += landed[hop].astype(F32)
                if last:
                    self.emit[number](total)
                else:
                    ref[where] = total.astype(ref.dtype)
        if self.done < len(self.order):
            axis = self.order[self.done]
            known = self.order[: self.done]
            if axis in "zZ" and "Z" in self.order:
                self.line_step(axis, known)
                self.done += 1
                return
            for hop in range(1, self.grid[axis]):
                theirs = self.index(known)
                theirs[axis] = self.place.shifted(axis, hop)
                for number, (ref, lead) in enumerate(self.parts):
                    landing = self.landings[number][self.done].at[hop - 1]
                    self.waits.append(
                        self.links.copy(
                            block_view(ref, lead, theirs), landing, landing, self.place.device(axis, hop)
                        )
                    )
        self.done += 1


    def line_step(self, axis, known):
        middle, end, pair, far_middle, far_end, far_first = self.place.on_line()
        known = [name for name in known if name != "z"]

        def send(source_z, landing, target_z, sends, lands):
            source = self.index(known)
            source["z"] = source_z
            for number, (ref, lead) in enumerate(self.parts):
                held = landing(self.landings[number])
                self.waits.append(
                    self.links.copy(
                        block_view(ref, lead, source), held, held, self.place.at_z(target_z), sends, lands
                    )
                )

        first = self.order.index("z")
        if axis == "z":
            send(pl.ds(far_first, 2), lambda held: held[first], pair, end, middle)
            self.pair_waits = []
            waits, self.waits = self.waits, []
            send(pair, lambda held: held[first + 1].at[0], pair, None, None)
            self.pair_waits, self.waits = self.waits, waits
        else:
            send(far_middle, lambda held: held[first + 1].at[1], far_middle, middle, middle)
            send(far_end, lambda held: held[first + 1].at[1], far_end, middle, end)
            self.waits += self.pair_waits

    def line_add(self):
        middle, _, _, _, _, far_first = self.place.on_line()
        first = self.order.index("z")
        index = self.index(self.order[:first])
        index["z"] = pl.ds(far_first, 2)

        @pl.when(middle)
        def _():
            for number, (ref, lead) in enumerate(self.parts):
                where = tuple(lead) + tuple(index[name] for name in AXES)
                ref[where] = ref[where] + self.landings[number][first][...]


def landing_shapes(grid, order, lead_shape, tail_shape):
    shapes, left = [], {axis: grid[axis] for axis in AXES}
    steps = steps_of(grid, order)
    for axis in steps:
        left[axis.lower()] = 1
        kept = tuple(left[name] for name in AXES if left[name] > 1)
        if axis == "z" and "Z" in steps:
            shape = lead_shape + (2,) + kept + tail_shape
        else:
            shape = (2 if axis == "Z" else grid[axis] - 1,) + lead_shape + kept + tail_shape
        shapes.append(pltpu.VMEM(shape, BF16))
    return shapes


def layer_kernel(
    sizes, grid,
    scalars_hbm, small_hbm,
    x_hbm, dy_hbm, in_hbm, out_hbm, expand_hbm, reduce_hbm, memory_ref,
    grad_small_refs,
    y_ref, dx_ref, grad_in_ref, grad_out_ref, grad_expand_ref, grad_reduce_ref, gmem_ref,
    scratch,
):
    s = scratch
    place = Place(sizes)
    links = Links(s["send"], s["recv"])
    x_ref, dy_ref = s["x"], s["dy"]
    slots, span, width = x_ref.shape
    rows = slots * span
    members, chunk = s["mem"].shape[1], s["mem"].shape[2]
    reach_span = members * chunk
    heads = width // HD
    pairs = heads // 2
    ff_blocks = (BLOCKS - EXPAND) // 2
    places = width // ROWS
    locals_used = [0]

    def local_copy(source, target):
        locals_used[0] += 1
        copy = pltpu.make_async_copy(source, target, s["local"].at[locals_used[0] - 1])
        copy.start()
        return copy

    barrier = pltpu.get_barrier_semaphore()
    lengths_ref, reaches_ref, routes_ref, all_lengths_ref, all_routes_ref = s["scalars"]
    attention_bias_ref, gain_ref, shift_ref, reduce_bias_ref, expand_bias_ref = s["params"]
    peers = []
    for axis in "zy":
        peers += [place.device(axis, hop) for hop in range(1, sizes[axis])]
    others = [lax.rem(place.mem + hop, members) for hop in range(1, members)]
    peers += [(place.bucket, other) for other in others]
    for peer in peers:
        pl.semaphore_signal(barrier, inc=1, device_id=peer, device_id_type=MESH)

    here = tuple(place.at[axis] if grid[axis] > 1 else 0 for axis in AXES)

    def block_parts(in_ref, out_ref, expand_ref, reduce_ref):
        parts = [(SQ + k, in_ref.at[k]) for k in range(3)] + [(CQ, in_ref.at[3]), (CK, in_ref.at[4])]
        parts += [(CV, in_ref.at[5]), (SO, out_ref.at[0]), (CO, out_ref.at[1])]
        for k in range(ff_blocks):
            lanes = pl.ds(k * width, width)
            parts += [(EXPAND + k, expand_ref.at[:, lanes]), (REDUCE + k, reduce_ref.at[:, lanes])]
        return sorted(parts, key=lambda part: part[0])

    own_small = [local_copy(source, target) for source, target in zip(small_hbm, s["params"])]
    own_small += [local_copy(source, target) for source, target in zip(scalars_hbm, s["scalars"])]
    own = [
        local_copy(part, s["w"].at[(number,) + here])
        for number, part in block_parts(in_hbm, out_hbm, expand_hbm, reduce_hbm)
    ]
    own_rows = [local_copy(x_hbm, x_ref), local_copy(dy_hbm, dy_ref)]
    own_memory = local_copy(memory_ref.at[pl.ds(place.mem * slots, slots)], s["mem"].at[:, place.mem])

    spot = here[0]
    for axis, at in zip(AXES[1:], here[1:]):
        spot = spot * grid[axis] + at
    share = expand_bias_ref.shape[1]
    group, pieces = LANES // ROWS, LANES // share
    for copy in own_small:
        copy.wait()
    packet = s["packet"]
    packet[...] = jnp.zeros_like(packet)
    packet[0:6, 0:ROWS] = attention_bias_ref[...].astype(F32)
    packet[6:9, 0:ROWS] = gain_ref[...].astype(F32)
    packet[9:12, 0:ROWS] = shift_ref[...].astype(F32)
    packet[12:13, 0:ROWS] = reduce_bias_ref[...].astype(F32)
    packet[13:14, 0:share] = expand_bias_ref[...].astype(F32)
    narrow = pltpu.roll(packet[...], lax.rem(spot, group) * ROWS, 1)
    wide = pltpu.roll(packet[...], lax.rem(spot, pieces) * share, 1)
    row = lax.broadcasted_iota(jnp.int32, (ROWS, LANES), 0)
    lane = lax.broadcasted_iota(jnp.int32, (ROWS, LANES), 1)
    live = jnp.zeros((ROWS, LANES), jnp.int32)
    for slot in range(all_lengths_ref.shape[0]):
        count = jnp.where(all_routes_ref[slot] >= 0, all_lengths_ref[slot], 0)
        live = jnp.where(lane == slot, count, live)
    value = jnp.where(row == 13, wide, jnp.where(row == 14, live.astype(F32), narrow))
    s["small"][here] = value.astype(BF16)
    for copy in own:
        copy.wait()
    pl.semaphore_wait(barrier, len(peers))

    gathers = []
    for low, high, order in GATHER_CHUNKS:
        parts = [(s["w"], (slice(low, high),))]
        if low == 0:
            parts.append((s["small"], ()))
        gathers.append(Gather(links, place, grid, order, parts))
    memory_waits = [[] for _ in range(slots)]
    half = chunk // 2

    def send_memory(slot, part):
        at = pl.ds(part * half, half)
        for hop, other in zip(range(1, members), others):
            sender = lax.rem(place.mem + members - hop, members)
            memory_waits[slot].append(
                links.copy(
                    memory_ref.at[other * slots + slot, at], s["mem"].at[slot, place.mem, at],
                    s["mem"].at[slot, sender, at], (place.bucket, other),
                )
            )

    def weight(number):
        return s["w"][number].reshape(width, width)

    def put_grad(number, value):
        ref = s["gw"]
        ref[number] = value.astype(BF16).reshape(ref.shape[1:])

    even_lanes = lax.broadcasted_iota(jnp.int32, (1, LANES), 1) < HD
    even = jnp.where(even_lanes, 1.0, 0.0)
    odd = 1.0 - even
    scale = HD ** (-0.5)

    def stack(value, factor=1.0):
        return jnp.concatenate([value * (even * factor).astype(BF16), value * (odd * factor).astype(BF16)], axis=0)

    def unstack(value, factor=1.0):
        return value[:span] * (even * factor) + value[span:] * (odd * factor)

    def normed(value):
        centered = value - jnp.mean(value, axis=-1, keepdims=True)
        rstd = lax.rsqrt(jnp.mean(centered * centered, axis=-1, keepdims=True) + EPS)
        return centered * rstd, rstd

    def norm_back(grad, unit, rstd, number):
        s["rows_grad"][6 + number : 7 + number, :] = jnp.sum(grad * unit, axis=0, keepdims=True)
        s["rows_grad"][9 + number : 10 + number, :] = jnp.sum(grad, axis=0, keepdims=True)
        scaled = grad * s["rows"][6 + number : 7 + number, :]
        return (
            scaled - jnp.mean(scaled, axis=-1, keepdims=True)
            - unit * jnp.mean(scaled * unit, axis=-1, keepdims=True)
        ) * rstd

    def column_sum(value):
        return jnp.sum(value.astype(F32), axis=0, keepdims=True)

    def bias(number):
        return s["rows"][number : number + 1, :]

    def unpack_small():
        every = s["small"][...].reshape(places, ROWS, LANES).astype(F32)
        columns = [jnp.sum(every[g * group : (g + 1) * group], axis=0) for g in range(places // group)]
        s["rows"][...] = jnp.concatenate(columns, axis=1)
        columns = [
            jnp.sum(every[g * pieces : (g + 1) * pieces, 13], axis=0, keepdims=True) for g in range(places // pieces)
        ]
        s["ebias"][...] = jnp.concatenate(columns, axis=1)
        tokens = jnp.sum(jnp.sum(every[:, 14], axis=0, keepdims=True), axis=1, keepdims=True)
        s["tokens"][...] = jnp.broadcast_to(tokens, s["tokens"].shape)

    def self_project():
        x = x_ref[...].reshape(rows, width)
        s["q"][...] = (mm(x, weight(SQ)) + bias(0)).astype(BF16)
        s["k"][...] = mm(x, weight(SK)).astype(BF16)
        s["v"][...] = (mm(x, weight(SV)) + bias(1)).astype(BF16)

    def attend(low_ref, share_ref, mixed_ref, queries, keys_in, values_in, keep, at, lanes):
        scores = jnp.where(keep, mm_nt(stack(queries, scale), keys_in), NEG)
        weights = jnp.exp(scores - jnp.max(scores, axis=-1, keepdims=True))
        part = 1.0 / jnp.sum(weights, axis=-1, keepdims=True)
        low = weights.astype(BF16)
        low_ref[...] = low
        share_ref[...] = part
        mixed_ref[at, lanes] = unstack(mm(low, values_in) * part)

    def attend_back(low_ref, share_ref, mixed, da, queries, keys_in, values_in):
        low, part = low_ref[...], share_ref[...]
        da = stack(da).astype(F32) * part
        delta = jnp.sum(da * jnp.concatenate([mixed, mixed], axis=0), axis=-1, keepdims=True)
        da = da.astype(BF16)
        ds = (low.astype(F32) * (mm_nt(da, values_in) - delta)).astype(BF16)
        return (
            unstack(mm(ds, keys_in), scale).astype(BF16),
            mm_tn(ds, stack(queries, scale)).astype(BF16),
            mm_tn(low, da).astype(BF16),
        )

    def self_attend():
        row = lax.broadcasted_iota(jnp.int32, (2 * span, span), 0) % span
        col = lax.broadcasted_iota(jnp.int32, (2 * span, span), 1)
        for slot in range(slots):
            keep = (col <= row) & (col < lengths_ref[slot])
            at = slice(slot * span, (slot + 1) * span)
            for pair in range(pairs):
                lanes = slice(pair * LANES, (pair + 1) * LANES)
                attend(
                    s["ps"].at[slot, pair], s["share"].at[slot, pair], s["af"],
                    s["q"][at, lanes], s["k"][at, lanes], s["v"][at, lanes], keep, at, lanes,
                )
        s["a"][...] = s["af"][...].astype(BF16)

    def self_close():
        x = x_ref[...].reshape(rows, width).astype(F32)
        unit, rstd = normed(x + mm(s["a"][...], weight(SO)) + bias(2))
        s["n1"][...], s["d1"][...] = unit, rstd
        h1 = unit * bias(6) + bias(9)
        s["h1"][...] = h1
        s["h1b"][...] = h1.astype(BF16)

    def cross_query():
        s["q2"][...] = (mm(s["h1b"][...], weight(CQ)) + bias(3)).astype(BF16)

    def cross_memory(slot):
        items = s["mem"][slot].reshape(reach_span, width)
        s["k2"][slot] = mm(items, weight(CK)).astype(BF16).reshape(members, chunk, width)
        s["v2"][slot] = (mm(items, weight(CV)) + bias(4)).astype(BF16).reshape(members, chunk, width)

    def keys(name, slot, lanes):
        return s[name][slot, :, :, lanes].reshape(reach_span, LANES)

    def cross_attend(slot):
        col = lax.broadcasted_iota(jnp.int32, (1, reach_span), 1)
        keep = col < reaches_ref[slot]
        at = slice(slot * span, (slot + 1) * span)

        def body(pair, carry):
            lanes = pl.ds(pl.multiple_of(pair * LANES, LANES), LANES)
            attend(
                s["pc"].at[slot, pair], s["share2"].at[slot, pair], s["a2f"],
                s["q2"][at, lanes], keys("k2", slot, lanes), keys("v2", slot, lanes), keep, at, lanes,
            )
            return carry
        lax.fori_loop(0, pairs, body, 0, unroll=4)

    def cross_close():
        s["a2"][...] = s["a2f"][...].astype(BF16)
        unit, rstd = normed(s["h1"][...] + mm(s["a2"][...], weight(CO)) + bias(5))
        s["n2"][...], s["d2"][...] = unit, rstd
        h2 = unit * bias(7) + bias(10)
        s["h2b"][...] = h2.astype(BF16)
        s["r3"][...] = h2 + bias(12)

    def ff_up(block):
        lanes = slice(block * width, (block + 1) * width)
        u = mm(s["h2b"][...], weight(EXPAND + block)) + s["ebias"][:, lanes]
        sig = 1.0 / (1.0 + jnp.exp(-u))
        s["f"][block] = (u * sig).astype(BF16)
        s["slope"][block] = sig * (1.0 + u * (1.0 - sig))

    def ff_down(block):
        s["r3"][...] += mm_nt(s["f"][block], weight(REDUCE + block))

    def live_rows(each):
        row = lax.broadcasted_iota(jnp.int32, (rows, 1), 0)
        count = jnp.zeros((rows, 1), jnp.int32)
        for slot in range(slots):
            here_count = jnp.where(routes_ref[slot] >= 0, each(slot), 0)
            count = jnp.where((row >= slot * span) & (row < (slot + 1) * span), here_count + slot * span, count)
        return row < count

    def close():
        unit, rstd = normed(s["r3"][...])
        y = unit * bias(8) + bias(11)
        y = jnp.where(live_rows(lambda slot: span), y, 0.0)
        y_ref[...] = y.astype(BF16).reshape(x_ref.shape)
        dy = dy_ref[...].reshape(rows, width).astype(F32)
        dy = jnp.where(live_rows(lambda slot: lengths_ref[slot]), dy, 0.0)
        dr3 = norm_back(dy, unit, rstd, 2)
        s["dr"][...] = dr3
        s["e"][...] = dr3.astype(BF16)
        s["rows_grad"][12:13, :] = column_sum(s["e"][...])

    def reduce_grad(block):
        put_grad(REDUCE + block, mm_tn(s["e"][...], s["f"][block]))

    def ff_back(block):
        lanes = slice(block * width, (block + 1) * width)
        du = (mm(s["e"][...], weight(REDUCE + block)) * s["slope"][block]).astype(BF16)
        s["ebias_grad"][:, lanes] = column_sum(du)
        put_grad(EXPAND + block, mm_tn(s["h2b"][...], du))
        s["dr"][...] += mm_nt(du, weight(EXPAND + block))

    def cross_open():
        dr2 = norm_back(s["dr"][...], s["n2"][...], s["d2"][...], 1)
        s["dr"][...] = dr2
        e2 = dr2.astype(BF16)
        s["rows_grad"][5:6, :] = column_sum(e2)
        put_grad(CO, mm_tn(s["a2"][...], e2))
        s["da"][...] = mm_nt(e2, weight(CO)).astype(BF16)

    def cross_back(slot):
        at = slice(slot * span, (slot + 1) * span)

        def body(pair, carry):
            lanes = pl.ds(pl.multiple_of(pair * LANES, LANES), LANES)
            shape = (members, chunk, LANES)
            dq, dk, dv = attend_back(
                s["pc"].at[slot, pair], s["share2"].at[slot, pair], s["a2f"][at, lanes], s["da"][at, lanes],
                s["q2"][at, lanes], keys("k2", slot, lanes), keys("v2", slot, lanes),
            )
            s["dq"][at, lanes] = dq
            s["dk2"][slot, :, :, lanes] = dk.reshape(shape)
            s["dv2"][slot, :, :, lanes] = dv.reshape(shape)
            return carry
        lax.fori_loop(0, pairs, body, 0, unroll=4)

    def memory_grad(slot):
        value = mm_nt(s["dk2"][slot].reshape(reach_span, width), weight(CK))
        value += mm_nt(s["dv2"][slot].reshape(reach_span, width), weight(CV))
        s["gmem"][slot] = value.astype(BF16).reshape(members, chunk, width)

    def send_memory_grad(slot):
        mine = gmem_ref.at[place.mem * slots + slot]
        local_waits.append(local_copy(s["gmem"].at[slot, place.mem], mine))
        for hop, other in zip(range(1, members), others):
            sender = lax.rem(place.mem + members - hop, members)
            grad_waits.append(
                links.copy(
                    s["gmem"].at[slot, other], mine, gmem_ref.at[sender * slots + slot], (place.bucket, other)
                )
            )

    local_waits, grad_waits = [], []

    def cross_query_grad():
        dq = s["dq"][...]
        s["rows_grad"][3:4, :] = column_sum(dq)
        put_grad(CQ, mm_tn(s["h1b"][...], dq))

    def memory_weight_grad():
        items = s["mem"][...].reshape(slots * reach_span, width)
        put_grad(CK, mm_tn(items, s["dk2"][...].reshape(slots * reach_span, width)))
        dv = s["dv2"][...].reshape(slots * reach_span, width)
        put_grad(CV, mm_tn(items, dv))
        s["rows_grad"][4:5, :] = column_sum(dv)

    def self_open():
        dh1 = s["dr"][...] + mm_nt(s["dq"][...], weight(CQ))
        dr1 = norm_back(dh1, s["n1"][...], s["d1"][...], 0)
        s["dr"][...] = dr1
        e1 = dr1.astype(BF16)
        s["rows_grad"][2:3, :] = column_sum(e1)
        put_grad(SO, mm_tn(s["a"][...], e1))
        s["da"][...] = mm_nt(e1, weight(SO)).astype(BF16)

    def self_back():
        for slot in range(slots):
            at = slice(slot * span, (slot + 1) * span)
            for pair in range(pairs):
                lanes = slice(pair * LANES, (pair + 1) * LANES)
                s["dq"][at, lanes], s["dk"][at, lanes], s["dv"][at, lanes] = attend_back(
                    s["ps"].at[slot, pair], s["share"].at[slot, pair], s["af"][at, lanes], s["da"][at, lanes],
                    s["q"][at, lanes], s["k"][at, lanes], s["v"][at, lanes],
                )

    def self_grads():
        x = x_ref[...].reshape(rows, width)
        put_grad(SV, mm_tn(x, s["dv"][...]))
        put_grad(SQ, mm_tn(x, s["dq"][...]))
        put_grad(SK, mm_tn(x, s["dk"][...]))
        s["rows_grad"][0:1, :] = column_sum(s["dq"][...])
        s["rows_grad"][1:2, :] = column_sum(s["dv"][...])

    def input_grad():
        total = s["dr"][...] + mm_nt(s["dq"][...], weight(SQ))
        total += mm_nt(s["dk"][...], weight(SK)) + mm_nt(s["dv"][...], weight(SV))
        dx_ref[...] = total.astype(BF16).reshape(x_ref.shape)

    def turned(value, lanes):
        return value if lanes == 0 else pltpu.roll(value, LANES - lanes, 1)

    def pack_small():
        row = lax.broadcasted_iota(jnp.int32, (ROWS, LANES), 0)
        for number in range(places):
            at = number // group * LANES
            base = turned(s["rows_grad"][:, at : at + LANES], number % group * ROWS)
            at = number // pieces * LANES
            extra = turned(s["ebias_grad"][:, at : at + LANES], number % pieces * share)
            index, rest = [], number
            for axis in reversed(AXES):
                index.insert(0, rest % grid[axis])
                rest //= grid[axis]
            s["gsmall"][tuple(index)] = jnp.where(row == 13, extra, base).astype(BF16)

    targets = dict(block_parts(grad_in_ref, grad_out_ref, grad_expand_ref, grad_reduce_ref))

    def emit_weight(low, high):
        def emit(total):
            for number in range(low, high):
                targets[number][...] = total[number - low] / s["tokens"][0:1, 0:1]
        return emit

    def emit_small(total):
        value = total / s["tokens"][0:1, 0:1]
        first = 0
        for target in grad_small_refs:
            target[...] = value[first : first + target.shape[0], 0 : target.shape[1]]
            first += target.shape[0]

    scatters = []
    for number, (low, high, order) in enumerate(SCATTER_CHUNKS):
        parts, landings, emit = [(s["gw"], (slice(low, high),))], [s["land"][number]], [emit_weight(low, high)]
        if number == len(SCATTER_CHUNKS) - 1:
            parts.append((s["gsmall"], ()))
            landings.append(s["land_small"])
            emit.append(emit_small)
        scatters.append(Scatter(links, place, grid, order, parts, landings, emit))

    def gather(*numbers):
        for number in numbers:
            gathers[number].step()

    def need(*numbers):
        for number in numbers:
            while not gathers[number].over:
                gathers[number].step()

    def scatter(*numbers):
        for number in numbers:
            scatters[number].step()

    def arrived(copies):
        for copy in copies:
            copy.wait()

    def arrived_memory(slot):
        for wait in memory_waits[slot]:
            wait.wait_recv()

    s["rows_grad"][...] = jnp.zeros_like(s["rows_grad"])
    gather(2, 3, 5, 0, 4, 1, 6, 8, 10, 9, 7)
    send_memory(0, 0)
    gather(2, 3, 0, 4, 1, 5, 10, 8, 6, 7, 3, 9, 1, 0, 4, 2, 8, 5, 3, 6, 10, 7, 0, 1)
    send_memory(0, 1)
    gather(2, 7, 6, 5)
    send_memory(1, 0)
    gather(0, 2)
    send_memory(1, 1)
    gather(4, 3, 0, 2, 1, 9, 10, 3, 1, 8)
    need(2)
    unpack_small()
    gather(7)
    need(0, 3)
    arrived(own_rows)
    self_project()
    gather(5)
    self_attend()
    need(1)
    self_close()
    gather(7)
    need(7)
    cross_query()
    gather(6, 5, 9)
    need(5)
    arrived([own_memory])
    arrived_memory(0)
    cross_memory(0)
    cross_attend(0)
    arrived_memory(1)
    cross_memory(1)
    gather(10, 8)
    cross_attend(1)
    gather(9, 6, 4)
    cross_close()
    gather(10)
    need(10)
    ff_up(0)
    gather(8)
    ff_up(1)
    need(8)
    ff_up(2)
    gather(9)
    ff_up(3)
    gather(4)
    need(4)
    ff_down(0)
    ff_down(1)
    need(9)
    ff_down(2)
    need(6)
    ff_down(3)
    close()
    reduce_grad(3)
    reduce_grad(2)
    reduce_grad(1)
    reduce_grad(0)
    scatter(0, 2, 1)
    ff_back(3)
    ff_back(2)
    ff_back(1)
    ff_back(0)
    cross_open()
    scatter(5, 1, 2, 0)
    cross_back(0)
    scatter(3)
    memory_grad(0)
    send_memory_grad(0)
    scatter(4, 5, 3)
    cross_back(1)
    scatter(4, 2)
    memory_grad(1)
    send_memory_grad(1)
    cross_query_grad()
    scatter(6)
    memory_weight_grad()
    scatter(0, 6, 7, 1)
    self_open()
    scatter(3, 4, 7)
    self_back()
    self_grads()
    scatter(10, 9, 8, 6)
    pack_small()
    scatter(11, 2)
    input_grad()
    scatter(9, 11, 4, 5, 8, 10, 3, 7, 0, 9, 1, 11, 10, 8, 5, 6, 0, 7, 4, 9, 2, 1, 10, 11, 8, 3, 7, 6, 5, 9, 11, 8, 10, 4, 1, 6, 2, 0, 3, 7, 9, 11, 5, 10, 8)
    for work in scatters:
        while not work.over:
            work.step()
    for wait in grad_waits:
        wait.wait_recv()
    for wait in local_waits:
        wait.wait()
    links.finish()


def copy_count(grid, members, slots):
    def copies(order):
        steps = steps_of(grid, order)
        return sum(2 if axis in "zZ" and "Z" in steps else grid[axis] - 1 for axis in steps)

    count = sum(copies(order) * (2 if low == 0 else 1) for low, _, order in GATHER_CHUNKS)
    count += sum(copies(order) for _, _, order in SCATTER_CHUNKS) + copies(SCATTER_CHUNKS[-1][2])
    return count + (members - 1) * (2 * slots + slots)


def run_layer(sizes, grid, scalars, small, large):
    x, memory = large[0], large[-1]
    slots, span, width = x.shape
    rows = slots * span
    members = sizes["x"] * sizes["c"]
    chunk = memory.shape[1]
    pairs = width // HD // 2
    ff_blocks = (BLOCKS - EXPAND) // 2
    place = tuple(grid[axis] for axis in AXES)
    mem_shape = (slots, members, chunk, width)
    count = copy_count(grid, members, slots)
    scratch = {
        "w": pltpu.VMEM((BLOCKS,) + place + (ROWS, width), BF16),
        "small": pltpu.VMEM(place + (ROWS, LANES), BF16),
        "packet": pltpu.VMEM((ROWS, LANES), F32),
        "gw": pltpu.VMEM((BLOCKS,) + place + (ROWS, width), BF16),
        "gsmall": pltpu.VMEM(place + (ROWS, LANES), BF16),
        "land": [
            landing_shapes(grid, order, (high - low,), (ROWS, width)) for low, high, order in SCATTER_CHUNKS
        ],
        "land_small": landing_shapes(grid, SCATTER_CHUNKS[-1][2], (), (ROWS, LANES)),
        "pc": pltpu.VMEM((slots, pairs, 2 * span, members * chunk), BF16),
        "ps": pltpu.VMEM((slots, pairs, 2 * span, span), BF16),
        "share": pltpu.VMEM((slots, pairs, 2 * span, 1), F32),
        "share2": pltpu.VMEM((slots, pairs, 2 * span, 1), F32),
        "f": pltpu.VMEM((ff_blocks, rows, width), BF16),
        "slope": pltpu.VMEM((ff_blocks, rows, width), F32),
        "rows": pltpu.VMEM((ROWS, width), F32),
        "rows_grad": pltpu.VMEM((ROWS, width), F32),
        "ebias": pltpu.VMEM((1, width * ff_blocks), F32),
        "ebias_grad": pltpu.VMEM((1, width * ff_blocks), F32),
        "tokens": pltpu.VMEM((8, LANES), F32),
        "d1": pltpu.VMEM((rows, 1), F32),
        "d2": pltpu.VMEM((rows, 1), F32),
        "send": pltpu.SemaphoreType.DMA((count,)),
        "recv": pltpu.SemaphoreType.DMA((count,)),
        "local": pltpu.SemaphoreType.DMA((BLOCKS + 3 + slots + len(small) + len(scalars),)),
        "scalars": [pltpu.SMEM(part.shape, part.dtype) for part in scalars],
        "params": [pltpu.VMEM(part.shape, BF16) for part in small],
    }
    for name in ("mem", "k2", "v2", "dk2", "dv2", "gmem"):
        scratch[name] = pltpu.VMEM(mem_shape, BF16)
    for name in ("q", "k", "v", "a", "h1b", "q2", "a2", "h2b", "e", "da", "dq", "dk", "dv"):
        scratch[name] = pltpu.VMEM((rows, width), BF16)
    for name in ("n1", "n2", "h1", "r3", "dr", "af", "a2f"):
        scratch[name] = pltpu.VMEM((rows, width), F32)
    for name in ("x", "dy"):
        scratch[name] = pltpu.VMEM(x.shape, BF16)
    leaves, tree = jax.tree.flatten(scratch)

    counts = (len(scalars), len(small), len(large), len(small), len(large))

    def kernel(*refs):
        groups, at = [], 0
        for size in counts:
            groups.append(refs[at : at + size])
            at += size
        layer_kernel(
            sizes, grid, groups[0], groups[1], *groups[2], groups[3], *groups[4],
            jax.tree.unflatten(tree, refs[at:]),
        )

    anywhere, vmem = pl.BlockSpec(memory_space=pl.ANY), pl.BlockSpec(memory_space=pltpu.VMEM)
    outs = [(part.shape, F32) for part in small]
    outs += [(x.shape, BF16), (x.shape, BF16)] + [(part.shape, F32) for part in large[2:6]] + [(memory.shape, BF16)]
    return pl.pallas_call(
        kernel,
        out_shape=tuple(pltpu.VMEM(shape, dtype) for shape, dtype in outs),
        in_specs=[anywhere] * sum(counts[:3]),
        out_specs=[vmem] * sum(counts[3:]),
        scratch_shapes=leaves,
        compiler_params=pltpu.CompilerParams(
            collective_id=0, has_side_effects=True, vmem_limit_bytes=58 << 20
        ),
    )(*scalars, *small, *large)


def copy_kernel(*refs):
    count, sems = len(refs) // 2, refs[-1]
    copies = [pltpu.make_async_copy(refs[n], refs[count + n], sems.at[n]) for n in range(count)]
    for copy in copies:
        copy.start()
    for copy in copies:
        copy.wait()


def handed_out(results):
    anywhere, vmem = pl.BlockSpec(memory_space=pl.ANY), pl.BlockSpec(memory_space=pltpu.VMEM)
    return pl.pallas_call(
        copy_kernel,
        out_shape=tuple(pltpu.HBM(part.shape, part.dtype) for part in results),
        in_specs=[vmem] * len(results),
        out_specs=[anywhere] * len(results),
        scratch_shapes=[pltpu.SemaphoreType.DMA((len(results),))],
        compiler_params=pltpu.CompilerParams(vmem_limit_bytes=32 << 20),
    )(*(pltpu.with_memory_space_constraint(part, pltpu.VMEM) for part in results))


def shards(
    sizes,
    decoder_in, memory, grad_out, decoder_lengths, memory_lengths, item_route,
    in_projection, out_projection, attention_bias, expand_weight, expand_bias,
    reduce_weight, reduce_bias, norm_gain, norm_bias,
):
    joined = in_projection.shape[1] < ROWS
    small = [attention_bias, norm_gain, norm_bias, reduce_bias[None], expand_bias[None]]
    weights = [in_projection, out_projection, expand_weight, reduce_weight.T]
    along = (1, 1, 0, 0)
    lengths, routes = decoder_lengths, item_route
    grid = dict(sizes)
    if joined:
        grid.update(x=1, c=1)
        small = [lax.all_gather(part, "mem", axis=1, tiled=True) for part in small]
        weights = [lax.all_gather(part, "mem", axis=axis, tiled=True) for part, axis in zip(weights, along)]
        lengths = lax.all_gather(lengths, "mem", tiled=True)
        routes = lax.all_gather(routes, "mem", tiled=True)
    results = run_layer(
        sizes, grid, (decoder_lengths, memory_lengths, item_route, lengths, routes), small,
        [decoder_in, grad_out] + weights + [memory],
    )
    if joined:
        results = list(results)
        for number in range(5):
            results[number] = lax.psum_scatter(results[number], "mem", scatter_dimension=1, tiled=True)
        for number, axis in zip(range(7, 11), along):
            results[number] = lax.psum_scatter(results[number], "mem", scatter_dimension=axis, tiled=True)
    else:
        results = handed_out(results)
    bias, gain, shift, reduce_shift, expand_shift, out, dx, g_in, g_out, g_expand, g_reduce, g_memory = results
    return (
        out, dx, g_memory, g_in, g_out, bias, g_expand, expand_shift[0], g_reduce.T, reduce_shift[0], gain, shift,
    )


def solution(mesh):
    both = ("bucket", "mem")
    buckets, members = mesh.shape["bucket"], mesh.shape["mem"]
    cores = 2
    across = members // cores
    sizes = {"z": buckets // across, "y": across, "x": across, "c": cores}
    in_specs = (
        P(both, None, None), P("bucket", "mem", None), P(both, None, None), P(both), P(both), P(both),
        P(None, both, None), P(None, both, None), P(None, both), P(both, None), P(both),
        P(None, both), P(both), P(None, both), P(None, both),
    )
    out_specs = (
        P(both, None, None), P(both, None, None), P("bucket", "mem", None),
        P(None, both, None), P(None, both, None), P(None, both), P(both, None), P(both),
        P(None, both), P(both), P(None, both), P(None, both),
    )
    return jax.shard_map(
        functools.partial(shards, sizes), mesh=mesh, in_specs=in_specs, out_specs=out_specs, check_vma=False
    )
```
